32 devices in a mesh: shot: 2 (over core), tile: 16 (over z, y, x).
Axes of the slice: x: 2, y: 2, z: 4, core: 2. Of those that a mesh axis runs over, the one named last changes fastest.
Arguments:
- adjoint_state: float32 [2, 9, 64, 64, 128], P('shot', None, 'tile'), may hold values from -6 to 6
- adjoint_source: bfloat16 [2, 3, 64, 64, 128], P('shot', None, 'tile'), may hold values from -6 to 6
- forward_field: bfloat16 [2, 9, 64, 64, 128], P('shot', None, 'tile'), may hold values from -6 to 6
- lame_first: float32 [64, 64, 128], P('tile'), may hold values from 0.5 to 1
- shear_modulus: float32 [64, 64, 128], P('tile'), may hold values from 0.3 to 1
- buoyancy: float32 [64, 64, 128], P('tile'), may hold values from 0.3 to 1
- active_blocks: int32 [16, 8, 4], P('tile'), may hold values from 0 to 1, as said below
- orientation: int32 [16, 8, 4], P('tile', 'shot'), may hold values from 0 to 3
Outputs:
- final_state: float32 [2, 9, 64, 64, 128], P('shot', None, 'tile')
- gradient: float32 [3, 64, 64, 128], P(None, 'tile', 'shot')
The draws below stay inside these ranges and needn't reach their ends.
Inputs may be any that keep to these rules, and one draw needn't show every extreme that they name: `active_blocks`: in each column of blocks (fixed first two indices) the blocks are 1 from depth index 0 up to a surface index and 0 above it; the block of depth index 0 is always 1.
All inputs are finite; a program needn't handle non-finite values.
Results may differ from the reference program's by a relative error of at most 0.0003.
Values sent between devices are 32-bit elements; how exact they have to be, the bound alone decides.
No kernel may reach another device: no remote copies, remote signals or barrier semaphores. Data moves between devices by JAX's collectives and lax.ppermute only.
A program may use at most 64 MiB of HBM per device.

```python
import math
import jax
import jax.numpy as jnp
from jax import lax

CX = 4
NY = 64
NZ = 128
BY = 8
BZ = 32
STEPS = 3
SWEEPS = 2
NX = 64
NBX = 16
NBY = 8
NBZ = 4
N_SHOT = 2


def draw_active_blocks(key, part):
    heights = jax.random.randint(key, (NBX, NBY, 1), 1, NBZ + 1)
    levels = jnp.arange(NBZ, dtype=jnp.int32)[None, None, :]
    return (levels < heights).astype(jnp.int32)


def with_ends(entries, stream_key, least, largest):
    place = [jax.random.randint(jax.random.fold_in(stream_key, axis), (), 0, length) for axis, length in enumerate(entries.shape)]
    main_axis = entries.shape.index(max(entries.shape))
    neighbour = place[:main_axis] + [(place[main_axis] + 1) % entries.shape[main_axis]] + place[main_axis + 1:]
    return entries.at[tuple(place)].set(least).at[tuple(neighbour)].set(largest)


def shard_levels(own_key, extent, split, smallest, high):
    level = 1.0
    for axis_at, parts in split:
        steps = jax.random.uniform(jax.random.fold_in(jax.random.fold_in(own_key, 6), axis_at), (parts,), jnp.float32, smallest / len(split), high / len(split))
        level = level * jnp.repeat(jnp.exp(steps), extent[axis_at] // parts).reshape((-1,) + (1,) * (len(extent) - 1 - axis_at))
    return level


def normal_values(stream_key, dims, deviation, bound, cuts=(), held_as=jnp.bfloat16):
    result = deviation * jax.random.normal(stream_key, dims, jnp.float32)
    if cuts:
        result = result * shard_levels(stream_key, dims, cuts, -0.22, 0.18)
    return jnp.clip(result, -bound, bound).astype(held_as)


def setup_inputs(seed: int = 0) -> dict:
    keys = jax.random.split(jax.random.key(seed), 9)
    return {
        "adjoint_state": normal_values(keys[0], (N_SHOT, 9, NX, NY, NZ), 1.0, 6.0, ((0, 2), (2, 16)), jnp.float32),
        "adjoint_source": normal_values(keys[1], (N_SHOT, STEPS, NX, NY, NZ), 1.0, 6.0, ((0, 2), (2, 16))),
        "forward_field": normal_values(keys[2], (N_SHOT, 9, NX, NY, NZ), 1.0, 6.0, ((0, 2), (2, 16))),
        "lame_first": jnp.clip(0.5 + 0.5 * jax.random.uniform(keys[3], (NX, NY, NZ), jnp.float32) ** shard_levels(keys[3], (NX, NY, NZ), ((0, 16),), -0.2, 0.2), 0.5, 1.0),
        "shear_modulus": jnp.clip(0.3 + 0.7 * jax.random.uniform(keys[4], (NX, NY, NZ), jnp.float32) ** shard_levels(keys[4], (NX, NY, NZ), ((0, 16),), -0.2, 0.2), 0.3, 1.0),
        "buoyancy": jnp.clip(jnp.exp(math.log(1.0) - 1.2039728 * jax.random.uniform(keys[5], (NX, NY, NZ), jnp.float32) ** shard_levels(keys[5], (NX, NY, NZ), ((0, 16),), -0.2, 0.2)), 0.3, 1.0),
        "active_blocks": draw_active_blocks(jax.random.fold_in(keys[8], 71), 0),
        "orientation": with_ends(jax.random.randint(keys[7], (NBX, NBY, NBZ), 0, 4), jax.random.fold_in(keys[7], 1), 0, 3).astype(jnp.int32),
    }


time_step = 0.25
smooth_rate = 0.1
weight_table = ((1.0, 1.0, 0.25), (0.25, 1.0, 1.0), (1.0, 0.25, 1.0), (0.6, 0.6, 0.6))


def prev_of(field, axis):
    size = field.shape[axis]
    zeros = jnp.zeros_like(lax.slice_in_dim(field, 0, 1, axis=axis))
    return jnp.concatenate([zeros, lax.slice_in_dim(field, 0, size - 1, axis=axis)], axis)


def next_of(field, axis):
    size = field.shape[axis]
    zeros = jnp.zeros_like(lax.slice_in_dim(field, 0, 1, axis=axis))
    return jnp.concatenate([lax.slice_in_dim(field, 1, size, axis=axis), zeros], axis)


def back_diff(field, axis):
    return field - prev_of(field, axis)


def ahead_diff(field, axis):
    return next_of(field, axis) - field


def expand_blocks(blocks):
    return jnp.repeat(jnp.repeat(jnp.repeat(blocks, CX, 0), BY, 1), BZ, 2)


def reference(adjoint_state, adjoint_source, forward_field, lame_first, shear_modulus, buoyancy, active_blocks, orientation):
    cells = expand_blocks(active_blocks.astype(jnp.float32))

    def one_shot(inputs):
        state, source, forward = inputs
        comps = [state[i] for i in range(9)]
        fwd = [forward[i].astype(jnp.float32) for i in range(9)]
        image_lame = jnp.zeros_like(cells)
        image_shear = jnp.zeros_like(cells)
        image_density = jnp.zeros_like(cells)
        for step_index in range(STEPS):
            vel_x, vel_y, vel_z, str_xx, str_yy, str_zz, str_xy, str_xz, str_yz = comps
            vel_x = cells * (vel_x + time_step * buoyancy * (back_diff(str_xx, 0) + back_diff(str_xy, 1) + back_diff(str_xz, 2)))
            vel_y = cells * (vel_y + time_step * buoyancy * (back_diff(str_xy, 0) + back_diff(str_yy, 1) + back_diff(str_yz, 2)))
            vel_z = cells * (vel_z + time_step * buoyancy * (back_diff(str_xz, 0) + back_diff(str_yz, 1) + back_diff(str_zz, 2)) + time_step * source[step_index].astype(jnp.float32))
            strain_xx = ahead_diff(vel_x, 0)
            strain_yy = ahead_diff(vel_y, 1)
            strain_zz = ahead_diff(vel_z, 2)
            diverge = strain_xx + strain_yy + strain_zz
            str_xx = cells * (str_xx + time_step * (lame_first * diverge + 2.0 * shear_modulus * strain_xx))
            str_yy = cells * (str_yy + time_step * (lame_first * diverge + 2.0 * shear_modulus * strain_yy))
            str_zz = cells * (str_zz + time_step * (lame_first * diverge + 2.0 * shear_modulus * strain_zz))
            str_xy = cells * (str_xy + time_step * shear_modulus * (ahead_diff(vel_x, 1) + ahead_diff(vel_y, 0)))
            str_xz = cells * (str_xz + time_step * shear_modulus * (ahead_diff(vel_x, 2) + ahead_diff(vel_z, 0)))
            str_yz = cells * (str_yz + time_step * shear_modulus * (ahead_diff(vel_y, 2) + ahead_diff(vel_z, 1)))
            comps = [vel_x, vel_y, vel_z, str_xx, str_yy, str_zz, str_xy, str_xz, str_yz]
            image_lame = image_lame + (str_xx + str_yy + str_zz) * (fwd[0] + fwd[1] + fwd[2])
            image_shear = image_shear + (str_xx * fwd[0] + str_yy * fwd[1] + str_zz * fwd[2] + str_xy * fwd[3] + str_xz * fwd[4] + str_yz * fwd[5])
            image_density = image_density + (vel_x * fwd[6] + vel_y * fwd[7] + vel_z * fwd[8])
        return jnp.stack(comps), jnp.stack([image_lame, image_shear, image_density])

    final_state, partial_value = lax.map(one_shot, (adjoint_state, adjoint_source, forward_field))
    summed = jnp.sum(partial_value, axis=0) * (STEPS * N_SHOT) ** -0.5
    weights = []
    for column in range(3):
        table = jnp.zeros(orientation.shape, jnp.float32)
        for klass in range(4):
            table = table + (orientation == klass).astype(jnp.float32) * weight_table[klass][column]
        weights.append(expand_blocks(table))
    grad = summed
    for sweep in range(SWEEPS):
        lap_x = next_of(grad, 1) + prev_of(grad, 1) - 2.0 * grad
        lap_y = next_of(grad, 2) + prev_of(grad, 2) - 2.0 * grad
        lap_z = next_of(grad, 3) + prev_of(grad, 3) - 2.0 * grad
        grad = grad + smooth_rate * (weights[0] * lap_x + weights[1] * lap_y + weights[2] * lap_z)
    return final_state, grad
```

```python
import functools

import jax
import jax.numpy as jnp
from jax import lax
from jax.experimental import pallas as pl
from jax.experimental.pallas import tpu as pltpu
from jax.sharding import PartitionSpec as P

BY = 8
BZ = 32
STEPS = 3
SWEEPS = 2

time_step = 0.25
smooth_rate = 0.1
weight_table = ((1.0, 1.0, 0.25), (0.25, 1.0, 1.0), (1.0, 0.25, 1.0), (0.6, 0.6, 0.6))

VX, VY, VZ, XX, YY, ZZ, XY, XZ, YZ = range(9)
CB, CL, CM, CB_NEXT = 9, 10, 11, 12
PLANES = 13
ROWS = 32
VMEM = pl.BlockSpec(memory_space=pltpu.VMEM)
SMEM = pl.BlockSpec(memory_space=pltpu.SMEM)
PARAMS = pltpu.CompilerParams(vmem_limit_bytes=24 * 1024 * 1024)


def lanes(shape):
    return lax.broadcasted_iota(jnp.int32, shape, len(shape) - 1)


def rows(shape):
    return lax.broadcasted_iota(jnp.int32, shape, len(shape) - 2)


def z_prev(f):
    return jnp.where(lanes(f.shape) == 0, 0.0, pltpu.roll(f, 1, f.ndim - 1))


def z_next(f):
    size = f.shape[-1]
    return jnp.where(lanes(f.shape) == size - 1, 0.0, pltpu.roll(f, size - 1, f.ndim - 1))


class Plane:
    def __init__(self, ref, *index):
        self.ref, self.index = ref, index
        self.size = ref.shape[len(index)]

    def at(self, row, count):
        return self.ref[self.index + (slice(row, row + count),)]

    def prev(self, row, count):
        if row:
            return self.at(row - 1, count)
        edge = pltpu.roll(self.at(0, 8), 1, 0)
        edge = jnp.where(rows(edge.shape) == 0, 0.0, edge)
        return jnp.concatenate([edge, self.at(7, count - 8)], 0)

    def next(self, row, count):
        if row + count < self.size:
            return self.at(row + 1, count)
        edge = pltpu.roll(self.at(self.size - 8, 8), 7, 0)
        edge = jnp.where(rows(edge.shape) == 7, 0.0, edge)
        return jnp.concatenate([self.at(row + 1, count - 8), edge], 0)

    def set(self, row, value):
        self.ref[self.index + (slice(row, row + value.shape[0]),)] = value


def planes(ref, comps, *index):
    return {c: Plane(ref, n, *index) for n, c in enumerate(comps)}


def divergence(s, before, row, count, have=(XX, YY, ZZ, XY, XZ, YZ)):
    def along_x(c):
        here = s[c].at(row, count)
        return here - before[c].at(row, count) if before is not None else here

    def along_y(c):
        return s[c].at(row, count) - s[c].prev(row, count)

    def along_z(c):
        here = s[c].at(row, count)
        return here - z_prev(here)

    out = []
    for c_x, c_y, c_z in ((XX, XY, XZ), (XY, YY, YZ), (XZ, YZ, ZZ)):
        terms = along_x(c_x)
        if c_y in have:
            terms = terms + along_y(c_y)
        if c_z in have:
            terms = terms + along_z(c_z)
        out.append(terms)
    return out


def strain(v, after, row, count, want=(XX, YY, ZZ, XY, XZ, YZ)):
    x, y, z = (v[c].at(row, count) for c in (VX, VY, VZ))
    if after is None:
        d_x = [-x, -y, -z]
    else:
        d_x = [after[c].at(row, count) - f for c, f in ((VX, x), (VY, y), (VZ, z))]
    out = {XX: d_x[0], YY: v[VY].next(row, count) - y, ZZ: z_next(z) - z}
    out["div"] = out[XX] + out[YY] + out[ZZ]
    if XY in want:
        out[XY] = v[VX].next(row, count) - x + d_x[1]
    if XZ in want:
        out[XZ] = z_next(x) - x + d_x[2]
    if YZ in want:
        out[YZ] = z_next(y) - y + (v[VZ].next(row, count) - z)
    return out


def stress_rate(e, lame, shear, want=(XX, YY, ZZ, XY, XZ, YZ)):
    spread = lame * e["div"]
    return {
        c: spread + 2.0 * shear * e[c] if c in (XX, YY, ZZ) else shear * e[c] for c in want
    }


def cell_plane(active, out):
    shape = (BY, out.shape[1])
    for j in range(out.shape[0] // BY):
        row = jnp.full(shape, active[0, j, 0].astype(jnp.float32))
        for k in range(1, out.shape[1] // BZ):
            row = jnp.where(lanes(shape) >= k * BZ, active[0, j, k].astype(jnp.float32), row)
        out[j * BY : (j + 1) * BY, :] = row


def chunks(size):
    return range(0, size, ROWS)


def first_kernel(
    active, state, source, lame, shear, buoyancy, by_pair, by_next, st, coef, cells, v2, s2, msg
):
    width, size_y = state.shape[1], state.shape[2]
    last = width - 1
    cell_plane(active, cells)

    def forced(step, x, row):
        return (
            time_step
            * cells[row : row + ROWS, :]
            * source[step, x, row : row + ROWS, :].astype(jnp.float32)
        )

    up, down = 0, 1
    for row in chunks(size_y):
        c = cells[row : row + ROWS, :]
        for x in range(width):
            for n, param in enumerate((buoyancy, lame, shear)):
                coef[n, x, row : row + ROWS, :] = time_step * c * param[x, row : row + ROWS, :]

    def coefs(x, row):
        return [coef[n, x, row : row + ROWS, :] for n in range(3)]

    raw = [{c: Plane(state, c, x) for c in range(9)} for x in range(width)]
    one = [{c: Plane(st, c, x) for c in range(9)} for x in range(width)]
    two = {x: {c: Plane(v2, n, c) for c in (VX, VY, VZ)} for n, x in enumerate((0, 1, last))}
    for x in range(width):
        for row in chunks(size_y):
            c = cells[row : row + ROWS, :]
            cb = coefs(x, row)[0]
            terms = divergence(raw[x], raw[x - 1] if x else None, row, ROWS)
            for comp, term in zip((VX, VY, VZ), terms):
                value = c * raw[x][comp].at(row, ROWS) + cb * term
                if comp == VZ:
                    value = value + forced(0, x, row)
                one[x][comp].set(row, value)
    for x in range(width):
        for row in chunks(size_y):
            c = cells[row : row + ROWS, :]
            _, cl, cm = coefs(x, row)
            rate = stress_rate(strain(one[x], one[x + 1] if x < last else None, row, ROWS), cl, cm)
            for comp, term in rate.items():
                one[x][comp].set(row, c * raw[x][comp].at(row, ROWS) + term)
    for x in two:
        for row in chunks(size_y):
            cb = coefs(x, row)[0]
            terms = divergence(one[x], one[x - 1] if x else None, row, ROWS)
            for comp, term in zip((VX, VY, VZ), terms):
                value = one[x][comp].at(row, ROWS) + cb * term
                if comp == VZ:
                    value = value + forced(1, x, row)
                two[x][comp].set(row, value)
    stress = {c: Plane(s2, c) for c in range(9) if c >= XX}
    for row in chunks(size_y):
        _, cl, cm = coefs(0, row)
        rate = stress_rate(strain(two[0], two[1], row, ROWS), cl, cm)
        for comp, term in rate.items():
            stress[comp].set(row, one[0][comp].at(row, ROWS) + term)
        _, cl, cm = coefs(last, row)
        want = (XX, XY, XZ)
        rate = stress_rate(strain(two[last], None, row, ROWS, want), cl, cm, want)
        for n, comp in enumerate(want):
            here = slice(row, row + ROWS)
            msg[up, n, here] = raw[last][comp].at(row, ROWS)
            msg[up, 3 + n, here] = one[last][comp].at(row, ROWS)
            msg[up, 6 + n, here] = one[last][comp].at(row, ROWS) + rate[comp]
    for row in chunks(size_y):
        cb = coefs(0, row)[0]
        here = slice(row, row + ROWS)
        terms = divergence(stress, None, row, ROWS)
        for n, (comp, term) in enumerate(zip((VX, VY, VZ), terms)):
            value = two[0][comp].at(row, ROWS) + cb * term
            if comp == VZ:
                value = value + forced(2, 0, row)
            msg[down, n, here] = one[0][comp].at(row, ROWS)
            msg[down, 3 + n, here] = two[0][comp].at(row, ROWS)
            msg[down, 6 + n, here] = value
        for n in range(3):
            msg[up, CB + n, here] = coef[n, last, here]
            msg[down, CB + n, here] = coef[n, 0, here]
        msg[up, CB_NEXT, here] = coef[0, last, here]
        msg[down, CB_NEXT, here] = coef[0, 1, here]

    even = lax.rem(lax.axis_index("tile"), 2) == 0

    @pl.when(even)
    def _():
        by_pair[...] = msg[up]
        by_next[...] = msg[down]

    @pl.when(jnp.logical_not(even))
    def _():
        by_pair[...] = msg[down]
        by_next[...] = msg[up]


def main_kernel(
    groups,
    active,
    orientation,
    by_pair,
    by_next,
    state,
    st,
    coef,
    source,
    forward,
    final,
    *rest,
):
    images, (cells, got, end, w, low_s, high_v, d_s, d_v, image) = rest[:-9], rest[-9:]
    width, size_y = st.shape[1], st.shape[2]
    last = width - 1
    lo, hi = 0, 1
    cell_plane(active, cells)
    even = lax.rem(lax.axis_index("tile"), 2) == 0

    @pl.when(even)
    def _():
        got[lo] = by_next[...]
        got[hi] = by_pair[...]

    @pl.when(jnp.logical_not(even))
    def _():
        got[lo] = by_pair[...]
        got[hi] = by_next[...]

    def forced(step, x, row):
        return (
            time_step
            * cells[row : row + ROWS, :]
            * source[step, x, row : row + ROWS, :].astype(jnp.float32)
        )

    def coefs(x, row):
        here = slice(row, row + ROWS)
        if x < 0:
            return [got[lo, CB + n, here] for n in range(3)]
        if x > last:
            return [got[hi, CB + n, here] for n in range(3)]
        return [coef[n, x, here] for n in range(3)]

    vel, side, stress = (VX, VY, VZ), (XX, XY, XZ), (XX, YY, ZZ, XY, XZ, YZ)
    raw = [{c: Plane(state, c, x) for c in range(9)} for x in range(width)]
    one = [{c: Plane(st, c, x) for c in range(9)} for x in range(width)]
    base = one[last]
    one[0] = {c: Plane(end, 0, c) for c in range(9)}
    one[last] = {c: Plane(st if c in vel else end, *((c, last) if c in vel else (1, c))) for c in range(9)}
    two = [{c: Plane(w, c, x) for c in range(9)} for x in range(width)]
    three = [{c: Plane(final, c, x) for c in range(9)} for x in range(width)]
    sent_low = [{c: Plane(got, lo, 3 * k + n) for n, c in enumerate(side)} for k in range(3)]
    sent_high = [{c: Plane(got, hi, 3 * k + c) for c in vel} for k in range(3)]
    low_one, low_two = ({c: Plane(low_s, k, n) for n, c in enumerate(side)} for k in range(2))
    high = [{c: Plane(high_v, k, c) for c in vel} for k in range(3)]
    d_low_s = {c: Plane(d_s, 0, c - XX) for c in stress}
    d_high_s = {c: Plane(d_s, 1, c - XX) for c in stress}
    d_high_s_two = {c: Plane(d_s, 2, c - XX) for c in stress}
    d_high_v, d_high_v_two, d_far_v, d_low_v = ({c: Plane(d_v, k, c) for c in vel} for k in range(4))

    for row in chunks(size_y):
        cb, cb_high = coefs(0, row)[0], coefs(last + 1, row)[0]
        for comp, c in zip(vel, side):
            one[0][comp].set(
                row, Plane(st, comp, 0).at(row, ROWS) - cb * sent_low[0][c].at(row, ROWS)
            )
            delta = -cb_high * raw[last][c].at(row, ROWS)
            d_high_v[comp].set(row, delta)
            high[0][comp].set(row, sent_high[0][comp].at(row, ROWS) + delta)
    for row in chunks(size_y):
        c = cells[row : row + ROWS, :]
        _, cl, cm = coefs(0, row)
        for comp, term in stress_rate(strain(one[0], one[1], row, ROWS), cl, cm).items():
            one[0][comp].set(row, c * raw[0][comp].at(row, ROWS) + term)
        _, cl, cm = coefs(last, row)
        v = [high[0][comp].at(row, ROWS) for comp in vel]
        spread = cl * v[0]
        terms = {XX: spread + 2.0 * cm * v[0], YY: spread, ZZ: spread, XY: cm * v[1], XZ: cm * v[2]}
        for comp in stress:
            value = base[comp].at(row, ROWS)
            one[last][comp].set(row, value + terms[comp] if comp in terms else value)
        _, cl, cm = coefs(-1, row)
        v = [one[0][comp].at(row, ROWS) for comp in vel]
        spread = cl * v[0]
        terms = {XX: spread + 2.0 * cm * v[0], YY: spread, ZZ: spread, XY: cm * v[1], XZ: cm * v[2]}
        for comp, term in terms.items():
            d_low_s[comp].set(row, term)
        for comp in side:
            low_one[comp].set(row, sent_low[1][comp].at(row, ROWS) + terms[comp])
        _, cl, cm = coefs(last + 1, row)
        for comp, term in stress_rate(strain(d_high_v, None, row, ROWS), cl, cm).items():
            d_high_s[comp].set(row, term)

    for row in chunks(size_y):
        for x in range(width):
            cb = coefs(x, row)[0]
            terms = divergence(one[x], one[x - 1] if x else low_one, row, ROWS)
            for comp, term in zip(vel, terms):
                value = one[x][comp].at(row, ROWS) + cb * term
                if comp == VZ:
                    value = value + forced(1, x, row)
                two[x][comp].set(row, value)
        cb = coefs(last + 1, row)[0]
        for comp, term in zip(vel, divergence(d_high_s, one[last], row, ROWS)):
            value = d_high_v[comp].at(row, ROWS) + cb * term
            d_high_v_two[comp].set(row, value)
            high[1][comp].set(row, sent_high[1][comp].at(row, ROWS) + value)
        cb = got[hi, CB_NEXT, row : row + ROWS]
        for comp, c in zip(vel, side):
            d_far_v[comp].set(row, -cb * d_high_s[c].at(row, ROWS))
        cb = coefs(-1, row)[0]
        terms = divergence(d_low_s, None, row, ROWS, (XX, YY, ZZ, XY, XZ))
        for comp, term in zip(vel, terms):
            d_low_v[comp].set(row, cb * term)
    for row in chunks(size_y):
        for x in range(width):
            _, cl, cm = coefs(x, row)
            after = two[x + 1] if x < last else high[1]
            for comp, term in stress_rate(strain(two[x], after, row, ROWS), cl, cm).items():
                two[x][comp].set(row, one[x][comp].at(row, ROWS) + term)
        _, cl, cm = coefs(-1, row)
        rate = stress_rate(strain(d_low_v, two[0], row, ROWS, side), cl, cm, side)
        for comp, term in rate.items():
            value = sent_low[2][comp].at(row, ROWS) + d_low_s[comp].at(row, ROWS)
            low_two[comp].set(row, value + term)
        _, cl, cm = coefs(last + 1, row)
        for comp, term in stress_rate(strain(d_high_v_two, d_far_v, row, ROWS), cl, cm).items():
            d_high_s_two[comp].set(row, d_high_s[comp].at(row, ROWS) + term)

    for row in chunks(size_y):
        for x in range(width):
            cb = coefs(x, row)[0]
            terms = divergence(two[x], two[x - 1] if x else low_two, row, ROWS)
            for comp, term in zip(vel, terms):
                value = two[x][comp].at(row, ROWS) + cb * term
                if comp == VZ:
                    value = value + forced(2, x, row)
                three[x][comp].set(row, value)
        cb = coefs(last + 1, row)[0]
        for comp, term in zip(vel, divergence(d_high_s_two, two[last], row, ROWS)):
            value = d_high_v_two[comp].at(row, ROWS) + cb * term
            high[2][comp].set(row, sent_high[2][comp].at(row, ROWS) + value)
    for row in chunks(size_y):
        here = slice(row, row + ROWS)
        for x in range(width):
            _, cl, cm = coefs(x, row)
            after = three[x + 1] if x < last else high[2]
            rate = stress_rate(strain(three[x], after, row, ROWS), cl, cm)
            sums = {}
            for comp in stress:
                before = two[x][comp].at(row, ROWS)
                value = before + rate[comp]
                three[x][comp].set(row, value)
                sums[comp] = one[x][comp].at(row, ROWS) + before + value
            f = [forward[n, x, here].astype(jnp.float32) for n in range(9)]
            image[0, x, here] = (sums[XX] + sums[YY] + sums[ZZ]) * (f[0] + f[1] + f[2])
            total = sums[XX] * f[0]
            for n, comp in enumerate(stress[1:]):
                total = total + sums[comp] * f[n + 1]
            image[1, x, here] = total
            total = 0.0
            for comp in vel:
                moved = [k[x][comp].at(row, ROWS) for k in (one, two, three)]
                total = total + (moved[0] + moved[1] + moved[2]) * f[6 + comp]
            image[2, x, here] = total

    if groups != 2:
        images[0][...] = image[...]
        return
    give, keep = images
    me = lax.axis_index("shot")
    count = keep.shape[0] // (3 * width)
    mine = pl.multiple_of(me * (size_y - count), 8)
    theirs = pl.multiple_of((1 - me) * (size_y - count), 8)
    for n in range(3):
        for x in range(width):
            here = slice((n * width + x) * count, (n * width + x + 1) * count)
            give[here, :] = image[n, x, pl.ds(theirs, count), :]
            keep[here, :] = image[n, x, pl.ds(mine, count), :]
    blocks = orientation.shape[1]
    give[3 * width * count :, :] = class_tile(orientation, jnp.where(me == 0, blocks - 1, 0), keep.shape[1])


def class_tile(orientation, j, size_z):
    shape = (BY, size_z)
    out = jnp.full(shape, orientation[0, j, 0].astype(jnp.float32))
    for k in range(1, size_z // BZ):
        out = jnp.where(lanes(shape) >= k * BZ, orientation[0, j, k].astype(jnp.float32), out)
    return out


def y_prev(f):
    return jnp.where(rows(f.shape) == 0, 0.0, pltpu.roll(f, 1, f.ndim - 2))


def y_next(f):
    size = f.shape[-2]
    return jnp.where(rows(f.shape) == size - 1, 0.0, pltpu.roll(f, size - 1, f.ndim - 2))


def sweep(here, before, after, weights):
    w_x, w_y, w_z = weights
    twice = 2.0 * here
    along_x = -twice
    for plane in (before, after):
        if plane is not None:
            along_x = along_x + plane
    along_y = y_next(here) + y_prev(here) - twice
    along_z = z_next(here) + z_prev(here) - twice
    return here + (w_x * along_x + w_y * along_y + w_z * along_z)


def edge_row(me, own):
    return jnp.where(me == 0, own, BY - 1)


def sum_kernel(scale, orientation, keep, received, by_pair, by_next, grad, swept, weights, classes, msg):
    width, count, size_z = grad.shape[1:]
    own = count - BY
    me = lax.axis_index("shot")
    first = pl.multiple_of(me * BY, BY)
    for j in range(own // BY):
        classes[pl.ds(first + j * BY, BY), :] = class_tile(orientation, j, size_z)
    beyond = pl.multiple_of((1 - me) * own, BY)
    classes[pl.ds(beyond, BY), :] = received[3 * width * count :, :]
    klass = classes[...]
    for column in range(3):
        table = jnp.full(klass.shape, weight_table[3][column], jnp.float32)
        for k in range(3):
            table = jnp.where(klass == k, weight_table[k][column], table)
        weights[column] = smooth_rate * table
    for n in range(3):
        for x in range(width):
            here = slice((n * width + x) * count, (n * width + x + 1) * count)
            grad[n, x] = (keep[here, :] + received[here, :]) * scale
    w = [weights[k] for k in range(3)]
    for n in range(3):
        for x in range(width):
            swept[n, x] = sweep(
                grad[n, x],
                grad[n, x - 1] if x else None,
                grad[n, x + 1] if x < width - 1 else None,
                w,
            )
    edge = edge_row(me, own)
    mine = pl.ds(first, own)
    for to, x in ((0, width - 1), (1, 0)):
        msg[to, 6 * own :, :] = jnp.zeros((BY, size_z), jnp.float32)
        for n in range(3):
            msg[to, 2 * n * own : (2 * n + 1) * own, :] = grad[n, x, mine, :]
            msg[to, (2 * n + 1) * own : (2 * n + 2) * own, :] = swept[n, x, mine, :]
            msg[to, 6 * own + n : 6 * own + n + 1, :] = grad[n, x, pl.ds(edge, 1), :]
        for j in range(own // BY):
            row = weights[0, pl.ds(pl.multiple_of(first + j * BY, BY), BY), :][0:1]
            msg[to, 6 * own + 3 + j : 6 * own + 4 + j, :] = row
    even = lax.rem(lax.axis_index("tile"), 2) == 0

    @pl.when(even)
    def _():
        by_pair[...] = msg[0]
        by_next[...] = msg[1]

    @pl.when(jnp.logical_not(even))
    def _():
        by_pair[...] = msg[1]
        by_next[...] = msg[0]


def smooth_kernel(by_pair, by_next, grad, swept, weights, out, got, beside, full, result):
    width, count, size_z = grad.shape[1:]
    own = count - BY
    last = width - 1
    even = lax.rem(lax.axis_index("tile"), 2) == 0
    me = lax.axis_index("shot")
    first = pl.multiple_of(me * BY, BY)
    mine = pl.ds(first, own)

    @pl.when(even)
    def _():
        got[0] = by_next[...]
        got[1] = by_pair[...]

    @pl.when(jnp.logical_not(even))
    def _():
        got[0] = by_pair[...]
        got[1] = by_next[...]

    edge = edge_row(me, own)
    beside[...] = jnp.zeros(beside.shape, jnp.float32)
    for side, x in ((0, 0), (1, last)):
        for n in range(3):
            beside[side, n, mine, :] = got[side, 2 * n * own : (2 * n + 1) * own, :]
            beside[side, n, pl.ds(edge, 1), :] = got[side, 6 * own + n : 6 * own + n + 1, :]
            beside[side, 3 + n, mine, :] = got[side, (2 * n + 1) * own : (2 * n + 2) * own, :]
        for j in range(own // BY):
            row = got[side, 6 * own + 3 + j : 6 * own + 4 + j, :]
            here = pl.ds(pl.multiple_of(first + j * BY, BY), BY)
            beside[side, 6, here, :] = jnp.broadcast_to(row, (BY, size_z))
    w = [weights[k] for k in range(3)]
    for n in range(3):
        for x in range(width):
            value = swept[n, x]
            if x == 0:
                value = value + w[0] * beside[0, n]
            if x == last:
                value = value + w[0] * beside[1, n]
            full[x + 1] = value
        full[0] = beside[0, 3 + n] + beside[0, 6] * grad[n, 0]
        full[width + 1] = beside[1, 3 + n] + beside[1, 6] * grad[n, last]
        for x in range(width):
            result[...] = sweep(full[x + 1], full[x], full[x + 2], w)
            out[n, x] = result[mine, :]


def extended(block, sides, width):
    for axis, dim in sides:
        count = lax.axis_size(axis)
        forward = [(i, i + 1) for i in range(count - 1)]
        backward = [(target, source) for source, target in forward]
        low = lax.ppermute(
            lax.slice_in_dim(block, block.shape[dim] - width, None, axis=dim), axis, forward
        )
        high = lax.ppermute(lax.slice_in_dim(block, 0, width, axis=dim), axis, backward)
        block = jnp.concatenate([low, block, high], axis=dim)
    return block


def smooth_anywhere(image, orientation):
    groups = lax.axis_size("shot")
    owned = image.shape[2] // groups
    total = lax.psum(image, "shot")
    grad = lax.dynamic_slice_in_dim(total, lax.axis_index("shot") * owned, owned, 2)
    grad = grad * (STEPS * groups) ** (-0.5)
    weights = []
    for column in range(3):
        table = jnp.zeros(orientation.shape, jnp.float32)
        for klass in range(4):
            table = table + (orientation == klass).astype(jnp.float32) * weight_table[klass][column]
        table = jnp.repeat(jnp.repeat(table, image.shape[1], 0), BY, 1)
        weights.append(jnp.repeat(table, BZ, 2))
    for _ in range(SWEEPS):
        padded = extended(grad, (("shot", 2), ("tile", 1)), 1)
        padded = jnp.pad(padded, ((0, 0), (0, 0), (0, 0), (1, 1)))
        center = padded[:, 1:-1, 1:-1, 1:-1]
        lap_x = padded[:, 2:, 1:-1, 1:-1] + padded[:, :-2, 1:-1, 1:-1] - 2.0 * center
        lap_y = padded[:, 1:-1, 2:, 1:-1] + padded[:, 1:-1, :-2, 1:-1] - 2.0 * center
        lap_z = padded[:, 1:-1, 1:-1, 2:] + padded[:, 1:-1, 1:-1, :-2] - 2.0 * center
        grad = grad + smooth_rate * (weights[0] * lap_x + weights[1] * lap_y + weights[2] * lap_z)
    return grad


def both_ways(by_pair, by_next):
    count = lax.axis_size("tile")
    out = []
    for array, start in ((by_next, 1), (by_pair, 0)):
        pairs = [(i, i + 1) for i in range(start, count - 1, 2)]
        out.append(lax.ppermute(array, "tile", pairs + [(b, a) for a, b in pairs]))
    return out[1], out[0]


def f32(*shape):
    return jax.ShapeDtypeStruct(shape, jnp.float32)


def call(kernel, outs, args, scratch, scalars=0):
    return pl.pallas_call(
        kernel,
        out_shape=outs,
        in_specs=[SMEM] * scalars + [VMEM] * (len(args) - scalars),
        out_specs=jax.tree.map(lambda _: VMEM, outs),
        scratch_shapes=[pltpu.VMEM(shape, jnp.float32) for shape in scratch],
        compiler_params=PARAMS,
    )(*args)


def local(
    adjoint_state,
    adjoint_source,
    forward_field,
    lame_first,
    shear_modulus,
    buoyancy,
    active_blocks,
    orientation,
):
    width, size_y, size_z = lame_first.shape
    plane = (size_y, size_z)
    groups = lax.axis_size("shot")
    state, source, forward = adjoint_state[0], adjoint_source[0], forward_field[0]
    by_pair, by_next, st, coef = call(
        first_kernel,
        (f32(PLANES, *plane), f32(PLANES, *plane), f32(9, width, *plane), f32(3, width, *plane)),
        (active_blocks, state, source, lame_first, shear_modulus, buoyancy),
        [plane, (3, 3, *plane), (9, *plane), (2, PLANES, *plane)],
        1,
    )
    by_pair, by_next = both_ways(by_pair, by_next)
    owned = size_y // groups
    count = owned + BY
    if groups == 2:
        images = (f32(3 * width * count + BY, size_z), f32(3 * width * count, size_z))
    else:
        images = (f32(3, width, *plane),)
    final, *images = call(
        functools.partial(main_kernel, groups),
        (f32(9, width, *plane), *images),
        (active_blocks, orientation, by_pair, by_next, state, st, coef, source, forward),
        [
            plane,
            (2, PLANES, *plane),
            (2, 9, *plane),
            (9, width, *plane),
            (2, 3, *plane),
            (3, 3, *plane),
            (3, 6, *plane),
            (4, 3, *plane),
            (3, width, *plane),
        ],
        2,
    )
    if groups != 2:
        return final[None], smooth_anywhere(images[0], orientation)
    give, keep = images
    received = lax.ppermute(give, "shot", [(0, 1), (1, 0)])
    block = (3, width, count, size_z)
    by_pair, by_next, grad, swept, weights = call(
        functools.partial(sum_kernel, (STEPS * groups) ** (-0.5)),
        (f32(6 * owned + BY, size_z), f32(6 * owned + BY, size_z), f32(*block), f32(*block), f32(3, count, size_z)),
        (orientation, keep, received),
        [(count, size_z), (2, 6 * owned + BY, size_z)],
        1,
    )
    by_pair, by_next = both_ways(by_pair, by_next)
    gradient = call(
        smooth_kernel,
        f32(3, width, owned, size_z),
        (by_pair, by_next, grad, swept, weights),
        [
            (2, 6 * owned + BY, size_z),
            (2, 7, count, size_z),
            (width + 2, count, size_z),
            (count, size_z),
        ],
    )
    return final[None], gradient


def solution(mesh):
    return jax.shard_map(
        local,
        mesh=mesh,
        in_specs=(
            P("shot", None, "tile", None, None),
            P("shot", None, "tile", None, None),
            P("shot", None, "tile", None, None),
            P("tile", None, None),
            P("tile", None, None),
            P("tile", None, None),
            P("tile", None, None),
            P("tile", "shot", None),
        ),
        out_specs=(P("shot", None, "tile", None, None), P(None, "tile", "shot", None)),
        check_vma=False,
    )
```

```python
import functools

import jax
import jax.numpy as jnp
from jax import lax
from jax.experimental import pallas as pl
from jax.experimental.pallas import tpu as pltpu
from jax.sharding import PartitionSpec as P

BY = 8
BZ = 32
STEPS = 3
SWEEPS = 2

time_step = 0.25
smooth_rate = 0.1
weight_table = ((1.0, 1.0, 0.25), (0.25, 1.0, 1.0), (1.0, 0.25, 1.0), (0.6, 0.6, 0.6))

VX, VY, VZ, XX, YY, ZZ, XY, XZ, YZ = range(9)
CB, CL, CM, CB_NEXT = 9, 10, 11, 12
PLANES = 13
ROWS = 32
VMEM = pl.BlockSpec(memory_space=pltpu.VMEM)
SMEM = pl.BlockSpec(memory_space=pltpu.SMEM)
HBM = pl.BlockSpec(memory_space=pltpu.HBM)


def lanes(shape):
    return lax.broadcasted_iota(jnp.int32, shape, len(shape) - 1)


def rows(shape):
    return lax.broadcasted_iota(jnp.int32, shape, len(shape) - 2)


def z_prev(f):
    return jnp.where(lanes(f.shape) == 0, 0.0, pltpu.roll(f, 1, f.ndim - 1))


def z_next(f):
    size = f.shape[-1]
    return jnp.where(lanes(f.shape) == size - 1, 0.0, pltpu.roll(f, size - 1, f.ndim - 1))


class Plane:
    def __init__(self, ref, *index):
        self.ref, self.index = ref, index
        self.size = ref.shape[len(index)]

    def at(self, row, count):
        return self.ref[self.index + (slice(row, row + count),)]

    def prev(self, row, count):
        if row:
            return self.at(row - 1, count)
        edge = pltpu.roll(self.at(0, 8), 1, 0)
        edge = jnp.where(rows(edge.shape) == 0, 0.0, edge)
        return jnp.concatenate([edge, self.at(7, count - 8)], 0)

    def next(self, row, count):
        if row + count < self.size:
            return self.at(row + 1, count)
        edge = pltpu.roll(self.at(self.size - 8, 8), 7, 0)
        edge = jnp.where(rows(edge.shape) == 7, 0.0, edge)
        return jnp.concatenate([self.at(row + 1, count - 8), edge], 0)

    def set(self, row, value):
        self.ref[self.index + (slice(row, row + value.shape[0]),)] = value


def planes(ref, comps, *index):
    return {c: Plane(ref, n, *index) for n, c in enumerate(comps)}


def divergence(s, before, row, count, have=(XX, YY, ZZ, XY, XZ, YZ)):
    def along_x(c):
        here = s[c].at(row, count)
        return here - before[c].at(row, count) if before is not None else here

    def along_y(c):
        return s[c].at(row, count) - s[c].prev(row, count)

    def along_z(c):
        here = s[c].at(row, count)
        return here - z_prev(here)

    out = []
    for c_x, c_y, c_z in ((XX, XY, XZ), (XY, YY, YZ), (XZ, YZ, ZZ)):
        terms = along_x(c_x)
        if c_y in have:
            terms = terms + along_y(c_y)
        if c_z in have:
            terms = terms + along_z(c_z)
        out.append(terms)
    return out


def strain(v, after, row, count, want=(XX, YY, ZZ, XY, XZ, YZ)):
    x, y, z = (v[c].at(row, count) for c in (VX, VY, VZ))
    if after is None:
        d_x = [-x, -y, -z]
    else:
        d_x = [after[c].at(row, count) - f for c, f in ((VX, x), (VY, y), (VZ, z))]
    out = {XX: d_x[0], YY: v[VY].next(row, count) - y, ZZ: z_next(z) - z}
    out["div"] = out[XX] + out[YY] + out[ZZ]
    if XY in want:
        out[XY] = v[VX].next(row, count) - x + d_x[1]
    if XZ in want:
        out[XZ] = z_next(x) - x + d_x[2]
    if YZ in want:
        out[YZ] = z_next(y) - y + (v[VZ].next(row, count) - z)
    return out


def stress_rate(e, lame, shear, want=(XX, YY, ZZ, XY, XZ, YZ)):
    spread = lame * e["div"]
    return {
        c: spread + 2.0 * shear * e[c] if c in (XX, YY, ZZ) else shear * e[c] for c in want
    }


def cell_plane(active, out):
    shape = (BY, out.shape[1])
    for j in range(out.shape[0] // BY):
        row = jnp.full(shape, active[0, 0, j].astype(jnp.float32))
        for k in range(1, out.shape[1] // BZ):
            row = jnp.where(lanes(shape) >= k * BZ, active[0, k, j].astype(jnp.float32), row)
        out[j * BY : (j + 1) * BY, :] = row


def chunks(size):
    return range(0, size, ROWS)


def first_kernel(
    active,
    state_hbm,
    source_hbm,
    lame_hbm,
    shear_hbm,
    buoyancy_hbm,
    by_pair,
    by_next,
    state,
    st,
    coef,
    cells,
    v2,
    s2,
    msg,
    params,
    source,
    sems,
):
    width, size_y = state.shape[1], state.shape[2]
    last = width - 1
    copies = [
        pltpu.make_async_copy(array, params.at[n], sems.at[n])
        for n, array in enumerate((buoyancy_hbm, lame_hbm, shear_hbm))
    ]
    copies += [
        pltpu.make_async_copy(state_hbm.at[c], state.at[c], sems.at[3 + c])
        for c in (XX, XY, XZ, YY, YZ, ZZ, VX, VY, VZ)
    ]
    copies.append(pltpu.make_async_copy(source_hbm, source, sems.at[12]))
    for copy in copies:
        copy.start()
    cell_plane(active, cells)
    for copy in copies[:3]:
        copy.wait()

    def forced(step, x, row):
        return (
            time_step
            * cells[row : row + ROWS, :]
            * source[step, x, row : row + ROWS, :].astype(jnp.float32)
        )

    up, down = 0, 1
    for row in chunks(size_y):
        c = cells[row : row + ROWS, :]
        for x in range(width):
            for n in range(3):
                coef[n, x, row : row + ROWS, :] = time_step * c * params[n, x, row : row + ROWS, :]
    for copy in copies[3:]:
        copy.wait()

    def coefs(x, row):
        return [coef[n, x, row : row + ROWS, :] for n in range(3)]

    raw = [{c: Plane(state, c, x) for c in range(9)} for x in range(width)]
    one = [{c: Plane(st, c, x) for c in range(9)} for x in range(width)]
    two = {x: {c: Plane(v2, n, c) for c in (VX, VY, VZ)} for n, x in enumerate((0, 1, last))}
    for x in range(width):
        for row in chunks(size_y):
            c = cells[row : row + ROWS, :]
            cb = coefs(x, row)[0]
            terms = divergence(raw[x], raw[x - 1] if x else None, row, ROWS)
            for comp, term in zip((VX, VY, VZ), terms):
                value = c * raw[x][comp].at(row, ROWS) + cb * term
                if comp == VZ:
                    value = value + forced(0, x, row)
                one[x][comp].set(row, value)
    for x in range(width):
        for row in chunks(size_y):
            c = cells[row : row + ROWS, :]
            _, cl, cm = coefs(x, row)
            rate = stress_rate(strain(one[x], one[x + 1] if x < last else None, row, ROWS), cl, cm)
            for comp, term in rate.items():
                one[x][comp].set(row, c * raw[x][comp].at(row, ROWS) + term)
    for x in two:
        for row in chunks(size_y):
            cb = coefs(x, row)[0]
            terms = divergence(one[x], one[x - 1] if x else None, row, ROWS)
            for comp, term in zip((VX, VY, VZ), terms):
                value = one[x][comp].at(row, ROWS) + cb * term
                if comp == VZ:
                    value = value + forced(1, x, row)
                two[x][comp].set(row, value)
    stress = {c: Plane(s2, c) for c in range(9) if c >= XX}
    for row in chunks(size_y):
        _, cl, cm = coefs(0, row)
        rate = stress_rate(strain(two[0], two[1], row, ROWS), cl, cm)
        for comp, term in rate.items():
            stress[comp].set(row, one[0][comp].at(row, ROWS) + term)
        _, cl, cm = coefs(last, row)
        want = (XX, XY, XZ)
        rate = stress_rate(strain(two[last], None, row, ROWS, want), cl, cm, want)
        for n, comp in enumerate(want):
            here = slice(row, row + ROWS)
            msg[up, n, here] = raw[last][comp].at(row, ROWS)
            msg[up, 3 + n, here] = one[last][comp].at(row, ROWS)
            msg[up, 6 + n, here] = one[last][comp].at(row, ROWS) + rate[comp]
    for row in chunks(size_y):
        cb = coefs(0, row)[0]
        here = slice(row, row + ROWS)
        terms = divergence(stress, None, row, ROWS)
        for n, (comp, term) in enumerate(zip((VX, VY, VZ), terms)):
            value = two[0][comp].at(row, ROWS) + cb * term
            if comp == VZ:
                value = value + forced(2, 0, row)
            msg[down, n, here] = one[0][comp].at(row, ROWS)
            msg[down, 3 + n, here] = two[0][comp].at(row, ROWS)
            msg[down, 6 + n, here] = value
        for n in range(3):
            msg[up, CB + n, here] = coef[n, last, here]
            msg[down, CB + n, here] = coef[n, 0, here]
        msg[up, CB_NEXT, here] = coef[0, last, here]
        msg[down, CB_NEXT, here] = coef[0, 1, here]

    even = lax.rem(lax.axis_index("tile"), 2) == 0

    @pl.when(even)
    def _():
        by_pair[...] = msg[up]
        by_next[...] = msg[down]

    @pl.when(jnp.logical_not(even))
    def _():
        by_pair[...] = msg[down]
        by_next[...] = msg[up]


def main_kernel(
    groups,
    active,
    orientation,
    by_next,
    by_pair,
    state,
    st,
    coef,
    source,
    forward,
    final,
    *rest,
):
    images, (cells, got, end, w, low_s, high_v, d_s, d_v, image) = rest[:-9], rest[-9:]
    width, size_y = st.shape[1], st.shape[2]
    last = width - 1
    lo, hi = 0, 1
    cell_plane(active, cells)
    even = lax.rem(lax.axis_index("tile"), 2) == 0

    @pl.when(even)
    def _():
        got[lo] = by_next[...]
        got[hi] = by_pair[...]

    @pl.when(jnp.logical_not(even))
    def _():
        got[lo] = by_pair[...]
        got[hi] = by_next[...]

    def forced(step, x, row):
        return (
            time_step
            * cells[row : row + ROWS, :]
            * source[step, x, row : row + ROWS, :].astype(jnp.float32)
        )

    def coefs(x, row):
        here = slice(row, row + ROWS)
        if x < 0:
            return [got[lo, CB + n, here] for n in range(3)]
        if x > last:
            return [got[hi, CB + n, here] for n in range(3)]
        return [coef[n, x, here] for n in range(3)]

    vel, side, stress = (VX, VY, VZ), (XX, XY, XZ), (XX, YY, ZZ, XY, XZ, YZ)
    raw = [{c: Plane(state, c, x) for c in range(9)} for x in range(width)]
    one = [{c: Plane(st, c, x) for c in range(9)} for x in range(width)]
    base = one[last]
    one[0] = {c: Plane(end, 0, c) for c in range(9)}
    one[last] = {c: Plane(st if c in vel else end, *((c, last) if c in vel else (1, c))) for c in range(9)}
    two = [{c: Plane(w, c, x) for c in range(9)} for x in range(width)]
    three = [{c: Plane(final, c, x) for c in range(9)} for x in range(width)]
    sent_low = [{c: Plane(got, lo, 3 * k + n) for n, c in enumerate(side)} for k in range(3)]
    sent_high = [{c: Plane(got, hi, 3 * k + c) for c in vel} for k in range(3)]
    low_one, low_two = ({c: Plane(low_s, k, n) for n, c in enumerate(side)} for k in range(2))
    high = [{c: Plane(high_v, k, c) for c in vel} for k in range(3)]
    d_low_s = {c: Plane(d_s, 0, c - XX) for c in stress}
    d_high_s = {c: Plane(d_s, 1, c - XX) for c in stress}
    d_high_s_two = {c: Plane(d_s, 2, c - XX) for c in stress}
    d_high_v, d_high_v_two, d_far_v, d_low_v = ({c: Plane(d_v, k, c) for c in vel} for k in range(4))

    for row in chunks(size_y):
        cb, cb_high = coefs(0, row)[0], coefs(last + 1, row)[0]
        for comp, c in zip(vel, side):
            one[0][comp].set(
                row, Plane(st, comp, 0).at(row, ROWS) - cb * sent_low[0][c].at(row, ROWS)
            )
            delta = -cb_high * raw[last][c].at(row, ROWS)
            d_high_v[comp].set(row, delta)
            high[0][comp].set(row, sent_high[0][comp].at(row, ROWS) + delta)
    for row in chunks(size_y):
        c = cells[row : row + ROWS, :]
        _, cl, cm = coefs(0, row)
        for comp, term in stress_rate(strain(one[0], one[1], row, ROWS), cl, cm).items():
            one[0][comp].set(row, c * raw[0][comp].at(row, ROWS) + term)
        _, cl, cm = coefs(last, row)
        v = [high[0][comp].at(row, ROWS) for comp in vel]
        spread = cl * v[0]
        terms = {XX: spread + 2.0 * cm * v[0], YY: spread, ZZ: spread, XY: cm * v[1], XZ: cm * v[2]}
        for comp in stress:
            value = base[comp].at(row, ROWS)
            one[last][comp].set(row, value + terms[comp] if comp in terms else value)
        _, cl, cm = coefs(-1, row)
        v = [one[0][comp].at(row, ROWS) for comp in vel]
        spread = cl * v[0]
        terms = {XX: spread + 2.0 * cm * v[0], YY: spread, ZZ: spread, XY: cm * v[1], XZ: cm * v[2]}
        for comp, term in terms.items():
            d_low_s[comp].set(row, term)
        for comp in side:
            low_one[comp].set(row, sent_low[1][comp].at(row, ROWS) + terms[comp])
        _, cl, cm = coefs(last + 1, row)
        for comp, term in stress_rate(strain(d_high_v, None, row, ROWS), cl, cm).items():
            d_high_s[comp].set(row, term)

    for row in chunks(size_y):
        for x in range(width):
            cb = coefs(x, row)[0]
            terms = divergence(one[x], one[x - 1] if x else low_one, row, ROWS)
            for comp, term in zip(vel, terms):
                value = one[x][comp].at(row, ROWS) + cb * term
                if comp == VZ:
                    value = value + forced(1, x, row)
                two[x][comp].set(row, value)
        cb = coefs(last + 1, row)[0]
        for comp, term in zip(vel, divergence(d_high_s, one[last], row, ROWS)):
            value = d_high_v[comp].at(row, ROWS) + cb * term
            d_high_v_two[comp].set(row, value)
            high[1][comp].set(row, sent_high[1][comp].at(row, ROWS) + value)
        cb = got[hi, CB_NEXT, row : row + ROWS]
        for comp, c in zip(vel, side):
            d_far_v[comp].set(row, -cb * d_high_s[c].at(row, ROWS))
        cb = coefs(-1, row)[0]
        terms = divergence(d_low_s, None, row, ROWS, (XX, YY, ZZ, XY, XZ))
        for comp, term in zip(vel, terms):
            d_low_v[comp].set(row, cb * term)
    for row in chunks(size_y):
        for x in range(width):
            _, cl, cm = coefs(x, row)
            after = two[x + 1] if x < last else high[1]
            for comp, term in stress_rate(strain(two[x], after, row, ROWS), cl, cm).items():
                two[x][comp].set(row, one[x][comp].at(row, ROWS) + term)
        _, cl, cm = coefs(-1, row)
        rate = stress_rate(strain(d_low_v, two[0], row, ROWS, side), cl, cm, side)
        for comp, term in rate.items():
            value = sent_low[2][comp].at(row, ROWS) + d_low_s[comp].at(row, ROWS)
            low_two[comp].set(row, value + term)
        _, cl, cm = coefs(last + 1, row)
        for comp, term in stress_rate(strain(d_high_v_two, d_far_v, row, ROWS), cl, cm).items():
            d_high_s_two[comp].set(row, d_high_s[comp].at(row, ROWS) + term)

    for row in chunks(size_y):
        for x in range(width):
            cb = coefs(x, row)[0]
            terms = divergence(two[x], two[x - 1] if x else low_two, row, ROWS)
            for comp, term in zip(vel, terms):
                value = two[x][comp].at(row, ROWS) + cb * term
                if comp == VZ:
                    value = value + forced(2, x, row)
                three[x][comp].set(row, value)
        cb = coefs(last + 1, row)[0]
        for comp, term in zip(vel, divergence(d_high_s_two, two[last], row, ROWS)):
            value = d_high_v_two[comp].at(row, ROWS) + cb * term
            high[2][comp].set(row, sent_high[2][comp].at(row, ROWS) + value)
    for row in chunks(size_y):
        here = slice(row, row + ROWS)
        for x in range(width):
            _, cl, cm = coefs(x, row)
            after = three[x + 1] if x < last else high[2]
            rate = stress_rate(strain(three[x], after, row, ROWS), cl, cm)
            sums = {}
            for comp in stress:
                before = two[x][comp].at(row, ROWS)
                value = before + rate[comp]
                three[x][comp].set(row, value)
                sums[comp] = one[x][comp].at(row, ROWS) + before + value
            f = [forward[n, x, here].astype(jnp.float32) for n in range(9)]
            image[0, x, here] = (sums[XX] + sums[YY] + sums[ZZ]) * (f[0] + f[1] + f[2])
            total = sums[XX] * f[0]
            for n, comp in enumerate(stress[1:]):
                total = total + sums[comp] * f[n + 1]
            image[1, x, here] = total
            total = 0.0
            for comp in vel:
                moved = [k[x][comp].at(row, ROWS) for k in (one, two, three)]
                total = total + (moved[0] + moved[1] + moved[2]) * f[6 + comp]
            image[2, x, here] = total

    if groups != 2:
        images[0][...] = image[...]
        return
    give, keep = images
    me = lax.axis_index("shot")
    count = keep.shape[0] // (3 * width)
    mine = pl.multiple_of(me * (size_y - count), 8)
    theirs = pl.multiple_of((1 - me) * (size_y - count), 8)
    for n in range(3):
        for x in range(width):
            here = slice((n * width + x) * count, (n * width + x + 1) * count)
            give[here, :] = image[n, x, pl.ds(theirs, count), :]
            keep[here, :] = image[n, x, pl.ds(mine, count), :]
    blocks = orientation.shape[1]
    give[3 * width * count :, :] = class_tile(orientation, jnp.where(me == 0, blocks - 1, 0), keep.shape[1])


def class_tile(orientation, j, size_z):
    shape = (BY, size_z)
    out = jnp.full(shape, orientation[0, j, 0].astype(jnp.float32))
    for k in range(1, size_z // BZ):
        out = jnp.where(lanes(shape) >= k * BZ, orientation[0, j, k].astype(jnp.float32), out)
    return out


def y_prev(f):
    return jnp.where(rows(f.shape) == 0, 0.0, pltpu.roll(f, 1, f.ndim - 2))


def y_next(f):
    size = f.shape[-2]
    return jnp.where(rows(f.shape) == size - 1, 0.0, pltpu.roll(f, size - 1, f.ndim - 2))


def sweep(here, before, after, weights):
    w_x, w_y, w_z = weights
    twice = 2.0 * here
    along_x = -twice
    for plane in (before, after):
        if plane is not None:
            along_x = along_x + plane
    along_y = y_next(here) + y_prev(here) - twice
    along_z = z_next(here) + z_prev(here) - twice
    return here + (w_x * along_x + w_y * along_y + w_z * along_z)


def edge_row(me, own):
    return jnp.where(me == 0, own, BY - 1)


def sum_kernel(scale, orientation, keep, received, by_pair, by_next, grad, swept, weights, classes, msg):
    width, count, size_z = grad.shape[1:]
    own = count - BY
    me = lax.axis_index("shot")
    first = pl.multiple_of(me * BY, BY)
    for j in range(own // BY):
        classes[pl.ds(first + j * BY, BY), :] = class_tile(orientation, j, size_z)
    beyond = pl.multiple_of((1 - me) * own, BY)
    classes[pl.ds(beyond, BY), :] = received[3 * width * count :, :]
    klass = classes[...]
    for column in range(3):
        table = jnp.full(klass.shape, weight_table[3][column], jnp.float32)
        for k in range(3):
            table = jnp.where(klass == k, weight_table[k][column], table)
        weights[column] = smooth_rate * table
    for n in range(3):
        for x in range(width):
            here = slice((n * width + x) * count, (n * width + x + 1) * count)
            grad[n, x] = (keep[here, :] + received[here, :]) * scale
    w = [weights[k] for k in range(3)]
    for n in range(3):
        for x in range(width):
            swept[n, x] = sweep(
                grad[n, x],
                grad[n, x - 1] if x else None,
                grad[n, x + 1] if x < width - 1 else None,
                w,
            )
    edge = edge_row(me, own)
    mine = pl.ds(first, own)
    for to, x in ((0, width - 1), (1, 0)):
        msg[to, 6 * own :, :] = jnp.zeros((BY, size_z), jnp.float32)
        for n in range(3):
            msg[to, 2 * n * own : (2 * n + 1) * own, :] = grad[n, x, mine, :]
            msg[to, (2 * n + 1) * own : (2 * n + 2) * own, :] = swept[n, x, mine, :]
            msg[to, 6 * own + n : 6 * own + n + 1, :] = grad[n, x, pl.ds(edge, 1), :]
        for j in range(own // BY):
            row = weights[0, pl.ds(pl.multiple_of(first + j * BY, BY), BY), :][0:1]
            msg[to, 6 * own + 3 + j : 6 * own + 4 + j, :] = row
    even = lax.rem(lax.axis_index("tile"), 2) == 0

    @pl.when(even)
    def _():
        by_pair[...] = msg[0]
        by_next[...] = msg[1]

    @pl.when(jnp.logical_not(even))
    def _():
        by_pair[...] = msg[1]
        by_next[...] = msg[0]


def smooth_kernel(by_next, by_pair, grad, swept, weights, out, got, beside, full, result):
    width, count, size_z = grad.shape[1:]
    own = count - BY
    last = width - 1
    even = lax.rem(lax.axis_index("tile"), 2) == 0
    me = lax.axis_index("shot")
    first = pl.multiple_of(me * BY, BY)
    mine = pl.ds(first, own)

    @pl.when(even)
    def _():
        got[0] = by_next[...]
        got[1] = by_pair[...]

    @pl.when(jnp.logical_not(even))
    def _():
        got[0] = by_pair[...]
        got[1] = by_next[...]

    edge = edge_row(me, own)
    beside[...] = jnp.zeros(beside.shape, jnp.float32)
    for side, x in ((0, 0), (1, last)):
        for n in range(3):
            beside[side, n, mine, :] = got[side, 2 * n * own : (2 * n + 1) * own, :]
            beside[side, n, pl.ds(edge, 1), :] = got[side, 6 * own + n : 6 * own + n + 1, :]
            beside[side, 3 + n, mine, :] = got[side, (2 * n + 1) * own : (2 * n + 2) * own, :]
        for j in range(own // BY):
            row = got[side, 6 * own + 3 + j : 6 * own + 4 + j, :]
            here = pl.ds(pl.multiple_of(first + j * BY, BY), BY)
            beside[side, 6, here, :] = jnp.broadcast_to(row, (BY, size_z))
    w = [weights[k] for k in range(3)]
    for n in range(3):
        for x in range(width):
            value = swept[n, x]
            if x == 0:
                value = value + w[0] * beside[0, n]
            if x == last:
                value = value + w[0] * beside[1, n]
            full[x + 1] = value
        full[0] = beside[0, 3 + n] + beside[0, 6] * grad[n, 0]
        full[width + 1] = beside[1, 3 + n] + beside[1, 6] * grad[n, last]
        for x in range(width):
            result[...] = sweep(full[x + 1], full[x], full[x + 2], w)
            out[n, x] = result[mine, :]


def extended(block, sides, width):
    for axis, dim in sides:
        count = lax.axis_size(axis)
        forward = [(i, i + 1) for i in range(count - 1)]
        backward = [(target, source) for source, target in forward]
        low = lax.ppermute(
            lax.slice_in_dim(block, block.shape[dim] - width, None, axis=dim), axis, forward
        )
        high = lax.ppermute(lax.slice_in_dim(block, 0, width, axis=dim), axis, backward)
        block = jnp.concatenate([low, block, high], axis=dim)
    return block


def smooth_anywhere(image, orientation):
    groups = lax.axis_size("shot")
    owned = image.shape[2] // groups
    total = lax.psum(image, "shot")
    grad = lax.dynamic_slice_in_dim(total, lax.axis_index("shot") * owned, owned, 2)
    grad = grad * (STEPS * groups) ** (-0.5)
    weights = []
    for column in range(3):
        table = jnp.zeros(orientation.shape, jnp.float32)
        for klass in range(4):
            table = table + (orientation == klass).astype(jnp.float32) * weight_table[klass][column]
        table = jnp.repeat(jnp.repeat(table, image.shape[1], 0), BY, 1)
        weights.append(jnp.repeat(table, BZ, 2))
    for _ in range(SWEEPS):
        padded = extended(grad, (("shot", 2), ("tile", 1)), 1)
        padded = jnp.pad(padded, ((0, 0), (0, 0), (0, 0), (1, 1)))
        center = padded[:, 1:-1, 1:-1, 1:-1]
        lap_x = padded[:, 2:, 1:-1, 1:-1] + padded[:, :-2, 1:-1, 1:-1] - 2.0 * center
        lap_y = padded[:, 1:-1, 2:, 1:-1] + padded[:, 1:-1, :-2, 1:-1] - 2.0 * center
        lap_z = padded[:, 1:-1, 1:-1, 2:] + padded[:, 1:-1, 1:-1, :-2] - 2.0 * center
        grad = grad + smooth_rate * (weights[0] * lap_x + weights[1] * lap_y + weights[2] * lap_z)
    return grad


def both_ways(by_pair, by_next):
    count = lax.axis_size("tile")
    out = []
    for array, start in ((by_next, 1), (by_pair, 0)):
        pairs = [(i, i + 1) for i in range(start, count - 1, 2)]
        out.append(lax.ppermute(array, "tile", pairs + [(b, a) for a, b in pairs]))
    return out[1], out[0]


def in_hbm(array):
    return pltpu.with_memory_space_constraint(array, pltpu.HBM)


def f32(*shape):
    return jax.ShapeDtypeStruct(shape, jnp.float32)


def call(kernel, outs, args, scratch, scalars=0, space=VMEM):
    return pl.pallas_call(
        kernel,
        out_shape=outs,
        in_specs=[SMEM] * scalars + [space] * (len(args) - scalars),
        out_specs=jax.tree.map(lambda _: VMEM, outs),
        scratch_shapes=[
            pltpu.VMEM(shape, jnp.float32) if isinstance(shape, tuple) else shape
            for shape in scratch
        ],
        compiler_params=pltpu.CompilerParams(vmem_limit_bytes=24 * 1024 * 1024),
    )(*args)


def local(
    adjoint_state,
    adjoint_source,
    forward_field,
    lame_first,
    shear_modulus,
    buoyancy,
    active_blocks,
    orientation,
):
    width, size_y, size_z = lame_first.shape
    plane = (size_y, size_z)
    groups = lax.axis_size("shot")
    state, source, forward = adjoint_state[0], adjoint_source[0], forward_field[0]
    active = jnp.swapaxes(active_blocks, 1, 2)
    grid = f32(9, width, *plane)
    by_pair, by_next, raw, st, coef = call(
        first_kernel,
        (f32(PLANES, *plane), f32(PLANES, *plane), grid, grid, f32(3, width, *plane)),
        [in_hbm(a) for a in (active, state, source, lame_first, shear_modulus, buoyancy)],
        [
            plane,
            (3, 3, *plane),
            (9, *plane),
            (2, PLANES, *plane),
            (3, width, *plane),
            pltpu.VMEM(source.shape, source.dtype),
            pltpu.SemaphoreType.DMA((13,)),
        ],
        1,
        HBM,
    )
    by_pair, by_next = both_ways(by_pair, by_next)
    owned = size_y // groups
    count = owned + BY
    if groups == 2:
        images = (f32(3 * width * count + BY, size_z), f32(3 * width * count, size_z))
    else:
        images = (f32(3, width, *plane),)
    final, *images = call(
        functools.partial(main_kernel, groups),
        (f32(9, width, *plane), *images),
        (active, orientation, by_next, by_pair, raw, st, coef, source, forward),
        [
            plane,
            (2, PLANES, *plane),
            (2, 9, *plane),
            (9, width, *plane),
            (2, 3, *plane),
            (3, 3, *plane),
            (3, 6, *plane),
            (4, 3, *plane),
            (3, width, *plane),
        ],
        2,
    )
    if groups != 2:
        return final[None], smooth_anywhere(images[0], orientation)
    give, keep = images
    received = lax.ppermute(give, "shot", [(0, 1), (1, 0)])
    block = (3, width, count, size_z)
    by_pair, by_next, grad, swept, weights = call(
        functools.partial(sum_kernel, (STEPS * groups) ** (-0.5)),
        (f32(6 * owned + BY, size_z), f32(6 * owned + BY, size_z), f32(*block), f32(*block), f32(3, count, size_z)),
        (orientation, keep, received),
        [(count, size_z), (2, 6 * owned + BY, size_z)],
        1,
    )
    by_pair, by_next = both_ways(by_pair, by_next)
    gradient = call(
        smooth_kernel,
        f32(3, width, owned, size_z),
        (by_next, by_pair, grad, swept, weights),
        [
            (2, 6 * owned + BY, size_z),
            (2, 7, count, size_z),
            (width + 2, count, size_z),
            (count, size_z),
        ],
    )
    return final[None], gradient


def solution(mesh):
    return jax.shard_map(
        local,
        mesh=mesh,
        in_specs=(
            P("shot", None, "tile", None, None),
            P("shot", None, "tile", None, None),
            P("shot", None, "tile", None, None),
            P("tile", None, None),
            P("tile", None, None),
            P("tile", None, None),
            P("tile", None, None),
            P("tile", "shot", None),
        ),
        out_specs=(P("shot", None, "tile", None, None), P(None, "tile", "shot", None)),
        check_vma=False,
    )
```

```python
import functools

import jax
import jax.numpy as jnp
from jax import lax
from jax.experimental import pallas as pl
from jax.experimental.pallas import tpu as pltpu
from jax.sharding import PartitionSpec as P

BY = 8
BZ = 32
STEPS = 3
SWEEPS = 2

time_step = 0.25
smooth_rate = 0.1
weight_table = ((1.0, 1.0, 0.25), (0.25, 1.0, 1.0), (1.0, 0.25, 1.0), (0.6, 0.6, 0.6))

VX, VY, VZ, XX, YY, ZZ, XY, XZ, YZ = range(9)
VEL = (VX, VY, VZ)
SIDE = (XX, XY, XZ)
STRESS = (XX, YY, ZZ, XY, XZ, YZ)
ROWS = 32
VMEM = pl.BlockSpec(memory_space=pltpu.VMEM)
SMEM = pl.BlockSpec(memory_space=pltpu.SMEM)
HBM = pl.BlockSpec(memory_space=pltpu.HBM)


def lanes(shape):
    return lax.broadcasted_iota(jnp.int32, shape, len(shape) - 1)


def rows(shape):
    return lax.broadcasted_iota(jnp.int32, shape, len(shape) - 2)


def z_prev(f):
    return jnp.where(lanes(f.shape) == 0, 0.0, pltpu.roll(f, 1, f.ndim - 1))


def z_next(f):
    size = f.shape[-1]
    return jnp.where(lanes(f.shape) == size - 1, 0.0, pltpu.roll(f, size - 1, f.ndim - 1))


class Plane:
    def __init__(self, ref, *index):
        self.ref, self.index = ref, index
        self.size = ref.shape[len(index)]

    def at(self, row, count):
        return self.ref[self.index + (slice(row, row + count),)]

    def prev(self, row, count):
        if row:
            return self.at(row - 1, count)
        edge = pltpu.roll(self.at(0, 8), 1, 0)
        edge = jnp.where(rows(edge.shape) == 0, 0.0, edge)
        return jnp.concatenate([edge, self.at(7, count - 8)], 0)

    def next(self, row, count):
        if row + count < self.size:
            return self.at(row + 1, count)
        edge = pltpu.roll(self.at(self.size - 8, 8), 7, 0)
        edge = jnp.where(rows(edge.shape) == 7, 0.0, edge)
        return jnp.concatenate([self.at(row + 1, count - 8), edge], 0)

    def set(self, row, value):
        self.ref[self.index + (slice(row, row + value.shape[0]),)] = value


def planes(ref, comps, *index):
    return {c: Plane(ref, n, *index) for n, c in enumerate(comps)}


def divergence(s, before, row, count, have=(XX, YY, ZZ, XY, XZ, YZ)):
    def along_x(c):
        here = s[c].at(row, count)
        return here - before[c].at(row, count) if before is not None else here

    def along_y(c):
        return s[c].at(row, count) - s[c].prev(row, count)

    def along_z(c):
        here = s[c].at(row, count)
        return here - z_prev(here)

    out = []
    for c_x, c_y, c_z in ((XX, XY, XZ), (XY, YY, YZ), (XZ, YZ, ZZ)):
        terms = along_x(c_x)
        if c_y in have:
            terms = terms + along_y(c_y)
        if c_z in have:
            terms = terms + along_z(c_z)
        out.append(terms)
    return out


def strain(v, after, row, count, want=(XX, YY, ZZ, XY, XZ, YZ)):
    x, y, z = (v[c].at(row, count) for c in (VX, VY, VZ))
    if after is None:
        d_x = [-x, -y, -z]
    else:
        d_x = [after[c].at(row, count) - f for c, f in ((VX, x), (VY, y), (VZ, z))]
    out = {XX: d_x[0], YY: v[VY].next(row, count) - y, ZZ: z_next(z) - z}
    out["div"] = out[XX] + out[YY] + out[ZZ]
    if XY in want:
        out[XY] = v[VX].next(row, count) - x + d_x[1]
    if XZ in want:
        out[XZ] = z_next(x) - x + d_x[2]
    if YZ in want:
        out[YZ] = z_next(y) - y + (v[VZ].next(row, count) - z)
    return out


def stress_rate(e, lame, shear, want=(XX, YY, ZZ, XY, XZ, YZ)):
    spread = lame * e["div"]
    return {
        c: spread + 2.0 * shear * e[c] if c in (XX, YY, ZZ) else shear * e[c] for c in want
    }


def cell_plane(active, out):
    shape = (BY, out.shape[1])
    for j in range(out.shape[0] // BY):
        row = jnp.full(shape, active[0, 0, j].astype(jnp.float32))
        for k in range(1, out.shape[1] // BZ):
            row = jnp.where(lanes(shape) >= k * BZ, active[0, k, j].astype(jnp.float32), row)
        out[j * BY : (j + 1) * BY, :] = row


def chunks(size):
    return range(0, size, ROWS)


def is_even():
    return lax.rem(lax.axis_index("tile"), 2) == 0


def hand_out(by_pair, by_next, up, down):
    even = is_even()

    @pl.when(even)
    def _():
        by_pair[...] = up[...]
        by_next[...] = down[...]

    @pl.when(jnp.logical_not(even))
    def _():
        by_pair[...] = down[...]
        by_next[...] = up[...]


def take_in(by_pair, by_next, low, high):
    even = is_even()

    @pl.when(even)
    def _():
        low[...] = by_next[...]
        high[...] = by_pair[...]

    @pl.when(jnp.logical_not(even))
    def _():
        low[...] = by_pair[...]
        high[...] = by_next[...]


def class_tile(orientation, j, size_z):
    shape = (BY, size_z)
    out = jnp.full(shape, orientation[0, j, 0].astype(jnp.float32))
    for k in range(1, size_z // BZ):
        out = jnp.where(lanes(shape) >= k * BZ, orientation[0, j, k].astype(jnp.float32), out)
    return out


def here(row):
    return slice(row, row + ROWS)


def early_kernel(
    groups,
    active,
    orientation,
    state_hbm,
    source_hbm,
    lame_hbm,
    shear_hbm,
    buoyancy_hbm,
    by_pair,
    by_next,
    state,
    source,
    coef,
    cells,
    tile,
    up,
    down,
    params,
    sems,
):
    width, size_y, size_z = state.shape[1:]
    last = width - 1
    copies = [
        pltpu.make_async_copy(array, params.at[n], sems.at[n])
        for n, array in enumerate((buoyancy_hbm, lame_hbm, shear_hbm))
    ]
    copies += [
        pltpu.make_async_copy(state_hbm.at[c], state.at[c], sems.at[3 + c])
        for c in (XX, XY, XZ, YY, YZ, ZZ, VX, VY, VZ)
    ]
    copies.append(pltpu.make_async_copy(source_hbm, source, sems.at[12]))
    for copy in copies:
        copy.start()
    cell_plane(active, cells)
    me = lax.axis_index("shot") if groups == 2 else 0
    blocks = orientation.shape[1]
    tile[...] = class_tile(orientation, jnp.where(me == 0, blocks - 1, 0), size_z)
    for copy in copies[:3]:
        copy.wait()
    for row in chunks(size_y):
        c = time_step * cells[here(row), :]
        for x in range(width):
            for n in range(3):
                coef[n, x, here(row)] = c * params[n, x, here(row)]
    count = (up.shape[0] - 3 * size_y) // 4
    mine = pl.ds(pl.multiple_of(me * count, 8), count) if groups == 2 else slice(0, count)
    for n in range(4):
        to = slice(3 * size_y + n * count, 3 * size_y + (n + 1) * count)
        up[to] = coef[n % 3, last, mine]
        down[to] = coef[n % 3, n // 3, mine]
    for copy in copies[3:]:
        copy.wait()
    raw = {c: Plane(state, c, 0) for c in range(9)}
    for row in chunks(size_y):
        c, cb = cells[here(row), :], coef[0, 0, here(row)]
        for n, term in enumerate(divergence(raw, None, row, ROWS)):
            value = c * raw[n].at(row, ROWS) + cb * term
            if n == VZ:
                push = source[0, 0, here(row)].astype(jnp.float32)
                value = value + time_step * c * push
            to = slice(n * size_y + row, n * size_y + row + ROWS)
            down[to] = value
            up[to] = state[SIDE[n], last, here(row)]
    hand_out(by_pair, by_next, up, down)


def late_kernel(state, source, coef, cells, by_pair, by_next, st, push, v2, s2, up, down):
    width, size_y = state.shape[1], state.shape[2]
    last = width - 1
    for row in chunks(size_y):
        c = time_step * cells[here(row), :]
        for step in range(STEPS):
            for x in range(width):
                push[step, x, here(row)] = c * source[step, x, here(row)].astype(jnp.float32)

    def coefs(x, row):
        return [coef[n, x, here(row)] for n in range(3)]

    raw = [{c: Plane(state, c, x) for c in range(9)} for x in range(width)]
    one = [{c: Plane(st, c, x) for c in range(9)} for x in range(width)]
    two = {x: {c: Plane(v2, n, c) for c in VEL} for n, x in enumerate((0, 1, last))}
    for x in range(width):
        for row in chunks(size_y):
            c = cells[here(row), :]
            cb = coefs(x, row)[0]
            terms = divergence(raw[x], raw[x - 1] if x else None, row, ROWS)
            for comp, term in zip(VEL, terms):
                value = c * raw[x][comp].at(row, ROWS) + cb * term
                if comp == VZ:
                    value = value + push[0, x, here(row)]
                one[x][comp].set(row, value)
    for x in range(width):
        for row in chunks(size_y):
            c = cells[here(row), :]
            _, cl, cm = coefs(x, row)
            rate = stress_rate(strain(one[x], one[x + 1] if x < last else None, row, ROWS), cl, cm)
            for comp, term in rate.items():
                one[x][comp].set(row, c * raw[x][comp].at(row, ROWS) + term)
    for x in two:
        for row in chunks(size_y):
            cb = coefs(x, row)[0]
            terms = divergence(one[x], one[x - 1] if x else None, row, ROWS)
            for comp, term in zip(VEL, terms):
                value = one[x][comp].at(row, ROWS) + cb * term
                if comp == VZ:
                    value = value + push[1, x, here(row)]
                two[x][comp].set(row, value)
    stress = {c: Plane(s2, c - XX) for c in STRESS}
    for row in chunks(size_y):
        _, cl, cm = coefs(0, row)
        rate = stress_rate(strain(two[0], two[1], row, ROWS), cl, cm)
        for comp, term in rate.items():
            stress[comp].set(row, one[0][comp].at(row, ROWS) + term)
        _, cl, cm = coefs(last, row)
        rate = stress_rate(strain(two[last], None, row, ROWS, SIDE), cl, cm, SIDE)
        for n, comp in enumerate(SIDE):
            value = one[last][comp].at(row, ROWS)
            up[n, here(row)] = value
            up[3 + n, here(row)] = value + rate[comp]
    for row in chunks(size_y):
        cb = coefs(0, row)[0]
        terms = divergence(stress, None, row, ROWS)
        for comp, term in zip(VEL, terms):
            before = two[0][comp].at(row, ROWS)
            value = before + cb * term
            if comp == VZ:
                value = value + push[2, 0, here(row)]
            down[comp, here(row)] = before
            down[3 + comp, here(row)] = value
    hand_out(by_pair, by_next, up, down)


def beyond(v, cl, cm):
    spread = cl * v[0]
    return {XX: spread + 2.0 * cm * v[0], YY: spread, ZZ: spread, XY: cm * v[1], XZ: cm * v[2]}


def own_planes(st, end):
    width = st.shape[1]
    one = [{c: Plane(st, c, x) for c in range(9)} for x in range(width)]
    one[0] = {c: Plane(end, 0, c) for c in range(9)}
    one[-1] = {c: Plane(st, c, width - 1) if c in VEL else Plane(end, 1, c) for c in range(9)}
    return one


def near_kernel(groups, *refs):
    by_pair, by_next, *refs = refs
    if groups == 2:
        swapped, orientation, *refs = refs
    state, st, coef, cells, push, end, w, third, outer, parts, *refs = refs
    if groups == 2:
        weights, *refs = refs
    low, high, high_v, d_s, d_v, *classes = refs
    width, size_y = st.shape[1], st.shape[2]
    last = width - 1
    take_in(by_pair, by_next, low, high)
    count = (low.shape[0] - 3 * size_y) // 4
    base = 3 * size_y
    if groups == 2:
        me = lax.axis_index("shot")
        mine = pl.ds(pl.multiple_of(me * count, 8), count)
        theirs = pl.ds(pl.multiple_of((1 - me) * count, 8), count)
        low_at = pl.multiple_of(jnp.where(is_even(), 4 * count, 0), 8)
        high_at = pl.multiple_of(jnp.where(is_even(), 0, 4 * count), 8)
        for n in range(4):
            if n < 3:
                outer[n, mine] = low[base + n * count : base + (n + 1) * count]
                outer[n, theirs] = swapped[pl.ds(low_at + n * count, count)]
            outer[3 + n, mine] = high[base + n * count : base + (n + 1) * count]
            outer[3 + n, theirs] = swapped[pl.ds(high_at + n * count, count)]
    else:
        for n in range(4):
            if n < 3:
                outer[n] = low[base + n * count : base + (n + 1) * count]
            outer[3 + n] = high[base + n * count : base + (n + 1) * count]

    def coefs(x, row):
        if x < 0:
            return [outer[n, here(row)] for n in range(3)]
        if x > last:
            return [outer[3 + n, here(row)] for n in range(3)]
        return [coef[n, x, here(row)] for n in range(3)]

    raw = [{c: Plane(state, c, x) for c in range(9)} for x in range(width)]
    old = [{c: Plane(st, c, x) for c in range(9)} for x in range(width)]
    one = own_planes(st, end)
    two = [{c: Plane(w, c, x) for c in range(9)} for x in range(width)]
    high_one = {c: Plane(high_v, c) for c in VEL}
    d_low_s, d_high_s, d_high_s_two = ({c: Plane(d_s, k, c - XX) for c in STRESS} for k in range(3))
    d_high_v, d_far_v, d_low_v = ({c: Plane(d_v, k, c) for c in VEL} for k in range(3))
    part_v, part_low, d_high_v_two, part_high = (
        {c: Plane(parts, k, n) for n, c in enumerate(names)}
        for k, names in enumerate((VEL, SIDE, VEL, VEL))
    )

    for row in chunks(size_y):
        cb, cb_high = coefs(0, row)[0], coefs(last + 1, row)[0]
        for n, (comp, c) in enumerate(zip(VEL, SIDE)):
            at = slice(n * size_y + row, n * size_y + row + ROWS)
            one[0][comp].set(row, old[0][comp].at(row, ROWS) - cb * low[at])
            delta = -cb_high * raw[last][c].at(row, ROWS)
            d_high_v[comp].set(row, delta)
            high_one[comp].set(row, high[at] + delta)
    for row in chunks(size_y):
        c = cells[here(row), :]
        _, cl, cm = coefs(0, row)
        for comp, term in stress_rate(strain(one[0], one[1], row, ROWS), cl, cm).items():
            one[0][comp].set(row, c * raw[0][comp].at(row, ROWS) + term)
        _, cl, cm = coefs(last, row)
        terms = beyond([high_one[comp].at(row, ROWS) for comp in VEL], cl, cm)
        for comp in STRESS:
            value = old[last][comp].at(row, ROWS)
            one[last][comp].set(row, value + terms[comp] if comp in terms else value)
        _, cl, cm = coefs(-1, row)
        for comp, term in beyond([one[0][comp].at(row, ROWS) for comp in VEL], cl, cm).items():
            d_low_s[comp].set(row, term)
        _, cl, cm = coefs(last + 1, row)
        for comp, term in stress_rate(strain(d_high_v, None, row, ROWS), cl, cm).items():
            d_high_s[comp].set(row, term)

    for row in chunks(size_y):
        for x in range(width):
            cb = coefs(x, row)[0]
            terms = divergence(one[x], one[x - 1] if x else d_low_s, row, ROWS)
            for comp, term in zip(VEL, terms):
                value = one[x][comp].at(row, ROWS) + cb * term
                if comp == VZ:
                    value = value + push[1, x, here(row)]
                (two[x] if x else part_v)[comp].set(row, value)
        cb = coefs(last + 1, row)[0]
        for comp, term in zip(VEL, divergence(d_high_s, one[last], row, ROWS)):
            d_high_v_two[comp].set(row, d_high_v[comp].at(row, ROWS) + cb * term)
        cb = outer[6, here(row)]
        for comp, c in zip(VEL, SIDE):
            d_far_v[comp].set(row, -cb * d_high_s[c].at(row, ROWS))
        cb = coefs(-1, row)[0]
        terms = divergence(d_low_s, None, row, ROWS, (XX, YY, ZZ, XY, XZ))
        for comp, term in zip(VEL, terms):
            d_low_v[comp].set(row, cb * term)
    for row in chunks(size_y):
        for x in range(1, width):
            _, cl, cm = coefs(x, row)
            after = two[x + 1] if x < last else None
            for comp, term in stress_rate(strain(two[x], after, row, ROWS), cl, cm).items():
                two[x][comp].set(row, one[x][comp].at(row, ROWS) + term)
        _, cl, cm = coefs(-1, row)
        rate = stress_rate(strain(d_low_v, None, row, ROWS, SIDE), cl, cm, SIDE)
        for comp, term in rate.items():
            part_low[comp].set(row, d_low_s[comp].at(row, ROWS) + term)
        _, cl, cm = coefs(last + 1, row)
        for comp, term in stress_rate(strain(d_high_v_two, d_far_v, row, ROWS), cl, cm).items():
            d_high_s_two[comp].set(row, d_high_s[comp].at(row, ROWS) + term)
    for row in chunks(size_y):
        cb = coefs(last + 1, row)[0]
        for comp, term in zip(VEL, divergence(d_high_s_two, None, row, ROWS)):
            part_high[comp].set(row, d_high_v_two[comp].at(row, ROWS) + cb * term)
        for x in range(2, last):
            cb = coefs(x, row)[0]
            for comp, term in zip(VEL, divergence(two[x], two[x - 1], row, ROWS)):
                value = two[x][comp].at(row, ROWS) + cb * term
                if comp == VZ:
                    value = value + push[2, x, here(row)]
                third[comp, x, here(row)] = value
    if groups != 2:
        return

    (classes,) = classes
    rows_held = weights.shape[1]
    own = rows_held - BY
    first = pl.multiple_of(me * BY, BY)
    for j in range(own // BY):
        classes[pl.ds(first + j * BY, BY), :] = class_tile(orientation, j, weights.shape[2])
    classes[pl.ds(pl.multiple_of((1 - me) * own, BY), BY), :] = swapped[8 * count :, :]
    klass = classes[...]
    for column in range(3):
        table = jnp.full(klass.shape, weight_table[3][column], jnp.float32)
        for k in range(3):
            table = jnp.where(klass == k, weight_table[k][column], table)
        weights[column] = smooth_rate * table


def far_kernel(groups, *refs):
    by_pair, by_next, st, end, w, third, outer, parts, coef, push, forward, final, *refs = refs
    *images, low, high, edge, low_s, high_v, image = refs
    width, size_y = st.shape[1], st.shape[2]
    last = width - 1
    take_in(by_pair, by_next, low, high)

    def coefs(x, row):
        if x < 0:
            return [outer[n, here(row)] for n in range(3)]
        if x > last:
            return [outer[3 + n, here(row)] for n in range(3)]
        return [coef[n, x, here(row)] for n in range(3)]

    one = own_planes(st, end)
    part = [{c: Plane(w, c, x) for c in range(9)} for x in range(width)]
    two = [dict(p) for p in part]
    for c in range(9):
        two[0][c] = Plane(edge, 0, c)
        if c >= XX:
            two[last][c] = Plane(edge, 1, c)
    three = [{c: Plane(final, c, x) for c in range(9)} for x in range(width)]
    part_v, part_low, d_high_v_two, part_high = (
        {c: Plane(parts, k, n) for n, c in enumerate(names)}
        for k, names in enumerate((VEL, SIDE, VEL, VEL))
    )
    low_two = {c: Plane(low_s, n) for n, c in enumerate(SIDE)}
    high_three = {c: Plane(high_v, c) for c in VEL}

    for row in chunks(size_y):
        cb = coefs(0, row)[0]
        moved = []
        for n, comp in enumerate(VEL):
            moved.append(part_v[comp].at(row, ROWS) - cb * low[n, here(row)])
            two[0][comp].set(row, moved[n])
        _, cl, cm = coefs(-1, row)
        terms = beyond(moved, cl, cm)
        for n, comp in enumerate(SIDE):
            value = low[3 + n, here(row)] + part_low[comp].at(row, ROWS)
            low_two[comp].set(row, value + terms[comp])
        _, cl, cm = coefs(last, row)
        cb = coefs(last + 1, row)[0]
        moved = [high[n, here(row)] + d_high_v_two[n].at(row, ROWS) for n in VEL]
        terms = beyond(moved, cl, cm)
        values = {}
        for comp in STRESS:
            value = part[last][comp].at(row, ROWS)
            values[comp] = value + terms[comp] if comp in terms else value
            two[last][comp].set(row, values[comp])
        for n, comp in enumerate(SIDE):
            value = high[3 + n, here(row)] + part_high[n].at(row, ROWS)
            high_three[n].set(row, value - cb * values[comp])
    for row in chunks(size_y):
        _, cl, cm = coefs(0, row)
        for comp, term in stress_rate(strain(two[0], two[1], row, ROWS), cl, cm).items():
            two[0][comp].set(row, one[0][comp].at(row, ROWS) + term)

    for row in chunks(size_y):
        for x in range(width):
            if 2 <= x < last:
                for comp in VEL:
                    three[x][comp].set(row, third[comp, x, here(row)])
                continue
            cb = coefs(x, row)[0]
            terms = divergence(two[x], two[x - 1] if x else low_two, row, ROWS)
            for comp, term in zip(VEL, terms):
                value = two[x][comp].at(row, ROWS) + cb * term
                if comp == VZ:
                    value = value + push[2, x, here(row)]
                three[x][comp].set(row, value)
    for row in chunks(size_y):
        for x in range(width):
            _, cl, cm = coefs(x, row)
            after = three[x + 1] if x < last else high_three
            rate = stress_rate(strain(three[x], after, row, ROWS), cl, cm)
            sums = {}
            for comp in STRESS:
                before = two[x][comp].at(row, ROWS)
                value = before + rate[comp]
                three[x][comp].set(row, value)
                sums[comp] = one[x][comp].at(row, ROWS) + before + value
            f = [forward[n, x, here(row)].astype(jnp.float32) for n in range(9)]
            image[0, x, here(row)] = (sums[XX] + sums[YY] + sums[ZZ]) * (f[0] + f[1] + f[2])
            total = sums[XX] * f[0]
            for n, comp in enumerate(STRESS[1:]):
                total = total + sums[comp] * f[n + 1]
            image[1, x, here(row)] = total
            total = 0.0
            for comp in VEL:
                moved = [k[x][comp].at(row, ROWS) for k in (one, two, three)]
                total = total + (moved[0] + moved[1] + moved[2]) * f[6 + comp]
            image[2, x, here(row)] = total

    if groups != 2:
        images[0][...] = image[...]
        return
    give, keep = images
    me = lax.axis_index("shot")
    count = keep.shape[2]
    mine = pl.ds(pl.multiple_of(me * (size_y - count), 8), count)
    theirs = pl.ds(pl.multiple_of((1 - me) * (size_y - count), 8), count)
    for n in range(3):
        for x in range(width):
            give[n, x] = image[n, x, theirs, :]
            keep[n, x] = image[n, x, mine, :]


def y_prev(f):
    return jnp.where(rows(f.shape) == 0, 0.0, pltpu.roll(f, 1, f.ndim - 2))


def y_next(f):
    size = f.shape[-2]
    return jnp.where(rows(f.shape) == size - 1, 0.0, pltpu.roll(f, size - 1, f.ndim - 2))


def sweep(g, before, after, weights):
    w_x, w_y, w_z = weights
    twice = 2.0 * g
    along_x = -twice
    for plane in (before, after):
        if plane is not None:
            along_x = along_x + plane
    along_y = y_next(g) + y_prev(g) - twice
    along_z = z_next(g) + z_prev(g) - twice
    return g + (w_x * along_x + w_y * along_y + w_z * along_z)


def edge_row(me, own):
    return jnp.where(me == 0, own, BY - 1)


def sum_kernel(scale, keep, received, weights, by_pair, by_next, grad, swept, up, down):
    width, count, size_z = grad.shape[1:]
    own = count - BY
    me = lax.axis_index("shot")
    first = pl.multiple_of(me * BY, BY)
    mine = pl.ds(first, own)
    edge = pl.ds(edge_row(me, own), 1)
    last = width - 1
    w = [weights[k] for k in range(3)]
    for to in (up, down):
        to[6 * own :, :] = jnp.zeros((BY, size_z), jnp.float32)
        for j in range(own // BY):
            row = weights[0, pl.ds(pl.multiple_of(first + j * BY, BY), BY), :][0:1]
            to[6 * own + 3 + j : 6 * own + 4 + j, :] = row
    for n in range(3):
        for x in range(width):
            grad[n, x] = (keep[n, x] + received[n, x]) * scale
        swept[n, 0] = sweep(grad[n, 0], None, grad[n, 1], w)
        swept[n, 1] = sweep(grad[n, last], grad[n, last - 1], None, w)
        for to, x, side in ((up, last, 1), (down, 0, 0)):
            to[2 * n * own : (2 * n + 1) * own, :] = grad[n, x, mine, :]
            to[(2 * n + 1) * own : (2 * n + 2) * own, :] = swept[n, side, mine, :]
            to[6 * own + n : 6 * own + n + 1, :] = grad[n, x, edge, :]
    hand_out(by_pair, by_next, up, down)


def inner_kernel(grad, swept, weights, full, half):
    width = grad.shape[1]
    last = width - 1
    w = [weights[k] for k in range(3)]
    for n in range(3):
        full[n, 0] = swept[n, 0]
        full[n, last] = swept[n, 1]
        for x in range(1, last):
            full[n, x] = sweep(grad[n, x], grad[n, x - 1], grad[n, x + 1], w)
        for x in range(1, last):
            half[n, x - 1] = sweep(
                full[n, x],
                full[n, x - 1] if x > 1 else None,
                full[n, x + 1] if x < last - 1 else None,
                w,
            )


def smooth_kernel(by_next, by_pair, grad, full, half, weights, out, low, high, beside, result):
    width, count, size_z = grad.shape[1:]
    own = count - BY
    last = width - 1
    me = lax.axis_index("shot")
    first = pl.multiple_of(me * BY, BY)
    mine = pl.ds(first, own)
    edge = pl.ds(edge_row(me, own), 1)
    take_in(by_pair, by_next, low, high)
    beside[...] = jnp.zeros(beside.shape, jnp.float32)
    for side, got in enumerate((low, high)):
        for n in range(3):
            beside[side, n, mine, :] = got[2 * n * own : (2 * n + 1) * own, :]
            beside[side, n, edge, :] = got[6 * own + n : 6 * own + n + 1, :]
            beside[side, 3 + n, mine, :] = got[(2 * n + 1) * own : (2 * n + 2) * own, :]
        for j in range(own // BY):
            row = got[6 * own + 3 + j : 6 * own + 4 + j, :]
            to = pl.ds(pl.multiple_of(first + j * BY, BY), BY)
            beside[side, 6, to, :] = jnp.broadcast_to(row, (BY, size_z))
    w = [weights[k] for k in range(3)]
    for n in range(3):
        ends = [full[n, x] + w[0] * beside[side, n] for side, x in ((0, 0), (1, last))]
        outer = [
            beside[side, 3 + n] + beside[side, 6] * grad[n, x] for side, x in ((0, 0), (1, last))
        ]
        result[0] = sweep(ends[0], outer[0], full[n, 1], w)
        result[last] = sweep(ends[1], full[n, last - 1], outer[1], w)
        for x in range(1, last):
            value = half[n, x - 1]
            if x == 1:
                value = value + w[0] * ends[0]
            if x == last - 1:
                value = value + w[0] * ends[1]
            result[x] = value
        for x in range(width):
            out[n, x] = result[x, mine, :]


def extended(block, sides, width):
    for axis, dim in sides:
        count = lax.axis_size(axis)
        forward = [(i, i + 1) for i in range(count - 1)]
        backward = [(target, source) for source, target in forward]
        low = lax.ppermute(
            lax.slice_in_dim(block, block.shape[dim] - width, None, axis=dim), axis, forward
        )
        high = lax.ppermute(lax.slice_in_dim(block, 0, width, axis=dim), axis, backward)
        block = jnp.concatenate([low, block, high], axis=dim)
    return block


def smooth_anywhere(image, orientation):
    groups = lax.axis_size("shot")
    owned = image.shape[2] // groups
    total = lax.psum(image, "shot")
    grad = lax.dynamic_slice_in_dim(total, lax.axis_index("shot") * owned, owned, 2)
    grad = grad * (STEPS * groups) ** (-0.5)
    weights = []
    for column in range(3):
        table = jnp.zeros(orientation.shape, jnp.float32)
        for klass in range(4):
            table = table + (orientation == klass).astype(jnp.float32) * weight_table[klass][column]
        table = jnp.repeat(jnp.repeat(table, image.shape[1], 0), BY, 1)
        weights.append(jnp.repeat(table, BZ, 2))
    for _ in range(SWEEPS):
        padded = extended(grad, (("shot", 2), ("tile", 1)), 1)
        padded = jnp.pad(padded, ((0, 0), (0, 0), (0, 0), (1, 1)))
        center = padded[:, 1:-1, 1:-1, 1:-1]
        lap_x = padded[:, 2:, 1:-1, 1:-1] + padded[:, :-2, 1:-1, 1:-1] - 2.0 * center
        lap_y = padded[:, 1:-1, 2:, 1:-1] + padded[:, 1:-1, :-2, 1:-1] - 2.0 * center
        lap_z = padded[:, 1:-1, 1:-1, 2:] + padded[:, 1:-1, 1:-1, :-2] - 2.0 * center
        grad = grad + smooth_rate * (weights[0] * lap_x + weights[1] * lap_y + weights[2] * lap_z)
    return grad


def both_ways(by_pair, by_next):
    count = lax.axis_size("tile")
    out = []
    for array, start in ((by_pair, 0), (by_next, 1)):
        pairs = [(i, i + 1) for i in range(start, count - 1, 2)]
        out.append(lax.ppermute(array, "tile", pairs + [(b, a) for a, b in pairs]))
    return out


def f32(*shape):
    return jax.ShapeDtypeStruct(shape, jnp.float32)


def in_hbm(array):
    return pltpu.with_memory_space_constraint(array, pltpu.HBM)


def call(kernel, outs, args, scratch, scalars=(), space=VMEM, flops=0):
    return pl.pallas_call(
        kernel,
        out_shape=outs,
        in_specs=[SMEM if n in scalars else space for n in range(len(args))],
        out_specs=jax.tree.map(lambda _: VMEM, outs),
        scratch_shapes=[
            pltpu.VMEM(shape, jnp.float32) if isinstance(shape, tuple) else shape
            for shape in scratch
        ],
        compiler_params=pltpu.CompilerParams(vmem_limit_bytes=24 * 1024 * 1024),
    )(*args)


def local(
    adjoint_state,
    adjoint_source,
    forward_field,
    lame_first,
    shear_modulus,
    buoyancy,
    active_blocks,
    orientation,
):
    width, size_y, size_z = lame_first.shape
    plane = (size_y, size_z)
    groups = lax.axis_size("shot")
    state, source, forward = adjoint_state[0], adjoint_source[0], forward_field[0]
    active = jnp.swapaxes(active_blocks, 1, 2)
    grid = f32(9, width, *plane)
    count = size_y // 2 if groups == 2 else size_y
    early = (3 * size_y + 4 * count, size_z)
    by_pair, by_next, raw, source, coef, cells, tile = call(
        functools.partial(early_kernel, groups),
        (
            f32(*early),
            f32(*early),
            grid,
            jax.ShapeDtypeStruct(source.shape, source.dtype),
            f32(3, width, *plane),
            f32(*plane),
            f32(BY, size_z),
        ),
        [
            in_hbm(a)
            for a in (active, orientation, state, source, lame_first, shear_modulus, buoyancy)
        ],
        [early, early, (3, width, *plane), pltpu.SemaphoreType.DMA((13,))],
        (0, 1),
        HBM,
    )
    by_pair, by_next = both_ways(by_pair, by_next)
    late_pair, late_next, st, push = call(
        late_kernel,
        (f32(6, *plane), f32(6, *plane), grid, f32(STEPS, width, *plane)),
        (raw, source, coef, cells),
        [(3, 3, *plane), (6, *plane), (6, *plane), (6, *plane)],
    )
    late_pair, late_next = both_ways(late_pair, late_next)
    args, outs, scalars = [by_pair, by_next], [], ()
    scratch = [early, early, (3, *plane), (3, 6, *plane), (3, 3, *plane)]
    owned = size_y // groups
    held = owned + BY
    if groups == 2:
        swapped = jnp.concatenate([by_pair[3 * size_y :], by_next[3 * size_y :], tile])
        swapped = lax.ppermute(swapped, "shot", [(0, 1), (1, 0)])
        args += [swapped, orientation]
        outs = [f32(3, held, size_z)]
        scratch += [(held, size_z)]
        scalars = (3,)
    end, w, third, outer, parts, *weights = call(
        functools.partial(near_kernel, groups),
        [f32(2, 9, *plane), grid, f32(3, width, *plane), f32(7, *plane), f32(4, 3, *plane), *outs],
        [*args, raw, st, coef, cells, push],
        scratch,
        scalars,
    )
    block = (3, width, held, size_z)
    images = [f32(*block), f32(*block)] if groups == 2 else [f32(3, width, *plane)]
    final, *images = call(
        functools.partial(far_kernel, groups),
        [grid, *images],
        [late_pair, late_next, st, end, w, third, outer, parts, coef, push, forward],
        [(6, *plane), (6, *plane), (2, 9, *plane), (3, *plane), (3, *plane), (3, width, *plane)],
    )
    if groups != 2:
        return final[None], smooth_anywhere(images[0], orientation)
    give, keep = images
    (weights,) = weights
    received = lax.ppermute(give, "shot", [(0, 1), (1, 0)])
    message = (6 * owned + BY, size_z)
    by_pair, by_next, grad, swept = call(
        functools.partial(sum_kernel, (STEPS * groups) ** (-0.5)),
        [f32(*message), f32(*message), f32(*block), f32(3, 2, held, size_z)],
        (keep, received, weights),
        [message, message],
    )
    by_pair, by_next = both_ways(by_pair, by_next)
    full, half = call(
        inner_kernel,
        [f32(*block), f32(3, width - 2, held, size_z)],
        (grad, swept, weights),
        [],
    )
    gradient = call(
        smooth_kernel,
        f32(3, width, owned, size_z),
        (by_next, by_pair, grad, full, half, weights),
        [message, message, (2, 7, held, size_z), (width, held, size_z)],
    )
    return final[None], gradient


def solution(mesh):
    return jax.shard_map(
        local,
        mesh=mesh,
        in_specs=(
            P("shot", None, "tile", None, None),
            P("shot", None, "tile", None, None),
            P("shot", None, "tile", None, None),
            P("tile", None, None),
            P("tile", None, None),
            P("tile", None, None),
            P("tile", None, None),
            P("tile", "shot", None),
        ),
        out_specs=(P("shot", None, "tile", None, None), P(None, "tile", "shot", None)),
        check_vma=False,
    )
```

```python
import functools

import jax
import jax.numpy as jnp
from jax import lax
from jax.experimental import pallas as pl
from jax.experimental.pallas import tpu as pltpu
from jax.sharding import PartitionSpec as P

BY = 8
BZ = 32
STEPS = 3
SWEEPS = 2

time_step = 0.25
smooth_rate = 0.1
weight_table = ((1.0, 1.0, 0.25), (0.25, 1.0, 1.0), (1.0, 0.25, 1.0), (0.6, 0.6, 0.6))

VX, VY, VZ, XX, YY, ZZ, XY, XZ, YZ = range(9)
VEL = (VX, VY, VZ)
SIDE = (XX, XY, XZ)
STRESS = (XX, YY, ZZ, XY, XZ, YZ)
ROWS = 32
VMEM = pl.BlockSpec(memory_space=pltpu.VMEM)
SMEM = pl.BlockSpec(memory_space=pltpu.SMEM)
HBM = pl.BlockSpec(memory_space=pltpu.HBM)


def lanes(shape):
    return lax.broadcasted_iota(jnp.int32, shape, len(shape) - 1)


def rows(shape):
    return lax.broadcasted_iota(jnp.int32, shape, len(shape) - 2)


def z_prev(f):
    return jnp.where(lanes(f.shape) == 0, 0.0, pltpu.roll(f, 1, f.ndim - 1))


def z_next(f):
    size = f.shape[-1]
    return jnp.where(lanes(f.shape) == size - 1, 0.0, pltpu.roll(f, size - 1, f.ndim - 1))


class Plane:
    def __init__(self, ref, *index):
        self.ref, self.index = ref, index
        self.size = ref.shape[len(index)]

    def at(self, row, count):
        return self.ref[self.index + (slice(row, row + count),)]

    def prev(self, row, count):
        if row:
            return self.at(row - 1, count)
        edge = pltpu.roll(self.at(0, 8), 1, 0)
        edge = jnp.where(rows(edge.shape) == 0, 0.0, edge)
        return jnp.concatenate([edge, self.at(7, count - 8)], 0)

    def next(self, row, count):
        if row + count < self.size:
            return self.at(row + 1, count)
        edge = pltpu.roll(self.at(self.size - 8, 8), 7, 0)
        edge = jnp.where(rows(edge.shape) == 7, 0.0, edge)
        return jnp.concatenate([self.at(row + 1, count - 8), edge], 0)

    def set(self, row, value):
        self.ref[self.index + (slice(row, row + value.shape[0]),)] = value


def planes(ref, comps, *index):
    return {c: Plane(ref, n, *index) for n, c in enumerate(comps)}


def divergence(s, before, row, count, have=(XX, YY, ZZ, XY, XZ, YZ)):
    def along_x(c):
        here = s[c].at(row, count)
        return here - before[c].at(row, count) if before is not None else here

    def along_y(c):
        return s[c].at(row, count) - s[c].prev(row, count)

    def along_z(c):
        here = s[c].at(row, count)
        return here - z_prev(here)

    out = []
    for c_x, c_y, c_z in ((XX, XY, XZ), (XY, YY, YZ), (XZ, YZ, ZZ)):
        terms = along_x(c_x)
        if c_y in have:
            terms = terms + along_y(c_y)
        if c_z in have:
            terms = terms + along_z(c_z)
        out.append(terms)
    return out


def strain(v, after, row, count, want=(XX, YY, ZZ, XY, XZ, YZ)):
    x, y, z = (v[c].at(row, count) for c in (VX, VY, VZ))
    if after is None:
        d_x = [-x, -y, -z]
    else:
        d_x = [after[c].at(row, count) - f for c, f in ((VX, x), (VY, y), (VZ, z))]
    out = {XX: d_x[0], YY: v[VY].next(row, count) - y, ZZ: z_next(z) - z}
    out["div"] = out[XX] + out[YY] + out[ZZ]
    if XY in want:
        out[XY] = v[VX].next(row, count) - x + d_x[1]
    if XZ in want:
        out[XZ] = z_next(x) - x + d_x[2]
    if YZ in want:
        out[YZ] = z_next(y) - y + (v[VZ].next(row, count) - z)
    return out


def stress_rate(e, lame, shear, want=(XX, YY, ZZ, XY, XZ, YZ)):
    spread = lame * e["div"]
    return {
        c: spread + 2.0 * shear * e[c] if c in (XX, YY, ZZ) else shear * e[c] for c in want
    }


def cell_plane(active, out):
    shape = (BY, out.shape[1])
    for j in range(out.shape[0] // BY):
        row = jnp.full(shape, active[0, 0, j].astype(jnp.float32))
        for k in range(1, out.shape[1] // BZ):
            row = jnp.where(lanes(shape) >= k * BZ, active[0, k, j].astype(jnp.float32), row)
        out[j * BY : (j + 1) * BY, :] = row


def chunks(size):
    return range(0, size, ROWS)


def is_even():
    return lax.rem(lax.axis_index("tile"), 2) == 0


def hand_out(by_pair, by_next, up, down):
    even = is_even()

    @pl.when(even)
    def _():
        by_pair[...] = up[...]
        by_next[...] = down[...]

    @pl.when(jnp.logical_not(even))
    def _():
        by_pair[...] = down[...]
        by_next[...] = up[...]


def take_in(by_pair, by_next, low, high):
    even = is_even()

    @pl.when(even)
    def _():
        low[...] = by_next[...]
        high[...] = by_pair[...]

    @pl.when(jnp.logical_not(even))
    def _():
        low[...] = by_pair[...]
        high[...] = by_next[...]


def class_tile(orientation, j, size_z):
    shape = (BY, size_z)
    out = jnp.full(shape, orientation[0, j, 0].astype(jnp.float32))
    for k in range(1, size_z // BZ):
        out = jnp.where(lanes(shape) >= k * BZ, orientation[0, j, k].astype(jnp.float32), out)
    return out


def here(row):
    return slice(row, row + ROWS)


def early_kernel(
    groups,
    active_hbm,
    orientation_hbm,
    state_hbm,
    source_hbm,
    lame_hbm,
    shear_hbm,
    buoyancy_hbm,
    by_pair,
    by_next,
    cells,
    tile,
    up,
    down,
    first,
    push,
    params,
    active,
    orientation,
    sems,
):
    size_y, size_z = cells.shape
    last = state_hbm.shape[1] - 1
    planes_at = (0, 0, 0, 1, last, last, last)
    arrays = (buoyancy_hbm, lame_hbm, shear_hbm)
    ends = [(active_hbm, active), (orientation_hbm, orientation)]
    ends += [(arrays[n % 3].at[x], params.at[n]) for n, x in enumerate(planes_at)]
    ends += [(state_hbm.at[:, 0], first), (source_hbm.at[0, 0], push)]
    ends += [
        (state_hbm.at[c, last], up.at[n * size_y : (n + 1) * size_y]) for n, c in enumerate(SIDE)
    ]
    copies = [pltpu.make_async_copy(*pair, sems.at[n]) for n, pair in enumerate(ends)]
    for copy in copies:
        copy.start()
    for copy in copies[:2]:
        copy.wait()
    cell_plane(active, cells)
    me = lax.axis_index("shot") if groups == 2 else 0
    last_block = orientation.shape[1] - 1
    tile[...] = class_tile(orientation, jnp.where(me == 0, last_block, 0), size_z)
    for copy in copies[2:9]:
        copy.wait()
    for row in chunks(size_y):
        c = time_step * cells[here(row), :]
        for n in range(7):
            params[n, here(row)] = c * params[n, here(row)]
    count = (up.shape[0] - 3 * size_y) // 4
    mine = pl.ds(pl.multiple_of(me * count, 8), count) if groups == 2 else slice(0, count)
    for n in range(4):
        to = slice(3 * size_y + n * count, 3 * size_y + (n + 1) * count)
        down[to] = params[n, mine]
        up[to] = params[(6, 4, 5, 6)[n], mine]
    for copy in copies[9:]:
        copy.wait()
    raw = {c: Plane(first, c) for c in range(9)}
    for row in chunks(size_y):
        c, cb = cells[here(row), :], params[0, here(row)]
        for n, term in enumerate(divergence(raw, None, row, ROWS)):
            value = c * raw[n].at(row, ROWS) + cb * term
            if n == VZ:
                value = value + time_step * c * push[here(row)].astype(jnp.float32)
            down[n * size_y + row : n * size_y + row + ROWS] = value
    hand_out(by_pair, by_next, up, down)


def late_kernel(
    state, source, buoyancy, lame, shear, cells, by_pair, by_next, st, push, coef, v2, s2, up, down
):
    width, size_y = state.shape[1], state.shape[2]
    last = width - 1
    for row in chunks(size_y):
        c = time_step * cells[here(row), :]
        for step in range(STEPS):
            for x in range(width):
                push[step, x, here(row)] = c * source[step, x, here(row)].astype(jnp.float32)
        for n, param in enumerate((buoyancy, lame, shear)):
            for x in range(width):
                coef[n, x, here(row)] = c * param[x, here(row)]

    def coefs(x, row):
        return [coef[n, x, here(row)] for n in range(3)]

    raw = [{c: Plane(state, c, x) for c in range(9)} for x in range(width)]
    one = [{c: Plane(st, c, x) for c in range(9)} for x in range(width)]
    two = {x: {c: Plane(v2, n, c) for c in VEL} for n, x in enumerate((0, 1, last))}
    for x in range(width):
        for row in chunks(size_y):
            c = cells[here(row), :]
            cb = coefs(x, row)[0]
            terms = divergence(raw[x], raw[x - 1] if x else None, row, ROWS)
            for comp, term in zip(VEL, terms):
                value = c * raw[x][comp].at(row, ROWS) + cb * term
                if comp == VZ:
                    value = value + push[0, x, here(row)]
                one[x][comp].set(row, value)
    for x in range(width):
        for row in chunks(size_y):
            c = cells[here(row), :]
            _, cl, cm = coefs(x, row)
            rate = stress_rate(strain(one[x], one[x + 1] if x < last else None, row, ROWS), cl, cm)
            for comp, term in rate.items():
                one[x][comp].set(row, c * raw[x][comp].at(row, ROWS) + term)
    for x in two:
        for row in chunks(size_y):
            cb = coefs(x, row)[0]
            terms = divergence(one[x], one[x - 1] if x else None, row, ROWS)
            for comp, term in zip(VEL, terms):
                value = one[x][comp].at(row, ROWS) + cb * term
                if comp == VZ:
                    value = value + push[1, x, here(row)]
                two[x][comp].set(row, value)
    stress = {c: Plane(s2, c - XX) for c in STRESS}
    for row in chunks(size_y):
        _, cl, cm = coefs(0, row)
        rate = stress_rate(strain(two[0], two[1], row, ROWS), cl, cm)
        for comp, term in rate.items():
            stress[comp].set(row, one[0][comp].at(row, ROWS) + term)
        _, cl, cm = coefs(last, row)
        rate = stress_rate(strain(two[last], None, row, ROWS, SIDE), cl, cm, SIDE)
        for n, comp in enumerate(SIDE):
            value = one[last][comp].at(row, ROWS)
            up[n, here(row)] = value
            up[3 + n, here(row)] = value + rate[comp]
    for row in chunks(size_y):
        cb = coefs(0, row)[0]
        terms = divergence(stress, None, row, ROWS)
        for comp, term in zip(VEL, terms):
            before = two[0][comp].at(row, ROWS)
            value = before + cb * term
            if comp == VZ:
                value = value + push[2, 0, here(row)]
            down[comp, here(row)] = before
            down[3 + comp, here(row)] = value
    hand_out(by_pair, by_next, up, down)


def beyond(v, cl, cm):
    spread = cl * v[0]
    return {XX: spread + 2.0 * cm * v[0], YY: spread, ZZ: spread, XY: cm * v[1], XZ: cm * v[2]}


def own_planes(st, end):
    width = st.shape[1]
    one = [{c: Plane(st, c, x) for c in range(9)} for x in range(width)]
    one[0] = {c: Plane(end, 0, c) for c in range(9)}
    one[-1] = {c: Plane(st, c, width - 1) if c in VEL else Plane(end, 1, c) for c in range(9)}
    return one


def near_kernel(groups, *refs):
    by_pair, by_next, *refs = refs
    if groups == 2:
        swapped, orientation, *refs = refs
    state, st, coef, cells, push, end, w, third, outer, parts, *refs = refs
    if groups == 2:
        weights, *refs = refs
    low, high, high_v, d_s, d_v, *classes = refs
    width, size_y = st.shape[1], st.shape[2]
    last = width - 1
    take_in(by_pair, by_next, low, high)
    count = (low.shape[0] - 3 * size_y) // 4
    base = 3 * size_y
    if groups == 2:
        me = lax.axis_index("shot")
        mine = pl.ds(pl.multiple_of(me * count, 8), count)
        theirs = pl.ds(pl.multiple_of((1 - me) * count, 8), count)
        low_at = pl.multiple_of(jnp.where(is_even(), 4 * count, 0), 8)
        high_at = pl.multiple_of(jnp.where(is_even(), 0, 4 * count), 8)
        for n in range(4):
            if n < 3:
                outer[n, mine] = low[base + n * count : base + (n + 1) * count]
                outer[n, theirs] = swapped[pl.ds(low_at + n * count, count)]
            outer[3 + n, mine] = high[base + n * count : base + (n + 1) * count]
            outer[3 + n, theirs] = swapped[pl.ds(high_at + n * count, count)]
    else:
        for n in range(4):
            if n < 3:
                outer[n] = low[base + n * count : base + (n + 1) * count]
            outer[3 + n] = high[base + n * count : base + (n + 1) * count]

    def coefs(x, row):
        if x < 0:
            return [outer[n, here(row)] for n in range(3)]
        if x > last:
            return [outer[3 + n, here(row)] for n in range(3)]
        return [coef[n, x, here(row)] for n in range(3)]

    raw = [{c: Plane(state, c, x) for c in range(9)} for x in range(width)]
    old = [{c: Plane(st, c, x) for c in range(9)} for x in range(width)]
    one = own_planes(st, end)
    two = [{c: Plane(w, c, x) for c in range(9)} for x in range(width)]
    high_one = {c: Plane(high_v, c) for c in VEL}
    d_low_s, d_high_s, d_high_s_two = ({c: Plane(d_s, k, c - XX) for c in STRESS} for k in range(3))
    d_high_v, d_far_v, d_low_v = ({c: Plane(d_v, k, c) for c in VEL} for k in range(3))
    part_v, part_low, d_high_v_two, part_high = (
        {c: Plane(parts, k, n) for n, c in enumerate(names)}
        for k, names in enumerate((VEL, SIDE, VEL, VEL))
    )

    for row in chunks(size_y):
        cb, cb_high = coefs(0, row)[0], coefs(last + 1, row)[0]
        for n, (comp, c) in enumerate(zip(VEL, SIDE)):
            at = slice(n * size_y + row, n * size_y + row + ROWS)
            one[0][comp].set(row, old[0][comp].at(row, ROWS) - cb * low[at])
            delta = -cb_high * raw[last][c].at(row, ROWS)
            d_high_v[comp].set(row, delta)
            high_one[comp].set(row, high[at] + delta)
    for row in chunks(size_y):
        c = cells[here(row), :]
        _, cl, cm = coefs(0, row)
        for comp, term in stress_rate(strain(one[0], one[1], row, ROWS), cl, cm).items():
            one[0][comp].set(row, c * raw[0][comp].at(row, ROWS) + term)
        _, cl, cm = coefs(last, row)
        terms = beyond([high_one[comp].at(row, ROWS) for comp in VEL], cl, cm)
        for comp in STRESS:
            value = old[last][comp].at(row, ROWS)
            one[last][comp].set(row, value + terms[comp] if comp in terms else value)
        _, cl, cm = coefs(-1, row)
        for comp, term in beyond([one[0][comp].at(row, ROWS) for comp in VEL], cl, cm).items():
            d_low_s[comp].set(row, term)
        _, cl, cm = coefs(last + 1, row)
        for comp, term in stress_rate(strain(d_high_v, None, row, ROWS), cl, cm).items():
            d_high_s[comp].set(row, term)

    for row in chunks(size_y):
        for x in range(width):
            cb = coefs(x, row)[0]
            terms = divergence(one[x], one[x - 1] if x else d_low_s, row, ROWS)
            for comp, term in zip(VEL, terms):
                value = one[x][comp].at(row, ROWS) + cb * term
                if comp == VZ:
                    value = value + push[1, x, here(row)]
                (two[x] if x else part_v)[comp].set(row, value)
        cb = coefs(last + 1, row)[0]
        for comp, term in zip(VEL, divergence(d_high_s, one[last], row, ROWS)):
            d_high_v_two[comp].set(row, d_high_v[comp].at(row, ROWS) + cb * term)
        cb = outer[6, here(row)]
        for comp, c in zip(VEL, SIDE):
            d_far_v[comp].set(row, -cb * d_high_s[c].at(row, ROWS))
        cb = coefs(-1, row)[0]
        terms = divergence(d_low_s, None, row, ROWS, (XX, YY, ZZ, XY, XZ))
        for comp, term in zip(VEL, terms):
            d_low_v[comp].set(row, cb * term)
    for row in chunks(size_y):
        for x in range(1, width):
            _, cl, cm = coefs(x, row)
            after = two[x + 1] if x < last else None
            for comp, term in stress_rate(strain(two[x], after, row, ROWS), cl, cm).items():
                two[x][comp].set(row, one[x][comp].at(row, ROWS) + term)
        _, cl, cm = coefs(-1, row)
        rate = stress_rate(strain(d_low_v, None, row, ROWS, SIDE), cl, cm, SIDE)
        for comp, term in rate.items():
            part_low[comp].set(row, d_low_s[comp].at(row, ROWS) + term)
        _, cl, cm = coefs(last + 1, row)
        for comp, term in stress_rate(strain(d_high_v_two, d_far_v, row, ROWS), cl, cm).items():
            d_high_s_two[comp].set(row, d_high_s[comp].at(row, ROWS) + term)
    for row in chunks(size_y):
        cb = coefs(last + 1, row)[0]
        for comp, term in zip(VEL, divergence(d_high_s_two, None, row, ROWS)):
            part_high[comp].set(row, d_high_v_two[comp].at(row, ROWS) + cb * term)
        for x in range(2, last):
            cb = coefs(x, row)[0]
            for comp, term in zip(VEL, divergence(two[x], two[x - 1], row, ROWS)):
                value = two[x][comp].at(row, ROWS) + cb * term
                if comp == VZ:
                    value = value + push[2, x, here(row)]
                third[comp, x, here(row)] = value
    if groups != 2:
        return

    (classes,) = classes
    rows_held = weights.shape[1]
    own = rows_held - BY
    first = pl.multiple_of(me * BY, BY)
    for j in range(own // BY):
        classes[pl.ds(first + j * BY, BY), :] = class_tile(orientation, j, weights.shape[2])
    classes[pl.ds(pl.multiple_of((1 - me) * own, BY), BY), :] = swapped[8 * count :, :]
    klass = classes[...]
    for column in range(3):
        table = jnp.full(klass.shape, weight_table[3][column], jnp.float32)
        for k in range(3):
            table = jnp.where(klass == k, weight_table[k][column], table)
        weights[column] = smooth_rate * table


def far_kernel(groups, *refs):
    by_pair, by_next, st, end, w, third, outer, parts, coef, push, forward, final, *refs = refs
    *images, low, high, edge, low_s, high_v, image = refs
    width, size_y = st.shape[1], st.shape[2]
    last = width - 1
    take_in(by_pair, by_next, low, high)

    def coefs(x, row):
        if x < 0:
            return [outer[n, here(row)] for n in range(3)]
        if x > last:
            return [outer[3 + n, here(row)] for n in range(3)]
        return [coef[n, x, here(row)] for n in range(3)]

    one = own_planes(st, end)
    part = [{c: Plane(w, c, x) for c in range(9)} for x in range(width)]
    two = [dict(p) for p in part]
    for c in range(9):
        two[0][c] = Plane(edge, 0, c)
        if c >= XX:
            two[last][c] = Plane(edge, 1, c)
    three = [{c: Plane(final, c, x) for c in range(9)} for x in range(width)]
    part_v, part_low, d_high_v_two, part_high = (
        {c: Plane(parts, k, n) for n, c in enumerate(names)}
        for k, names in enumerate((VEL, SIDE, VEL, VEL))
    )
    low_two = {c: Plane(low_s, n) for n, c in enumerate(SIDE)}
    high_three = {c: Plane(high_v, c) for c in VEL}

    for row in chunks(size_y):
        cb = coefs(0, row)[0]
        moved = []
        for n, comp in enumerate(VEL):
            moved.append(part_v[comp].at(row, ROWS) - cb * low[n, here(row)])
            two[0][comp].set(row, moved[n])
        _, cl, cm = coefs(-1, row)
        terms = beyond(moved, cl, cm)
        for n, comp in enumerate(SIDE):
            value = low[3 + n, here(row)] + part_low[comp].at(row, ROWS)
            low_two[comp].set(row, value + terms[comp])
        _, cl, cm = coefs(last, row)
        cb = coefs(last + 1, row)[0]
        moved = [high[n, here(row)] + d_high_v_two[n].at(row, ROWS) for n in VEL]
        terms = beyond(moved, cl, cm)
        values = {}
        for comp in STRESS:
            value = part[last][comp].at(row, ROWS)
            values[comp] = value + terms[comp] if comp in terms else value
            two[last][comp].set(row, values[comp])
        for n, comp in enumerate(SIDE):
            value = high[3 + n, here(row)] + part_high[n].at(row, ROWS)
            high_three[n].set(row, value - cb * values[comp])
    for row in chunks(size_y):
        _, cl, cm = coefs(0, row)
        for comp, term in stress_rate(strain(two[0], two[1], row, ROWS), cl, cm).items():
            two[0][comp].set(row, one[0][comp].at(row, ROWS) + term)

    for row in chunks(size_y):
        for x in range(width):
            if 2 <= x < last:
                for comp in VEL:
                    three[x][comp].set(row, third[comp, x, here(row)])
                continue
            cb = coefs(x, row)[0]
            terms = divergence(two[x], two[x - 1] if x else low_two, row, ROWS)
            for comp, term in zip(VEL, terms):
                value = two[x][comp].at(row, ROWS) + cb * term
                if comp == VZ:
                    value = value + push[2, x, here(row)]
                three[x][comp].set(row, value)
    for row in chunks(size_y):
        for x in range(width):
            _, cl, cm = coefs(x, row)
            after = three[x + 1] if x < last else high_three
            rate = stress_rate(strain(three[x], after, row, ROWS), cl, cm)
            sums = {}
            for comp in STRESS:
                before = two[x][comp].at(row, ROWS)
                value = before + rate[comp]
                three[x][comp].set(row, value)
                sums[comp] = one[x][comp].at(row, ROWS) + before + value
            f = [forward[n, x, here(row)].astype(jnp.float32) for n in range(9)]
            image[0, x, here(row)] = (sums[XX] + sums[YY] + sums[ZZ]) * (f[0] + f[1] + f[2])
            total = sums[XX] * f[0]
            for n, comp in enumerate(STRESS[1:]):
                total = total + sums[comp] * f[n + 1]
            image[1, x, here(row)] = total
            total = 0.0
            for comp in VEL:
                moved = [k[x][comp].at(row, ROWS) for k in (one, two, three)]
                total = total + (moved[0] + moved[1] + moved[2]) * f[6 + comp]
            image[2, x, here(row)] = total

    if groups != 2:
        images[0][...] = image[...]
        return
    give, keep = images
    me = lax.axis_index("shot")
    count = keep.shape[2]
    mine = pl.ds(pl.multiple_of(me * (size_y - count), 8), count)
    theirs = pl.ds(pl.multiple_of((1 - me) * (size_y - count), 8), count)
    for n in range(3):
        for x in range(width):
            give[n, x] = image[n, x, theirs, :]
            keep[n, x] = image[n, x, mine, :]


def y_prev(f):
    return jnp.where(rows(f.shape) == 0, 0.0, pltpu.roll(f, 1, f.ndim - 2))


def y_next(f):
    size = f.shape[-2]
    return jnp.where(rows(f.shape) == size - 1, 0.0, pltpu.roll(f, size - 1, f.ndim - 2))


def sweep(g, before, after, weights):
    w_x, w_y, w_z = weights
    twice = 2.0 * g
    along_x = -twice
    for plane in (before, after):
        if plane is not None:
            along_x = along_x + plane
    along_y = y_next(g) + y_prev(g) - twice
    along_z = z_next(g) + z_prev(g) - twice
    return g + (w_x * along_x + w_y * along_y + w_z * along_z)


def edge_row(me, own):
    return jnp.where(me == 0, own, BY - 1)


def sum_kernel(scale, keep, received, weights, by_pair, by_next, grad, swept, up, down):
    width, count, size_z = grad.shape[1:]
    own = count - BY
    me = lax.axis_index("shot")
    first = pl.multiple_of(me * BY, BY)
    mine = pl.ds(first, own)
    edge = pl.ds(edge_row(me, own), 1)
    last = width - 1
    w = [weights[k] for k in range(3)]
    for to in (up, down):
        to[6 * own :, :] = jnp.zeros((BY, size_z), jnp.float32)
        for j in range(own // BY):
            row = weights[0, pl.ds(pl.multiple_of(first + j * BY, BY), BY), :][0:1]
            to[6 * own + 3 + j : 6 * own + 4 + j, :] = row
    for n in range(3):
        for x in range(width):
            grad[n, x] = (keep[n, x] + received[n, x]) * scale
        swept[n, 0] = sweep(grad[n, 0], None, grad[n, 1], w)
        swept[n, 1] = sweep(grad[n, last], grad[n, last - 1], None, w)
        for to, x, side in ((up, last, 1), (down, 0, 0)):
            to[2 * n * own : (2 * n + 1) * own, :] = grad[n, x, mine, :]
            to[(2 * n + 1) * own : (2 * n + 2) * own, :] = swept[n, side, mine, :]
            to[6 * own + n : 6 * own + n + 1, :] = grad[n, x, edge, :]
    hand_out(by_pair, by_next, up, down)


def inner_kernel(grad, swept, weights, full, half):
    width = grad.shape[1]
    last = width - 1
    w = [weights[k] for k in range(3)]
    for n in range(3):
        full[n, 0] = swept[n, 0]
        full[n, last] = swept[n, 1]
        for x in range(1, last):
            full[n, x] = sweep(grad[n, x], grad[n, x - 1], grad[n, x + 1], w)
        for x in range(1, last):
            half[n, x - 1] = sweep(
                full[n, x],
                full[n, x - 1] if x > 1 else None,
                full[n, x + 1] if x < last - 1 else None,
                w,
            )


def smooth_kernel(by_pair, by_next, grad, full, half, weights, out, low, high, beside, result):
    width, count, size_z = grad.shape[1:]
    own = count - BY
    last = width - 1
    me = lax.axis_index("shot")
    first = pl.multiple_of(me * BY, BY)
    mine = pl.ds(first, own)
    edge = pl.ds(edge_row(me, own), 1)
    take_in(by_pair, by_next, low, high)
    beside[...] = jnp.zeros(beside.shape, jnp.float32)
    for side, got in enumerate((low, high)):
        for n in range(3):
            beside[side, n, mine, :] = got[2 * n * own : (2 * n + 1) * own, :]
            beside[side, n, edge, :] = got[6 * own + n : 6 * own + n + 1, :]
            beside[side, 3 + n, mine, :] = got[(2 * n + 1) * own : (2 * n + 2) * own, :]
        for j in range(own // BY):
            row = got[6 * own + 3 + j : 6 * own + 4 + j, :]
            to = pl.ds(pl.multiple_of(first + j * BY, BY), BY)
            beside[side, 6, to, :] = jnp.broadcast_to(row, (BY, size_z))
    w = [weights[k] for k in range(3)]
    for n in range(3):
        ends = [full[n, x] + w[0] * beside[side, n] for side, x in ((0, 0), (1, last))]
        outer = [
            beside[side, 3 + n] + beside[side, 6] * grad[n, x] for side, x in ((0, 0), (1, last))
        ]
        result[0] = sweep(ends[0], outer[0], full[n, 1], w)
        result[last] = sweep(ends[1], full[n, last - 1], outer[1], w)
        for x in range(1, last):
            value = half[n, x - 1]
            if x == 1:
                value = value + w[0] * ends[0]
            if x == last - 1:
                value = value + w[0] * ends[1]
            result[x] = value
        for x in range(width):
            out[n, x] = result[x, mine, :]


def extended(block, sides, width):
    for axis, dim in sides:
        count = lax.axis_size(axis)
        forward = [(i, i + 1) for i in range(count - 1)]
        backward = [(target, source) for source, target in forward]
        low = lax.ppermute(
            lax.slice_in_dim(block, block.shape[dim] - width, None, axis=dim), axis, forward
        )
        high = lax.ppermute(lax.slice_in_dim(block, 0, width, axis=dim), axis, backward)
        block = jnp.concatenate([low, block, high], axis=dim)
    return block


def smooth_anywhere(image, orientation):
    groups = lax.axis_size("shot")
    owned = image.shape[2] // groups
    total = lax.psum(image, "shot")
    grad = lax.dynamic_slice_in_dim(total, lax.axis_index("shot") * owned, owned, 2)
    grad = grad * (STEPS * groups) ** (-0.5)
    weights = []
    for column in range(3):
        table = jnp.zeros(orientation.shape, jnp.float32)
        for klass in range(4):
            table = table + (orientation == klass).astype(jnp.float32) * weight_table[klass][column]
        table = jnp.repeat(jnp.repeat(table, image.shape[1], 0), BY, 1)
        weights.append(jnp.repeat(table, BZ, 2))
    for _ in range(SWEEPS):
        padded = extended(grad, (("shot", 2), ("tile", 1)), 1)
        padded = jnp.pad(padded, ((0, 0), (0, 0), (0, 0), (1, 1)))
        center = padded[:, 1:-1, 1:-1, 1:-1]
        lap_x = padded[:, 2:, 1:-1, 1:-1] + padded[:, :-2, 1:-1, 1:-1] - 2.0 * center
        lap_y = padded[:, 1:-1, 2:, 1:-1] + padded[:, 1:-1, :-2, 1:-1] - 2.0 * center
        lap_z = padded[:, 1:-1, 1:-1, 2:] + padded[:, 1:-1, 1:-1, :-2] - 2.0 * center
        grad = grad + smooth_rate * (weights[0] * lap_x + weights[1] * lap_y + weights[2] * lap_z)
    return grad


def both_ways(by_pair, by_next):
    count = lax.axis_size("tile")
    out = []
    for array, start in ((by_pair, 0), (by_next, 1)):
        pairs = [(i, i + 1) for i in range(start, count - 1, 2)]
        out.append(lax.ppermute(array, "tile", pairs + [(b, a) for a, b in pairs]))
    return out


def f32(*shape):
    return jax.ShapeDtypeStruct(shape, jnp.float32)


def in_hbm(array):
    return pltpu.with_memory_space_constraint(array, pltpu.HBM)


def call(kernel, outs, args, scratch, scalars=(), space=VMEM):
    return pl.pallas_call(
        kernel,
        out_shape=outs,
        in_specs=[SMEM if n in scalars else space for n in range(len(args))],
        out_specs=jax.tree.map(lambda _: VMEM, outs),
        scratch_shapes=[
            pltpu.VMEM(shape, jnp.float32) if isinstance(shape, tuple) else shape
            for shape in scratch
        ],
        compiler_params=pltpu.CompilerParams(vmem_limit_bytes=24 * 1024 * 1024),
    )(*args)


def local(
    adjoint_state,
    adjoint_source,
    forward_field,
    lame_first,
    shear_modulus,
    buoyancy,
    active_blocks,
    orientation,
):
    width, size_y, size_z = lame_first.shape
    plane = (size_y, size_z)
    groups = lax.axis_size("shot")
    state, source, forward = adjoint_state[0], adjoint_source[0], forward_field[0]
    active = jnp.swapaxes(active_blocks, 1, 2)
    grid = f32(9, width, *plane)
    count = size_y // 2 if groups == 2 else size_y
    early = (3 * size_y + 4 * count, size_z)
    by_pair, by_next, cells, tile = call(
        functools.partial(early_kernel, groups),
        [f32(*early), f32(*early), f32(*plane), f32(BY, size_z)],
        [
            in_hbm(a)
            for a in (active, orientation, state, source, lame_first, shear_modulus, buoyancy)
        ],
        [
            early,
            early,
            (9, *plane),
            pltpu.VMEM(plane, source.dtype),
            (7, *plane),
            pltpu.SMEM(active.shape, jnp.int32),
            pltpu.SMEM(orientation.shape, jnp.int32),
            pltpu.SemaphoreType.DMA((14,)),
        ],
        space=HBM,
    )
    by_pair, by_next = both_ways(by_pair, by_next)
    late_pair, late_next, st, push, coef = call(
        late_kernel,
        [f32(6, *plane), f32(6, *plane), grid, f32(STEPS, width, *plane), f32(3, width, *plane)],
        (state, source, buoyancy, lame_first, shear_modulus, cells),
        [(3, 3, *plane), (6, *plane), (6, *plane), (6, *plane)],
    )
    late_pair, late_next = both_ways(late_pair, late_next)
    args, outs, scalars = [by_pair, by_next], [], ()
    scratch = [early, early, (3, *plane), (3, 6, *plane), (3, 3, *plane)]
    owned = size_y // groups
    held = owned + BY
    if groups == 2:
        swapped = jnp.concatenate([by_pair[3 * size_y :], by_next[3 * size_y :], tile])
        swapped = lax.ppermute(swapped, "shot", [(0, 1), (1, 0)])
        args += [swapped, orientation]
        outs = [f32(3, held, size_z)]
        scratch += [(held, size_z)]
        scalars = (3,)
    end, w, third, outer, parts, *weights = call(
        functools.partial(near_kernel, groups),
        [f32(2, 9, *plane), grid, f32(3, width, *plane), f32(7, *plane), f32(4, 3, *plane), *outs],
        [*args, state, st, coef, cells, push],
        scratch,
        scalars,
    )
    block = (3, width, held, size_z)
    images = [f32(*block), f32(*block)] if groups == 2 else [f32(3, width, *plane)]
    final, *images = call(
        functools.partial(far_kernel, groups),
        [pltpu.VMEM(grid.shape, grid.dtype), *images],
        [late_pair, late_next, st, end, w, third, outer, parts, coef, push, forward],
        [(6, *plane), (6, *plane), (2, 9, *plane), (3, *plane), (3, *plane), (3, width, *plane)],
    )
    if groups != 2:
        return final[None], smooth_anywhere(images[0], orientation)
    give, keep = images
    (weights,) = weights
    received = lax.ppermute(give, "shot", [(0, 1), (1, 0)])
    message = (6 * owned + BY, size_z)
    by_pair, by_next, grad, swept = call(
        functools.partial(sum_kernel, (STEPS * groups) ** (-0.5)),
        [f32(*message), f32(*message), f32(*block), f32(3, 2, held, size_z)],
        (keep, received, weights),
        [message, message],
    )
    by_pair, by_next = both_ways(by_pair, by_next)
    full, half = call(
        inner_kernel,
        [f32(*block), f32(3, width - 2, held, size_z)],
        (grad, swept, weights),
        [],
    )
    gradient = call(
        smooth_kernel,
        f32(3, width, owned, size_z),
        (by_pair, by_next, grad, full, half, weights),
        [message, message, (2, 7, held, size_z), (width, held, size_z)],
    )
    return final[None], gradient


def solution(mesh):
    return jax.shard_map(
        local,
        mesh=mesh,
        in_specs=(
            P("shot", None, "tile", None, None),
            P("shot", None, "tile", None, None),
            P("shot", None, "tile", None, None),
            P("tile", None, None),
            P("tile", None, None),
            P("tile", None, None),
            P("tile", None, None),
            P("tile", "shot", None),
        ),
        out_specs=(P("shot", None, "tile", None, None), P(None, "tile", "shot", None)),
        check_vma=False,
    )
```

```python
import functools

import jax
import jax.numpy as jnp
from jax import lax
from jax.experimental import pallas as pl
from jax.experimental.pallas import tpu as pltpu
from jax.sharding import PartitionSpec as P

BY = 8
BZ = 32
STEPS = 3
SWEEPS = 2

time_step = 0.25
smooth_rate = 0.1
weight_table = ((1.0, 1.0, 0.25), (0.25, 1.0, 1.0), (1.0, 0.25, 1.0), (0.6, 0.6, 0.6))

VX, VY, VZ, XX, YY, ZZ, XY, XZ, YZ = range(9)
VEL = (VX, VY, VZ)
SIDE = (XX, XY, XZ)
STRESS = (XX, YY, ZZ, XY, XZ, YZ)
ROWS = 32
VMEM = pl.BlockSpec(memory_space=pltpu.VMEM)
SMEM = pl.BlockSpec(memory_space=pltpu.SMEM)
HBM = pl.BlockSpec(memory_space=pltpu.HBM)


def lanes(shape):
    return lax.broadcasted_iota(jnp.int32, shape, len(shape) - 1)


def rows(shape):
    return lax.broadcasted_iota(jnp.int32, shape, len(shape) - 2)


def z_prev(f):
    return jnp.where(lanes(f.shape) == 0, 0.0, pltpu.roll(f, 1, f.ndim - 1))


def z_next(f):
    size = f.shape[-1]
    return jnp.where(lanes(f.shape) == size - 1, 0.0, pltpu.roll(f, size - 1, f.ndim - 1))


class Plane:
    def __init__(self, ref, *index):
        self.ref, self.index = ref, index
        self.size = ref.shape[len(index)]

    def at(self, row, count):
        return self.ref[self.index + (slice(row, row + count),)]

    def prev(self, row, count):
        if row:
            return self.at(row - 1, count)
        edge = pltpu.roll(self.at(0, 8), 1, 0)
        edge = jnp.where(rows(edge.shape) == 0, 0.0, edge)
        return jnp.concatenate([edge, self.at(7, count - 8)], 0)

    def next(self, row, count):
        if row + count < self.size:
            return self.at(row + 1, count)
        edge = pltpu.roll(self.at(self.size - 8, 8), 7, 0)
        edge = jnp.where(rows(edge.shape) == 7, 0.0, edge)
        return jnp.concatenate([self.at(row + 1, count - 8), edge], 0)

    def set(self, row, value):
        self.ref[self.index + (slice(row, row + value.shape[0]),)] = value


def planes(ref, comps, *index):
    return {c: Plane(ref, n, *index) for n, c in enumerate(comps)}


def divergence(s, before, row, count, have=(XX, YY, ZZ, XY, XZ, YZ)):
    def along_x(c):
        here = s[c].at(row, count)
        return here - before[c].at(row, count) if before is not None else here

    def along_y(c):
        return s[c].at(row, count) - s[c].prev(row, count)

    def along_z(c):
        here = s[c].at(row, count)
        return here - z_prev(here)

    out = []
    for c_x, c_y, c_z in ((XX, XY, XZ), (XY, YY, YZ), (XZ, YZ, ZZ)):
        terms = along_x(c_x)
        if c_y in have:
            terms = terms + along_y(c_y)
        if c_z in have:
            terms = terms + along_z(c_z)
        out.append(terms)
    return out


def strain(v, after, row, count, want=(XX, YY, ZZ, XY, XZ, YZ)):
    x, y, z = (v[c].at(row, count) for c in (VX, VY, VZ))
    if after is None:
        d_x = [-x, -y, -z]
    else:
        d_x = [after[c].at(row, count) - f for c, f in ((VX, x), (VY, y), (VZ, z))]
    out = {XX: d_x[0], YY: v[VY].next(row, count) - y, ZZ: z_next(z) - z}
    out["div"] = out[XX] + out[YY] + out[ZZ]
    if XY in want:
        out[XY] = v[VX].next(row, count) - x + d_x[1]
    if XZ in want:
        out[XZ] = z_next(x) - x + d_x[2]
    if YZ in want:
        out[YZ] = z_next(y) - y + (v[VZ].next(row, count) - z)
    return out


def stress_rate(e, lame, shear, want=(XX, YY, ZZ, XY, XZ, YZ)):
    spread = lame * e["div"]
    return {
        c: spread + 2.0 * shear * e[c] if c in (XX, YY, ZZ) else shear * e[c] for c in want
    }


def cell_plane(active, out):
    shape = (BY, out.shape[1])
    for j in range(out.shape[0] // BY):
        row = jnp.full(shape, active[0, 0, j].astype(jnp.float32))
        for k in range(1, out.shape[1] // BZ):
            row = jnp.where(lanes(shape) >= k * BZ, active[0, k, j].astype(jnp.float32), row)
        out[j * BY : (j + 1) * BY, :] = row


def chunks(size):
    return range(0, size, ROWS)


def is_even():
    return lax.rem(lax.axis_index("tile"), 2) == 0


def hand_out(by_pair, by_next, up, down):
    even = is_even()

    @pl.when(even)
    def _():
        by_pair[...] = up[...]
        by_next[...] = down[...]

    @pl.when(jnp.logical_not(even))
    def _():
        by_pair[...] = down[...]
        by_next[...] = up[...]


def take_in(by_pair, by_next, low, high):
    even = is_even()

    @pl.when(even)
    def _():
        low[...] = by_next[...]
        high[...] = by_pair[...]

    @pl.when(jnp.logical_not(even))
    def _():
        low[...] = by_pair[...]
        high[...] = by_next[...]


def class_tile(orientation, j, size_z):
    shape = (BY, size_z)
    out = jnp.full(shape, orientation[0, j, 0].astype(jnp.float32))
    for k in range(1, size_z // BZ):
        out = jnp.where(lanes(shape) >= k * BZ, orientation[0, j, k].astype(jnp.float32), out)
    return out


def here(row):
    return slice(row, row + ROWS)


def early_kernel(
    groups,
    active_hbm,
    orientation_hbm,
    state_hbm,
    source_hbm,
    lame_hbm,
    shear_hbm,
    buoyancy_hbm,
    by_pair,
    by_next,
    cells,
    tile,
    up,
    down,
    first,
    push,
    params,
    active,
    orientation,
    sems,
):
    size_y, size_z = cells.shape
    last = state_hbm.shape[1] - 1
    planes_at = (0, 0, 0, 1, last, last, last)
    arrays = (buoyancy_hbm, lame_hbm, shear_hbm)
    ends = [(active_hbm, active), (orientation_hbm, orientation)]
    ends += [(arrays[n % 3].at[x], params.at[n]) for n, x in enumerate(planes_at)]
    ends += [(state_hbm.at[:, 0], first), (source_hbm.at[0, 0], push)]
    ends += [
        (state_hbm.at[c, last], up.at[n * size_y : (n + 1) * size_y]) for n, c in enumerate(SIDE)
    ]
    copies = [pltpu.make_async_copy(*pair, sems.at[n]) for n, pair in enumerate(ends)]
    for copy in copies:
        copy.start()
    for copy in copies[:2]:
        copy.wait()
    cell_plane(active, cells)
    me = lax.axis_index("shot") if groups == 2 else 0
    last_block = orientation.shape[1] - 1
    tile[...] = class_tile(orientation, jnp.where(me == 0, last_block, 0), size_z)
    for copy in copies[2:9]:
        copy.wait()
    for row in chunks(size_y):
        c = time_step * cells[here(row), :]
        for n in range(7):
            params[n, here(row)] = c * params[n, here(row)]
    count = (up.shape[0] - 3 * size_y) // 4
    mine = pl.ds(pl.multiple_of(me * count, 8), count) if groups == 2 else slice(0, count)
    for n in range(4):
        to = slice(3 * size_y + n * count, 3 * size_y + (n + 1) * count)
        down[to] = params[n, mine]
        up[to] = params[(6, 4, 5, 6)[n], mine]
    for copy in copies[9:]:
        copy.wait()
    raw = {c: Plane(first, c) for c in range(9)}
    for row in chunks(size_y):
        c, cb = cells[here(row), :], params[0, here(row)]
        for n, term in enumerate(divergence(raw, None, row, ROWS)):
            value = c * raw[n].at(row, ROWS) + cb * term
            if n == VZ:
                value = value + time_step * c * push[here(row)].astype(jnp.float32)
            down[n * size_y + row : n * size_y + row + ROWS] = value
    hand_out(by_pair, by_next, up, down)


def late_kernel(
    state, source, buoyancy, lame, shear, cells, by_pair, by_next, st, push, coef, v2, s2, up, down
):
    width, size_y = state.shape[1], state.shape[2]
    last = width - 1
    for row in chunks(size_y):
        c = time_step * cells[here(row), :]
        for step in range(STEPS):
            for x in range(width):
                push[step, x, here(row)] = c * source[step, x, here(row)].astype(jnp.float32)
        for n, param in enumerate((buoyancy, lame, shear)):
            for x in range(width):
                coef[n, x, here(row)] = c * param[x, here(row)]

    def coefs(x, row):
        return [coef[n, x, here(row)] for n in range(3)]

    raw = [{c: Plane(state, c, x) for c in range(9)} for x in range(width)]
    one = [{c: Plane(st, c, x) for c in range(9)} for x in range(width)]
    two = {x: {c: Plane(v2, n, c) for c in VEL} for n, x in enumerate((0, 1, last))}
    for x in range(width):
        for row in chunks(size_y):
            c = cells[here(row), :]
            cb = coefs(x, row)[0]
            terms = divergence(raw[x], raw[x - 1] if x else None, row, ROWS)
            for comp, term in zip(VEL, terms):
                value = c * raw[x][comp].at(row, ROWS) + cb * term
                if comp == VZ:
                    value = value + push[0, x, here(row)]
                one[x][comp].set(row, value)
    for x in range(width):
        for row in chunks(size_y):
            c = cells[here(row), :]
            _, cl, cm = coefs(x, row)
            rate = stress_rate(strain(one[x], one[x + 1] if x < last else None, row, ROWS), cl, cm)
            for comp, term in rate.items():
                one[x][comp].set(row, c * raw[x][comp].at(row, ROWS) + term)
    for x in two:
        for row in chunks(size_y):
            cb = coefs(x, row)[0]
            terms = divergence(one[x], one[x - 1] if x else None, row, ROWS)
            for comp, term in zip(VEL, terms):
                value = one[x][comp].at(row, ROWS) + cb * term
                if comp == VZ:
                    value = value + push[1, x, here(row)]
                two[x][comp].set(row, value)
    stress = {c: Plane(s2, c - XX) for c in STRESS}
    for row in chunks(size_y):
        _, cl, cm = coefs(0, row)
        rate = stress_rate(strain(two[0], two[1], row, ROWS), cl, cm)
        for comp, term in rate.items():
            stress[comp].set(row, one[0][comp].at(row, ROWS) + term)
        _, cl, cm = coefs(last, row)
        rate = stress_rate(strain(two[last], None, row, ROWS, SIDE), cl, cm, SIDE)
        for n, comp in enumerate(SIDE):
            value = one[last][comp].at(row, ROWS)
            up[n, here(row)] = value
            up[3 + n, here(row)] = value + rate[comp]
    for row in chunks(size_y):
        cb = coefs(0, row)[0]
        terms = divergence(stress, None, row, ROWS)
        for comp, term in zip(VEL, terms):
            before = two[0][comp].at(row, ROWS)
            value = before + cb * term
            if comp == VZ:
                value = value + push[2, 0, here(row)]
            down[comp, here(row)] = before
            down[3 + comp, here(row)] = value
    hand_out(by_pair, by_next, up, down)


def beyond(v, cl, cm):
    spread = cl * v[0]
    return {XX: spread + 2.0 * cm * v[0], YY: spread, ZZ: spread, XY: cm * v[1], XZ: cm * v[2]}


def add(terms):
    return functools.reduce(jnp.add, terms)


def imaged(moved, forward, x, row):
    f = [forward[n, x, here(row)].astype(jnp.float32) for n in range(9)]
    trace = (moved[XX] + moved[YY] + moved[ZZ]) * (f[0] + f[1] + f[2])
    shear = add([moved[comp] * f[n] for n, comp in enumerate(STRESS)])
    density = add([moved[c] * f[6 + c] for c in VEL]) if VX in moved else None
    return trace, shear, density


def own_planes(st, end):
    width = st.shape[1]
    one = [{c: Plane(st, c, x) for c in range(9)} for x in range(width)]
    one[0] = {c: Plane(end, 0, c) for c in range(9)}
    one[-1] = {c: Plane(st, c, width - 1) if c in VEL else Plane(end, 1, c) for c in range(9)}
    return one


def near_kernel(groups, *refs):
    by_pair, by_next, *refs = refs
    if groups == 2:
        swapped, orientation, *refs = refs
    state, st, coef, cells, push, forward, end, w, third, outer, parts, known, *refs = refs
    if groups == 2:
        weights, *refs = refs
    low, high, high_v, d_s, d_v, *classes = refs
    width, size_y = st.shape[1], st.shape[2]
    last = width - 1
    take_in(by_pair, by_next, low, high)
    count = (low.shape[0] - 3 * size_y) // 4
    base = 3 * size_y
    if groups == 2:
        me = lax.axis_index("shot")
        mine = pl.ds(pl.multiple_of(me * count, 8), count)
        theirs = pl.ds(pl.multiple_of((1 - me) * count, 8), count)
        low_at = pl.multiple_of(jnp.where(is_even(), 4 * count, 0), 8)
        high_at = pl.multiple_of(jnp.where(is_even(), 0, 4 * count), 8)
        for n in range(4):
            if n < 3:
                outer[n, mine] = low[base + n * count : base + (n + 1) * count]
                outer[n, theirs] = swapped[pl.ds(low_at + n * count, count)]
            outer[3 + n, mine] = high[base + n * count : base + (n + 1) * count]
            outer[3 + n, theirs] = swapped[pl.ds(high_at + n * count, count)]
    else:
        for n in range(4):
            if n < 3:
                outer[n] = low[base + n * count : base + (n + 1) * count]
            outer[3 + n] = high[base + n * count : base + (n + 1) * count]

    def coefs(x, row):
        if x < 0:
            return [outer[n, here(row)] for n in range(3)]
        if x > last:
            return [outer[3 + n, here(row)] for n in range(3)]
        return [coef[n, x, here(row)] for n in range(3)]

    raw = [{c: Plane(state, c, x) for c in range(9)} for x in range(width)]
    old = [{c: Plane(st, c, x) for c in range(9)} for x in range(width)]
    one = own_planes(st, end)
    two = [{c: Plane(w, c, x) for c in range(9)} for x in range(width)]
    high_one = {c: Plane(high_v, c) for c in VEL}
    d_low_s, d_high_s, d_high_s_two = ({c: Plane(d_s, k, c - XX) for c in STRESS} for k in range(3))
    d_high_v, d_far_v, d_low_v = ({c: Plane(d_v, k, c) for c in VEL} for k in range(3))
    part_v, part_low, d_high_v_two, part_high = (
        {c: Plane(parts, k, n) for n, c in enumerate(names)}
        for k, names in enumerate((VEL, SIDE, VEL, VEL))
    )

    for row in chunks(size_y):
        cb, cb_high = coefs(0, row)[0], coefs(last + 1, row)[0]
        for n, (comp, c) in enumerate(zip(VEL, SIDE)):
            at = slice(n * size_y + row, n * size_y + row + ROWS)
            one[0][comp].set(row, old[0][comp].at(row, ROWS) - cb * low[at])
            delta = -cb_high * raw[last][c].at(row, ROWS)
            d_high_v[comp].set(row, delta)
            high_one[comp].set(row, high[at] + delta)
    for row in chunks(size_y):
        c = cells[here(row), :]
        _, cl, cm = coefs(0, row)
        for comp, term in stress_rate(strain(one[0], one[1], row, ROWS), cl, cm).items():
            one[0][comp].set(row, c * raw[0][comp].at(row, ROWS) + term)
        _, cl, cm = coefs(last, row)
        terms = beyond([high_one[comp].at(row, ROWS) for comp in VEL], cl, cm)
        for comp in STRESS:
            value = old[last][comp].at(row, ROWS)
            one[last][comp].set(row, value + terms[comp] if comp in terms else value)
        _, cl, cm = coefs(-1, row)
        for comp, term in beyond([one[0][comp].at(row, ROWS) for comp in VEL], cl, cm).items():
            d_low_s[comp].set(row, term)
        _, cl, cm = coefs(last + 1, row)
        for comp, term in stress_rate(strain(d_high_v, None, row, ROWS), cl, cm).items():
            d_high_s[comp].set(row, term)

    for row in chunks(size_y):
        for x in range(width):
            cb = coefs(x, row)[0]
            terms = divergence(one[x], one[x - 1] if x else d_low_s, row, ROWS)
            for comp, term in zip(VEL, terms):
                value = one[x][comp].at(row, ROWS) + cb * term
                if comp == VZ:
                    value = value + push[1, x, here(row)]
                (two[x] if x else part_v)[comp].set(row, value)
        cb = coefs(last + 1, row)[0]
        for comp, term in zip(VEL, divergence(d_high_s, one[last], row, ROWS)):
            d_high_v_two[comp].set(row, d_high_v[comp].at(row, ROWS) + cb * term)
        cb = outer[6, here(row)]
        for comp, c in zip(VEL, SIDE):
            d_far_v[comp].set(row, -cb * d_high_s[c].at(row, ROWS))
        cb = coefs(-1, row)[0]
        terms = divergence(d_low_s, None, row, ROWS, (XX, YY, ZZ, XY, XZ))
        for comp, term in zip(VEL, terms):
            d_low_v[comp].set(row, cb * term)
    for row in chunks(size_y):
        for x in range(1, width):
            _, cl, cm = coefs(x, row)
            after = two[x + 1] if x < last else None
            for comp, term in stress_rate(strain(two[x], after, row, ROWS), cl, cm).items():
                two[x][comp].set(row, one[x][comp].at(row, ROWS) + term)
        _, cl, cm = coefs(-1, row)
        rate = stress_rate(strain(d_low_v, None, row, ROWS, SIDE), cl, cm, SIDE)
        for comp, term in rate.items():
            part_low[comp].set(row, d_low_s[comp].at(row, ROWS) + term)
        _, cl, cm = coefs(last + 1, row)
        for comp, term in stress_rate(strain(d_high_v_two, d_far_v, row, ROWS), cl, cm).items():
            d_high_s_two[comp].set(row, d_high_s[comp].at(row, ROWS) + term)
    for row in chunks(size_y):
        cb = coefs(last + 1, row)[0]
        for comp, term in zip(VEL, divergence(d_high_s_two, None, row, ROWS)):
            part_high[comp].set(row, d_high_v_two[comp].at(row, ROWS) + cb * term)
        for x in range(2, last):
            cb = coefs(x, row)[0]
            for comp, term in zip(VEL, divergence(two[x], two[x - 1], row, ROWS)):
                value = two[x][comp].at(row, ROWS) + cb * term
                if comp == VZ:
                    value = value + push[2, x, here(row)]
                third[comp, x, here(row)] = value
    for row in chunks(size_y):
        for x in range(width):
            inner = 1 <= x < last
            v, t = [one[x]], [one[x]] + [two[x]] * inner
            if x:
                v.append(two[x])
            if 2 <= x < last:
                v.append({c: Plane(third, c, x) for c in VEL})
            moved = {c: add([k[c].at(row, ROWS) for k in v]) for c in VEL}
            moved |= {c: add([k[c].at(row, ROWS) for k in t]) for c in STRESS}
            for n, value in enumerate(imaged(moved, forward, x, row)):
                known[n, x, here(row)] = value
    if groups != 2:
        return

    (classes,) = classes
    rows_held = weights.shape[1]
    own = rows_held - BY
    first = pl.multiple_of(me * BY, BY)
    for j in range(own // BY):
        classes[pl.ds(first + j * BY, BY), :] = class_tile(orientation, j, weights.shape[2])
    classes[pl.ds(pl.multiple_of((1 - me) * own, BY), BY), :] = swapped[8 * count :, :]
    klass = classes[...]
    for column in range(3):
        table = jnp.full(klass.shape, weight_table[3][column], jnp.float32)
        for k in range(3):
            table = jnp.where(klass == k, weight_table[k][column], table)
        weights[column] = smooth_rate * table


def far_kernel(groups, *refs):
    by_pair, by_next, st, end, w, third, outer, parts, known, coef, push, forward, final, *refs = refs
    *images, low, high, edge, low_s, high_v, image = refs
    width, size_y = st.shape[1], st.shape[2]
    last = width - 1
    take_in(by_pair, by_next, low, high)

    def coefs(x, row):
        if x < 0:
            return [outer[n, here(row)] for n in range(3)]
        if x > last:
            return [outer[3 + n, here(row)] for n in range(3)]
        return [coef[n, x, here(row)] for n in range(3)]

    one = own_planes(st, end)
    part = [{c: Plane(w, c, x) for c in range(9)} for x in range(width)]
    two = [dict(p) for p in part]
    for c in range(9):
        two[0][c] = Plane(edge, 0, c)
        if c >= XX:
            two[last][c] = Plane(edge, 1, c)
    three = [{c: Plane(final, c, x) for c in range(9)} for x in range(width)]
    part_v, part_low, d_high_v_two, part_high = (
        {c: Plane(parts, k, n) for n, c in enumerate(names)}
        for k, names in enumerate((VEL, SIDE, VEL, VEL))
    )
    low_two = {c: Plane(low_s, n) for n, c in enumerate(SIDE)}
    high_three = {c: Plane(high_v, c) for c in VEL}

    for row in chunks(size_y):
        cb = coefs(0, row)[0]
        moved = []
        for n, comp in enumerate(VEL):
            moved.append(part_v[comp].at(row, ROWS) - cb * low[n, here(row)])
            two[0][comp].set(row, moved[n])
        _, cl, cm = coefs(-1, row)
        terms = beyond(moved, cl, cm)
        for n, comp in enumerate(SIDE):
            value = low[3 + n, here(row)] + part_low[comp].at(row, ROWS)
            low_two[comp].set(row, value + terms[comp])
        _, cl, cm = coefs(last, row)
        cb = coefs(last + 1, row)[0]
        moved = [high[n, here(row)] + d_high_v_two[n].at(row, ROWS) for n in VEL]
        terms = beyond(moved, cl, cm)
        values = {}
        for comp in STRESS:
            value = part[last][comp].at(row, ROWS)
            values[comp] = value + terms[comp] if comp in terms else value
            two[last][comp].set(row, values[comp])
        for n, comp in enumerate(SIDE):
            value = high[3 + n, here(row)] + part_high[n].at(row, ROWS)
            high_three[n].set(row, value - cb * values[comp])
    for row in chunks(size_y):
        _, cl, cm = coefs(0, row)
        for comp, term in stress_rate(strain(two[0], two[1], row, ROWS), cl, cm).items():
            two[0][comp].set(row, one[0][comp].at(row, ROWS) + term)

    for row in chunks(size_y):
        for x in range(width):
            if 2 <= x < last:
                for comp in VEL:
                    three[x][comp].set(row, third[comp, x, here(row)])
                continue
            cb = coefs(x, row)[0]
            terms = divergence(two[x], two[x - 1] if x else low_two, row, ROWS)
            for comp, term in zip(VEL, terms):
                value = two[x][comp].at(row, ROWS) + cb * term
                if comp == VZ:
                    value = value + push[2, x, here(row)]
                three[x][comp].set(row, value)
    for row in chunks(size_y):
        for x in range(width):
            _, cl, cm = coefs(x, row)
            after = three[x + 1] if x < last else high_three
            rate = stress_rate(strain(three[x], after, row, ROWS), cl, cm)
            moved = {}
            for comp in STRESS:
                before = two[x][comp].at(row, ROWS)
                value = before + rate[comp]
                three[x][comp].set(row, value)
                moved[comp] = value if 1 <= x < last else before + value
            if not 2 <= x < last:
                for comp in VEL:
                    moved[comp] = three[x][comp].at(row, ROWS)
                    if not x:
                        moved[comp] = two[x][comp].at(row, ROWS) + moved[comp]
            for n, value in enumerate(imaged(moved, forward, x, row)):
                before = known[n, x, here(row)]
                image[n, x, here(row)] = before if value is None else before + value

    if groups != 2:
        images[0][...] = image[...]
        return
    give, keep = images
    me = lax.axis_index("shot")
    count = keep.shape[2]
    mine = pl.ds(pl.multiple_of(me * (size_y - count), 8), count)
    theirs = pl.ds(pl.multiple_of((1 - me) * (size_y - count), 8), count)
    for n in range(3):
        for x in range(width):
            give[n, x] = image[n, x, theirs, :]
            keep[n, x] = image[n, x, mine, :]


def y_prev(f):
    return jnp.where(rows(f.shape) == 0, 0.0, pltpu.roll(f, 1, f.ndim - 2))


def y_next(f):
    size = f.shape[-2]
    return jnp.where(rows(f.shape) == size - 1, 0.0, pltpu.roll(f, size - 1, f.ndim - 2))


def sweep(g, before, after, weights):
    w_x, w_y, w_z = weights
    twice = 2.0 * g
    along_x = -twice
    for plane in (before, after):
        if plane is not None:
            along_x = along_x + plane
    along_y = y_next(g) + y_prev(g) - twice
    along_z = z_next(g) + z_prev(g) - twice
    return g + (w_x * along_x + w_y * along_y + w_z * along_z)


def edge_row(me, own):
    return jnp.where(me == 0, own, BY - 1)


def sum_kernel(scale, keep, received, weights, by_pair, by_next, grad, swept, up, down):
    width, count, size_z = grad.shape[1:]
    own = count - BY
    me = lax.axis_index("shot")
    first = pl.multiple_of(me * BY, BY)
    mine = pl.ds(first, own)
    edge = pl.ds(edge_row(me, own), 1)
    last = width - 1
    w = [weights[k] for k in range(3)]
    for to in (up, down):
        to[6 * own :, :] = jnp.zeros((BY, size_z), jnp.float32)
        for j in range(own // BY):
            row = weights[0, pl.ds(pl.multiple_of(first + j * BY, BY), BY), :][0:1]
            to[6 * own + 3 + j : 6 * own + 4 + j, :] = row
    for n in range(3):
        for x in range(width):
            grad[n, x] = (keep[n, x] + received[n, x]) * scale
        swept[n, 0] = sweep(grad[n, 0], None, grad[n, 1], w)
        swept[n, 1] = sweep(grad[n, last], grad[n, last - 1], None, w)
        for to, x, side in ((up, last, 1), (down, 0, 0)):
            to[2 * n * own : (2 * n + 1) * own, :] = grad[n, x, mine, :]
            to[(2 * n + 1) * own : (2 * n + 2) * own, :] = swept[n, side, mine, :]
            to[6 * own + n : 6 * own + n + 1, :] = grad[n, x, edge, :]
    hand_out(by_pair, by_next, up, down)


def inner_kernel(grad, swept, weights, full, half):
    width = grad.shape[1]
    last = width - 1
    w = [weights[k] for k in range(3)]
    for n in range(3):
        full[n, 0] = swept[n, 0]
        full[n, last] = swept[n, 1]
        for x in range(1, last):
            full[n, x] = sweep(grad[n, x], grad[n, x - 1], grad[n, x + 1], w)
        for x in range(1, last):
            half[n, x - 1] = sweep(
                full[n, x],
                full[n, x - 1] if x > 1 else None,
                full[n, x + 1] if x < last - 1 else None,
                w,
            )


def side_kernel(near, *refs):
    got, *refs = refs
    if not near:
        _, *refs = refs
    grad, full, half, weights, out, beside, result, sems = refs
    width, count, size_z = grad.shape[1:]
    own = count - BY
    me = lax.axis_index("shot")
    first = pl.multiple_of(me * BY, BY)
    mine = pl.ds(first, own)
    edge = pl.ds(edge_row(me, own), 1)
    upper = is_even() if near else jnp.logical_not(is_even())
    end = jnp.where(upper, width - 1, 0)
    inner = jnp.where(upper, width - 2, 1)
    beside[...] = jnp.zeros(beside.shape, jnp.float32)
    for n in range(3):
        beside[n, mine, :] = got[2 * n * own : (2 * n + 1) * own, :]
        beside[n, edge, :] = got[6 * own + n : 6 * own + n + 1, :]
        beside[3 + n, mine, :] = got[(2 * n + 1) * own : (2 * n + 2) * own, :]
    for j in range(own // BY):
        row = got[6 * own + 3 + j : 6 * own + 4 + j, :]
        to = pl.ds(pl.multiple_of(first + j * BY, BY), BY)
        beside[6, to, :] = jnp.broadcast_to(row, (BY, size_z))
    w = [weights[k] for k in range(3)]
    for n in range(3):
        value = full[n, end] + w[0] * beside[n]
        outer = beside[3 + n] + beside[6] * grad[n, end]
        result[n, 0] = sweep(value, outer, full[n, inner], w)
        result[n, 1] = half[n, inner - 1] + w[0] * value
    copies = [
        pltpu.make_async_copy(result.at[:, k, mine, :], out.at[:, x], sems.at[k])
        for k, x in enumerate((end, inner))
    ]
    for copy in copies:
        copy.start()
    for copy in copies:
        copy.wait()


def extended(block, sides, width):
    for axis, dim in sides:
        count = lax.axis_size(axis)
        forward = [(i, i + 1) for i in range(count - 1)]
        backward = [(target, source) for source, target in forward]
        low = lax.ppermute(
            lax.slice_in_dim(block, block.shape[dim] - width, None, axis=dim), axis, forward
        )
        high = lax.ppermute(lax.slice_in_dim(block, 0, width, axis=dim), axis, backward)
        block = jnp.concatenate([low, block, high], axis=dim)
    return block


def smooth_anywhere(image, orientation):
    groups = lax.axis_size("shot")
    owned = image.shape[2] // groups
    total = lax.psum(image, "shot")
    grad = lax.dynamic_slice_in_dim(total, lax.axis_index("shot") * owned, owned, 2)
    grad = grad * (STEPS * groups) ** (-0.5)
    weights = []
    for column in range(3):
        table = jnp.zeros(orientation.shape, jnp.float32)
        for klass in range(4):
            table = table + (orientation == klass).astype(jnp.float32) * weight_table[klass][column]
        table = jnp.repeat(jnp.repeat(table, image.shape[1], 0), BY, 1)
        weights.append(jnp.repeat(table, BZ, 2))
    for _ in range(SWEEPS):
        padded = extended(grad, (("shot", 2), ("tile", 1)), 1)
        padded = jnp.pad(padded, ((0, 0), (0, 0), (0, 0), (1, 1)))
        center = padded[:, 1:-1, 1:-1, 1:-1]
        lap_x = padded[:, 2:, 1:-1, 1:-1] + padded[:, :-2, 1:-1, 1:-1] - 2.0 * center
        lap_y = padded[:, 1:-1, 2:, 1:-1] + padded[:, 1:-1, :-2, 1:-1] - 2.0 * center
        lap_z = padded[:, 1:-1, 1:-1, 2:] + padded[:, 1:-1, 1:-1, :-2] - 2.0 * center
        grad = grad + smooth_rate * (weights[0] * lap_x + weights[1] * lap_y + weights[2] * lap_z)
    return grad


def both_ways(by_pair, by_next):
    count = lax.axis_size("tile")
    out = []
    for array, start in ((by_pair, 0), (by_next, 1)):
        pairs = [(i, i + 1) for i in range(start, count - 1, 2)]
        out.append(lax.ppermute(array, "tile", pairs + [(b, a) for a, b in pairs]))
    return out


def f32(*shape):
    return jax.ShapeDtypeStruct(shape, jnp.float32)


def in_hbm(array):
    return pltpu.with_memory_space_constraint(array, pltpu.HBM)


def call(kernel, outs, args, scratch, scalars=(), space=VMEM, out_space=VMEM, held=None):
    specs = [SMEM if n in scalars else HBM if n == held else space for n in range(len(args))]
    return pl.pallas_call(
        kernel,
        out_shape=outs,
        in_specs=specs,
        out_specs=jax.tree.map(lambda _: out_space, outs),
        scratch_shapes=[
            pltpu.VMEM(shape, jnp.float32) if isinstance(shape, tuple) else shape
            for shape in scratch
        ],
        input_output_aliases={} if held is None else {held: 0},
        compiler_params=pltpu.CompilerParams(vmem_limit_bytes=24 * 1024 * 1024),
    )(*args)


def local(
    adjoint_state,
    adjoint_source,
    forward_field,
    lame_first,
    shear_modulus,
    buoyancy,
    active_blocks,
    orientation,
):
    width, size_y, size_z = lame_first.shape
    plane = (size_y, size_z)
    groups = lax.axis_size("shot")
    state, source, forward = adjoint_state[0], adjoint_source[0], forward_field[0]
    active = jnp.swapaxes(active_blocks, 1, 2)
    grid = f32(9, width, *plane)
    count = size_y // 2 if groups == 2 else size_y
    early = (3 * size_y + 4 * count, size_z)
    by_pair, by_next, cells, tile = call(
        functools.partial(early_kernel, groups),
        [f32(*early), f32(*early), f32(*plane), f32(BY, size_z)],
        [
            in_hbm(a)
            for a in (active, orientation, state, source, lame_first, shear_modulus, buoyancy)
        ],
        [
            early,
            early,
            (9, *plane),
            pltpu.VMEM(plane, source.dtype),
            (7, *plane),
            pltpu.SMEM(active.shape, jnp.int32),
            pltpu.SMEM(orientation.shape, jnp.int32),
            pltpu.SemaphoreType.DMA((14,)),
        ],
        space=HBM,
    )
    by_pair, by_next = both_ways(by_pair, by_next)
    late_pair, late_next, st, push, coef = call(
        late_kernel,
        [f32(6, *plane), f32(6, *plane), grid, f32(STEPS, width, *plane), f32(3, width, *plane)],
        (state, source, buoyancy, lame_first, shear_modulus, cells),
        [(3, 3, *plane), (6, *plane), (6, *plane), (6, *plane)],
    )
    late_pair, late_next = both_ways(late_pair, late_next)
    args, outs, scalars = [by_pair, by_next], [], ()
    scratch = [early, early, (3, *plane), (3, 6, *plane), (3, 3, *plane)]
    owned = size_y // groups
    held = owned + BY
    if groups == 2:
        swapped = jnp.concatenate([by_pair[3 * size_y :], by_next[3 * size_y :], tile])
        swapped = lax.ppermute(swapped, "shot", [(0, 1), (1, 0)])
        args += [swapped, orientation]
        outs = [f32(3, held, size_z)]
        scratch += [(held, size_z)]
        scalars = (3,)
    three = f32(3, width, *plane)
    end, w, third, outer, parts, known, *weights = call(
        functools.partial(near_kernel, groups),
        [f32(2, 9, *plane), grid, three, f32(7, *plane), f32(4, 3, *plane), three, *outs],
        [*args, state, st, coef, cells, push, forward],
        scratch,
        scalars,
    )
    block = (3, width, held, size_z)
    images = [f32(*block), f32(*block)] if groups == 2 else [f32(3, width, *plane)]
    final, *images = call(
        functools.partial(far_kernel, groups),
        [pltpu.VMEM(grid.shape, grid.dtype), *images],
        [late_pair, late_next, st, end, w, third, outer, parts, known, coef, push, forward],
        [(6, *plane), (6, *plane), (2, 9, *plane), (3, *plane), (3, *plane), (3, width, *plane)],
    )
    if groups != 2:
        return final[None], smooth_anywhere(images[0], orientation)
    give, keep = images
    (weights,) = weights
    received = lax.ppermute(give, "shot", [(0, 1), (1, 0)])
    message = (6 * owned + BY, size_z)
    by_pair, by_next, grad, swept = call(
        functools.partial(sum_kernel, (STEPS * groups) ** (-0.5)),
        [f32(*message), f32(*message), f32(*block), f32(3, 2, held, size_z)],
        (keep, received, weights),
        [message, message],
    )
    by_pair, by_next = both_ways(by_pair, by_next)
    full, half = call(
        inner_kernel,
        [f32(*block), f32(3, width - 2, held, size_z)],
        (grad, swept, weights),
        [],
    )
    gradient = f32(3, width, owned, size_z)
    scratch = [(7, held, size_z), (3, 2, held, size_z), pltpu.SemaphoreType.DMA((2,))]
    rest = (grad, full, half, weights)
    gradient = call(
        functools.partial(side_kernel, True), gradient, (by_pair, *rest), scratch, out_space=HBM
    )
    gradient = call(
        functools.partial(side_kernel, False),
        f32(*gradient.shape),
        (by_next, gradient, *rest),
        scratch,
        out_space=HBM,
        held=1,
    )
    return final[None], gradient


def solution(mesh):
    return jax.shard_map(
        local,
        mesh=mesh,
        in_specs=(
            P("shot", None, "tile", None, None),
            P("shot", None, "tile", None, None),
            P("shot", None, "tile", None, None),
            P("tile", None, None),
            P("tile", None, None),
            P("tile", None, None),
            P("tile", None, None),
            P("tile", "shot", None),
        ),
        out_specs=(P("shot", None, "tile", None, None), P(None, "tile", "shot", None)),
        check_vma=False,
    )
```

```python
import functools

import jax
import jax.numpy as jnp
from jax import lax
from jax.experimental import pallas as pl
from jax.experimental.pallas import tpu as pltpu
from jax.sharding import PartitionSpec as P

BY = 8
BZ = 32
STEPS = 3
SWEEPS = 2

time_step = 0.25
smooth_rate = 0.1
weight_table = ((1.0, 1.0, 0.25), (0.25, 1.0, 1.0), (1.0, 0.25, 1.0), (0.6, 0.6, 0.6))

VX, VY, VZ, XX, YY, ZZ, XY, XZ, YZ = range(9)
VEL = (VX, VY, VZ)
SIDE = (XX, XY, XZ)
STRESS = (XX, YY, ZZ, XY, XZ, YZ)
ROWS = 32
VMEM = pl.BlockSpec(memory_space=pltpu.VMEM)
SMEM = pl.BlockSpec(memory_space=pltpu.SMEM)
HBM = pl.BlockSpec(memory_space=pltpu.HBM)


def lanes(shape):
    return lax.broadcasted_iota(jnp.int32, shape, len(shape) - 1)


def rows(shape):
    return lax.broadcasted_iota(jnp.int32, shape, len(shape) - 2)


def z_prev(f):
    return jnp.where(lanes(f.shape) == 0, 0.0, pltpu.roll(f, 1, f.ndim - 1))


def z_next(f):
    size = f.shape[-1]
    return jnp.where(lanes(f.shape) == size - 1, 0.0, pltpu.roll(f, size - 1, f.ndim - 1))


class Plane:
    def __init__(self, ref, *index):
        self.ref, self.index = ref, index
        self.size = ref.shape[len(index)]

    def at(self, row, count):
        return self.ref[self.index + (slice(row, row + count),)]

    def prev(self, row, count):
        if row:
            return self.at(row - 1, count)
        edge = pltpu.roll(self.at(0, 8), 1, 0)
        edge = jnp.where(rows(edge.shape) == 0, 0.0, edge)
        return jnp.concatenate([edge, self.at(7, count - 8)], 0)

    def next(self, row, count):
        if row + count < self.size:
            return self.at(row + 1, count)
        edge = pltpu.roll(self.at(self.size - 8, 8), 7, 0)
        edge = jnp.where(rows(edge.shape) == 7, 0.0, edge)
        return jnp.concatenate([self.at(row + 1, count - 8), edge], 0)

    def set(self, row, value):
        self.ref[self.index + (slice(row, row + value.shape[0]),)] = value


def planes(ref, comps, *index):
    return {c: Plane(ref, n, *index) for n, c in enumerate(comps)}


def divergence(s, before, row, count, have=(XX, YY, ZZ, XY, XZ, YZ)):
    def along_x(c):
        here = s[c].at(row, count)
        return here - before[c].at(row, count) if before is not None else here

    def along_y(c):
        return s[c].at(row, count) - s[c].prev(row, count)

    def along_z(c):
        here = s[c].at(row, count)
        return here - z_prev(here)

    out = []
    for c_x, c_y, c_z in ((XX, XY, XZ), (XY, YY, YZ), (XZ, YZ, ZZ)):
        terms = along_x(c_x)
        if c_y in have:
            terms = terms + along_y(c_y)
        if c_z in have:
            terms = terms + along_z(c_z)
        out.append(terms)
    return out


def strain(v, after, row, count, want=(XX, YY, ZZ, XY, XZ, YZ)):
    x, y, z = (v[c].at(row, count) for c in (VX, VY, VZ))
    if after is None:
        d_x = [-x, -y, -z]
    else:
        d_x = [after[c].at(row, count) - f for c, f in ((VX, x), (VY, y), (VZ, z))]
    out = {XX: d_x[0], YY: v[VY].next(row, count) - y, ZZ: z_next(z) - z}
    out["div"] = out[XX] + out[YY] + out[ZZ]
    if XY in want:
        out[XY] = v[VX].next(row, count) - x + d_x[1]
    if XZ in want:
        out[XZ] = z_next(x) - x + d_x[2]
    if YZ in want:
        out[YZ] = z_next(y) - y + (v[VZ].next(row, count) - z)
    return out


def stress_rate(e, lame, shear, want=(XX, YY, ZZ, XY, XZ, YZ)):
    spread = lame * e["div"]
    return {
        c: spread + 2.0 * shear * e[c] if c in (XX, YY, ZZ) else shear * e[c] for c in want
    }


def cell_plane(active, out):
    shape = (BY, out.shape[1])
    for j in range(out.shape[0] // BY):
        row = jnp.full(shape, active[0, 0, j].astype(jnp.float32))
        for k in range(1, out.shape[1] // BZ):
            row = jnp.where(lanes(shape) >= k * BZ, active[0, k, j].astype(jnp.float32), row)
        out[j * BY : (j + 1) * BY, :] = row


def chunks(size):
    return range(0, size, ROWS)


def is_even():
    return lax.rem(lax.axis_index("tile"), 2) == 0


def hand_out(by_pair, by_next, up, down):
    even = is_even()

    @pl.when(even)
    def _():
        by_pair[...] = up[...]
        by_next[...] = down[...]

    @pl.when(jnp.logical_not(even))
    def _():
        by_pair[...] = down[...]
        by_next[...] = up[...]


def take_in(by_pair, by_next, low, high):
    even = is_even()

    @pl.when(even)
    def _():
        low[...] = by_next[...]
        high[...] = by_pair[...]

    @pl.when(jnp.logical_not(even))
    def _():
        low[...] = by_pair[...]
        high[...] = by_next[...]


def class_tile(orientation, j, size_z):
    shape = (BY, size_z)
    out = jnp.full(shape, orientation[0, j, 0].astype(jnp.float32))
    for k in range(1, size_z // BZ):
        out = jnp.where(lanes(shape) >= k * BZ, orientation[0, j, k].astype(jnp.float32), out)
    return out


def here(row):
    return slice(row, row + ROWS)


def early_kernel(
    groups,
    active_hbm,
    orientation_hbm,
    state_hbm,
    source_hbm,
    lame_hbm,
    shear_hbm,
    buoyancy_hbm,
    by_pair,
    by_next,
    cells,
    tile,
    up,
    down,
    first,
    push,
    params,
    active,
    orientation,
    sems,
):
    size_y, size_z = cells.shape
    last = state_hbm.shape[1] - 1
    planes_at = (0, 0, 0, 1, last, last, last)
    arrays = (buoyancy_hbm, lame_hbm, shear_hbm)
    ends = [(active_hbm, active), (orientation_hbm, orientation)]
    ends += [(arrays[n % 3].at[x], params.at[n]) for n, x in enumerate(planes_at)]
    ends += [(state_hbm.at[:, 0], first), (source_hbm.at[0, 0], push)]
    ends += [
        (state_hbm.at[c, last], up.at[n * size_y : (n + 1) * size_y]) for n, c in enumerate(SIDE)
    ]
    copies = [pltpu.make_async_copy(*pair, sems.at[n]) for n, pair in enumerate(ends)]
    for copy in copies:
        copy.start()
    for copy in copies[:2]:
        copy.wait()
    cell_plane(active, cells)
    me = lax.axis_index("shot") if groups == 2 else 0
    last_block = orientation.shape[1] - 1
    tile[...] = class_tile(orientation, jnp.where(me == 0, last_block, 0), size_z)
    for copy in copies[2:9]:
        copy.wait()
    for row in chunks(size_y):
        c = time_step * cells[here(row), :]
        for n in range(7):
            params[n, here(row)] = c * params[n, here(row)]
    count = (up.shape[0] - 3 * size_y) // 4
    mine = pl.ds(pl.multiple_of(me * count, 8), count) if groups == 2 else slice(0, count)
    for n in range(4):
        to = slice(3 * size_y + n * count, 3 * size_y + (n + 1) * count)
        down[to] = params[n, mine]
        up[to] = params[(6, 4, 5, 6)[n], mine]
    for copy in copies[9:]:
        copy.wait()
    raw = {c: Plane(first, c) for c in range(9)}
    for row in chunks(size_y):
        c, cb = cells[here(row), :], params[0, here(row)]
        for n, term in enumerate(divergence(raw, None, row, ROWS)):
            value = c * raw[n].at(row, ROWS) + cb * term
            if n == VZ:
                value = value + time_step * c * push[here(row)].astype(jnp.float32)
            down[n * size_y + row : n * size_y + row + ROWS] = value
    hand_out(by_pair, by_next, up, down)


def late_kernel(
    state, source, buoyancy, lame, shear, cells, by_pair, by_next, st, push, coef, v2, s2, up, down
):
    width, size_y = state.shape[1], state.shape[2]
    last = width - 1
    for row in chunks(size_y):
        c = time_step * cells[here(row), :]
        for step in range(STEPS):
            for x in range(width):
                push[step, x, here(row)] = c * source[step, x, here(row)].astype(jnp.float32)
        for n, param in enumerate((buoyancy, lame, shear)):
            for x in range(width):
                coef[n, x, here(row)] = c * param[x, here(row)]

    def coefs(x, row):
        return [coef[n, x, here(row)] for n in range(3)]

    raw = [{c: Plane(state, c, x) for c in range(9)} for x in range(width)]
    one = [{c: Plane(st, c, x) for c in range(9)} for x in range(width)]
    two = {x: {c: Plane(v2, n, c) for c in VEL} for n, x in enumerate((0, 1, last))}
    for x in range(width):
        for row in chunks(size_y):
            c = cells[here(row), :]
            cb = coefs(x, row)[0]
            terms = divergence(raw[x], raw[x - 1] if x else None, row, ROWS)
            for comp, term in zip(VEL, terms):
                value = c * raw[x][comp].at(row, ROWS) + cb * term
                if comp == VZ:
                    value = value + push[0, x, here(row)]
                one[x][comp].set(row, value)
    for x in range(width):
        for row in chunks(size_y):
            c = cells[here(row), :]
            _, cl, cm = coefs(x, row)
            rate = stress_rate(strain(one[x], one[x + 1] if x < last else None, row, ROWS), cl, cm)
            for comp, term in rate.items():
                one[x][comp].set(row, c * raw[x][comp].at(row, ROWS) + term)
    for x in two:
        for row in chunks(size_y):
            cb = coefs(x, row)[0]
            terms = divergence(one[x], one[x - 1] if x else None, row, ROWS)
            for comp, term in zip(VEL, terms):
                value = one[x][comp].at(row, ROWS) + cb * term
                if comp == VZ:
                    value = value + push[1, x, here(row)]
                two[x][comp].set(row, value)
    stress = {c: Plane(s2, c - XX) for c in STRESS}
    for row in chunks(size_y):
        _, cl, cm = coefs(0, row)
        rate = stress_rate(strain(two[0], two[1], row, ROWS), cl, cm)
        for comp, term in rate.items():
            stress[comp].set(row, one[0][comp].at(row, ROWS) + term)
        _, cl, cm = coefs(last, row)
        rate = stress_rate(strain(two[last], None, row, ROWS, SIDE), cl, cm, SIDE)
        for n, comp in enumerate(SIDE):
            value = one[last][comp].at(row, ROWS)
            up[n, here(row)] = value
            up[3 + n, here(row)] = value + rate[comp]
    for row in chunks(size_y):
        cb = coefs(0, row)[0]
        terms = divergence(stress, None, row, ROWS)
        for comp, term in zip(VEL, terms):
            before = two[0][comp].at(row, ROWS)
            value = before + cb * term
            if comp == VZ:
                value = value + push[2, 0, here(row)]
            down[comp, here(row)] = before
            down[3 + comp, here(row)] = value
    hand_out(by_pair, by_next, up, down)


def beyond(v, cl, cm):
    spread = cl * v[0]
    return {XX: spread + 2.0 * cm * v[0], YY: spread, ZZ: spread, XY: cm * v[1], XZ: cm * v[2]}


def add(terms):
    return functools.reduce(jnp.add, terms)


def imaged(moved, forward, x, row):
    f = [forward[n, x, here(row)].astype(jnp.float32) for n in range(9)]
    trace = (moved[XX] + moved[YY] + moved[ZZ]) * (f[0] + f[1] + f[2])
    shear = add([moved[comp] * f[n] for n, comp in enumerate(STRESS)])
    density = add([moved[c] * f[6 + c] for c in VEL]) if VX in moved else None
    return trace, shear, density


def own_planes(st, end):
    width = st.shape[1]
    one = [{c: Plane(st, c, x) for c in range(9)} for x in range(width)]
    one[0] = {c: Plane(end, 0, c) for c in range(9)}
    one[-1] = {c: Plane(st, c, width - 1) if c in VEL else Plane(end, 1, c) for c in range(9)}
    return one


def near_kernel(groups, *refs):
    by_pair, by_next, *refs = refs
    if groups == 2:
        swapped, orientation, *refs = refs
    state, st, coef, cells, push, forward, end, w, third, outer, parts, known, *refs = refs
    if groups == 2:
        weights, *refs = refs
    low, high, high_v, d_s, d_v, *classes = refs
    width, size_y = st.shape[1], st.shape[2]
    last = width - 1
    take_in(by_pair, by_next, low, high)
    count = (low.shape[0] - 3 * size_y) // 4
    base = 3 * size_y
    if groups == 2:
        me = lax.axis_index("shot")
        mine = pl.ds(pl.multiple_of(me * count, 8), count)
        theirs = pl.ds(pl.multiple_of((1 - me) * count, 8), count)
        low_at = pl.multiple_of(jnp.where(is_even(), 4 * count, 0), 8)
        high_at = pl.multiple_of(jnp.where(is_even(), 0, 4 * count), 8)
        for n in range(4):
            if n < 3:
                outer[n, mine] = low[base + n * count : base + (n + 1) * count]
                outer[n, theirs] = swapped[pl.ds(low_at + n * count, count)]
            outer[3 + n, mine] = high[base + n * count : base + (n + 1) * count]
            outer[3 + n, theirs] = swapped[pl.ds(high_at + n * count, count)]
    else:
        for n in range(4):
            if n < 3:
                outer[n] = low[base + n * count : base + (n + 1) * count]
            outer[3 + n] = high[base + n * count : base + (n + 1) * count]

    def coefs(x, row):
        if x < 0:
            return [outer[n, here(row)] for n in range(3)]
        if x > last:
            return [outer[3 + n, here(row)] for n in range(3)]
        return [coef[n, x, here(row)] for n in range(3)]

    raw = [{c: Plane(state, c, x) for c in range(9)} for x in range(width)]
    old = [{c: Plane(st, c, x) for c in range(9)} for x in range(width)]
    one = own_planes(st, end)
    two = [{c: Plane(w, c, x) for c in range(9)} for x in range(width)]
    high_one = {c: Plane(high_v, c) for c in VEL}
    d_low_s, d_high_s, d_high_s_two = ({c: Plane(d_s, k, c - XX) for c in STRESS} for k in range(3))
    d_high_v, d_far_v, d_low_v = ({c: Plane(d_v, k, c) for c in VEL} for k in range(3))
    part_v, part_low, d_high_v_two, part_high = (
        {c: Plane(parts, k, n) for n, c in enumerate(names)}
        for k, names in enumerate((VEL, SIDE, VEL, VEL))
    )

    for row in chunks(size_y):
        cb, cb_high = coefs(0, row)[0], coefs(last + 1, row)[0]
        for n, (comp, c) in enumerate(zip(VEL, SIDE)):
            at = slice(n * size_y + row, n * size_y + row + ROWS)
            one[0][comp].set(row, old[0][comp].at(row, ROWS) - cb * low[at])
            delta = -cb_high * raw[last][c].at(row, ROWS)
            d_high_v[comp].set(row, delta)
            high_one[comp].set(row, high[at] + delta)
    for row in chunks(size_y):
        c = cells[here(row), :]
        _, cl, cm = coefs(0, row)
        for comp, term in stress_rate(strain(one[0], one[1], row, ROWS), cl, cm).items():
            one[0][comp].set(row, c * raw[0][comp].at(row, ROWS) + term)
        _, cl, cm = coefs(last, row)
        terms = beyond([high_one[comp].at(row, ROWS) for comp in VEL], cl, cm)
        for comp in STRESS:
            value = old[last][comp].at(row, ROWS)
            one[last][comp].set(row, value + terms[comp] if comp in terms else value)
        _, cl, cm = coefs(-1, row)
        for comp, term in beyond([one[0][comp].at(row, ROWS) for comp in VEL], cl, cm).items():
            d_low_s[comp].set(row, term)
        _, cl, cm = coefs(last + 1, row)
        for comp, term in stress_rate(strain(d_high_v, None, row, ROWS), cl, cm).items():
            d_high_s[comp].set(row, term)

    for row in chunks(size_y):
        for x in range(width):
            cb = coefs(x, row)[0]
            terms = divergence(one[x], one[x - 1] if x else d_low_s, row, ROWS)
            for comp, term in zip(VEL, terms):
                value = one[x][comp].at(row, ROWS) + cb * term
                if comp == VZ:
                    value = value + push[1, x, here(row)]
                (two[x] if x else part_v)[comp].set(row, value)
        cb = coefs(last + 1, row)[0]
        for comp, term in zip(VEL, divergence(d_high_s, one[last], row, ROWS)):
            d_high_v_two[comp].set(row, d_high_v[comp].at(row, ROWS) + cb * term)
        cb = outer[6, here(row)]
        for comp, c in zip(VEL, SIDE):
            d_far_v[comp].set(row, -cb * d_high_s[c].at(row, ROWS))
        cb = coefs(-1, row)[0]
        terms = divergence(d_low_s, None, row, ROWS, (XX, YY, ZZ, XY, XZ))
        for comp, term in zip(VEL, terms):
            d_low_v[comp].set(row, cb * term)
    for row in chunks(size_y):
        for x in range(1, width):
            _, cl, cm = coefs(x, row)
            after = two[x + 1] if x < last else None
            for comp, term in stress_rate(strain(two[x], after, row, ROWS), cl, cm).items():
                two[x][comp].set(row, one[x][comp].at(row, ROWS) + term)
        _, cl, cm = coefs(-1, row)
        rate = stress_rate(strain(d_low_v, None, row, ROWS, SIDE), cl, cm, SIDE)
        for comp, term in rate.items():
            part_low[comp].set(row, d_low_s[comp].at(row, ROWS) + term)
        _, cl, cm = coefs(last + 1, row)
        for comp, term in stress_rate(strain(d_high_v_two, d_far_v, row, ROWS), cl, cm).items():
            d_high_s_two[comp].set(row, d_high_s[comp].at(row, ROWS) + term)
    for row in chunks(size_y):
        cb = coefs(last + 1, row)[0]
        for comp, term in zip(VEL, divergence(d_high_s_two, None, row, ROWS)):
            part_high[comp].set(row, d_high_v_two[comp].at(row, ROWS) + cb * term)
        for x in range(2, last):
            cb = coefs(x, row)[0]
            for comp, term in zip(VEL, divergence(two[x], two[x - 1], row, ROWS)):
                value = two[x][comp].at(row, ROWS) + cb * term
                if comp == VZ:
                    value = value + push[2, x, here(row)]
                third[comp, x, here(row)] = value
    for row in chunks(size_y):
        for x in range(width):
            inner = 1 <= x < last
            v, t = [one[x]], [one[x]] + [two[x]] * inner
            if x:
                v.append(two[x])
            if 2 <= x < last:
                v.append({c: Plane(third, c, x) for c in VEL})
            moved = {c: add([k[c].at(row, ROWS) for k in v]) for c in VEL}
            moved |= {c: add([k[c].at(row, ROWS) for k in t]) for c in STRESS}
            for n, value in enumerate(imaged(moved, forward, x, row)):
                known[n, x, here(row)] = value
    if groups != 2:
        return

    (classes,) = classes
    rows_held = weights.shape[1]
    own = rows_held - BY
    first = pl.multiple_of(me * BY, BY)
    for j in range(own // BY):
        classes[pl.ds(first + j * BY, BY), :] = class_tile(orientation, j, weights.shape[2])
    classes[pl.ds(pl.multiple_of((1 - me) * own, BY), BY), :] = swapped[8 * count :, :]
    klass = classes[...]
    for column in range(3):
        table = jnp.full(klass.shape, weight_table[3][column], jnp.float32)
        for k in range(3):
            table = jnp.where(klass == k, weight_table[k][column], table)
        weights[column] = smooth_rate * table


def far_kernel(groups, *refs):
    by_pair, by_next, st, end, w, third, outer, parts, known, coef, push, forward, final, *refs = refs
    *images, low, high, edge, low_s, high_v, image = refs
    width, size_y = st.shape[1], st.shape[2]
    last = width - 1
    take_in(by_pair, by_next, low, high)

    def coefs(x, row):
        if x < 0:
            return [outer[n, here(row)] for n in range(3)]
        if x > last:
            return [outer[3 + n, here(row)] for n in range(3)]
        return [coef[n, x, here(row)] for n in range(3)]

    one = own_planes(st, end)
    part = [{c: Plane(w, c, x) for c in range(9)} for x in range(width)]
    two = [dict(p) for p in part]
    for c in range(9):
        two[0][c] = Plane(edge, 0, c)
        if c >= XX:
            two[last][c] = Plane(edge, 1, c)
    three = [{c: Plane(final, c, x) for c in range(9)} for x in range(width)]
    part_v, part_low, d_high_v_two, part_high = (
        {c: Plane(parts, k, n) for n, c in enumerate(names)}
        for k, names in enumerate((VEL, SIDE, VEL, VEL))
    )
    low_two = {c: Plane(low_s, n) for n, c in enumerate(SIDE)}
    high_three = {c: Plane(high_v, c) for c in VEL}

    for row in chunks(size_y):
        cb = coefs(0, row)[0]
        moved = []
        for n, comp in enumerate(VEL):
            moved.append(part_v[comp].at(row, ROWS) - cb * low[n, here(row)])
            two[0][comp].set(row, moved[n])
        _, cl, cm = coefs(-1, row)
        terms = beyond(moved, cl, cm)
        for n, comp in enumerate(SIDE):
            value = low[3 + n, here(row)] + part_low[comp].at(row, ROWS)
            low_two[comp].set(row, value + terms[comp])
        _, cl, cm = coefs(last, row)
        cb = coefs(last + 1, row)[0]
        moved = [high[n, here(row)] + d_high_v_two[n].at(row, ROWS) for n in VEL]
        terms = beyond(moved, cl, cm)
        values = {}
        for comp in STRESS:
            value = part[last][comp].at(row, ROWS)
            values[comp] = value + terms[comp] if comp in terms else value
            two[last][comp].set(row, values[comp])
        for n, comp in enumerate(SIDE):
            value = high[3 + n, here(row)] + part_high[n].at(row, ROWS)
            high_three[n].set(row, value - cb * values[comp])
    for row in chunks(size_y):
        _, cl, cm = coefs(0, row)
        for comp, term in stress_rate(strain(two[0], two[1], row, ROWS), cl, cm).items():
            two[0][comp].set(row, one[0][comp].at(row, ROWS) + term)

    for row in chunks(size_y):
        for x in range(width):
            if 2 <= x < last:
                for comp in VEL:
                    three[x][comp].set(row, third[comp, x, here(row)])
                continue
            cb = coefs(x, row)[0]
            terms = divergence(two[x], two[x - 1] if x else low_two, row, ROWS)
            for comp, term in zip(VEL, terms):
                value = two[x][comp].at(row, ROWS) + cb * term
                if comp == VZ:
                    value = value + push[2, x, here(row)]
                three[x][comp].set(row, value)
    for row in chunks(size_y):
        for x in range(width):
            _, cl, cm = coefs(x, row)
            after = three[x + 1] if x < last else high_three
            rate = stress_rate(strain(three[x], after, row, ROWS), cl, cm)
            moved = {}
            for comp in STRESS:
                before = two[x][comp].at(row, ROWS)
                value = before + rate[comp]
                three[x][comp].set(row, value)
                moved[comp] = value if 1 <= x < last else before + value
            if not 2 <= x < last:
                for comp in VEL:
                    moved[comp] = three[x][comp].at(row, ROWS)
                    if not x:
                        moved[comp] = two[x][comp].at(row, ROWS) + moved[comp]
            for n, value in enumerate(imaged(moved, forward, x, row)):
                before = known[n, x, here(row)]
                image[n, x, here(row)] = before if value is None else before + value

    if groups != 2:
        images[0][...] = image[...]
        return
    give, keep = images
    me = lax.axis_index("shot")
    count = keep.shape[2]
    mine = pl.ds(pl.multiple_of(me * (size_y - count), 8), count)
    theirs = pl.ds(pl.multiple_of((1 - me) * (size_y - count), 8), count)
    for n in range(3):
        for x in range(width):
            give[n, x] = image[n, x, theirs, :]
            keep[n, x] = image[n, x, mine, :]


def y_prev(f):
    return jnp.where(rows(f.shape) == 0, 0.0, pltpu.roll(f, 1, f.ndim - 2))


def y_next(f):
    size = f.shape[-2]
    return jnp.where(rows(f.shape) == size - 1, 0.0, pltpu.roll(f, size - 1, f.ndim - 2))


def sweep(g, before, after, weights):
    w_x, w_y, w_z = weights
    twice = 2.0 * g
    along_x = -twice
    for plane in (before, after):
        if plane is not None:
            along_x = along_x + plane
    along_y = y_next(g) + y_prev(g) - twice
    along_z = z_next(g) + z_prev(g) - twice
    return g + (w_x * along_x + w_y * along_y + w_z * along_z)


def edge_row(me, own):
    return jnp.where(me == 0, own, BY - 1)


def sum_kernel(scale, keep, received, weights, by_pair, by_next, grad, swept, up, down):
    width, count, size_z = grad.shape[1:]
    own = count - BY
    me = lax.axis_index("shot")
    first = pl.multiple_of(me * BY, BY)
    mine = pl.ds(first, own)
    edge = pl.ds(edge_row(me, own), 1)
    last = width - 1
    w = [weights[k] for k in range(3)]
    for to in (up, down):
        to[6 * own :, :] = jnp.zeros((BY, size_z), jnp.float32)
        for j in range(own // BY):
            row = weights[0, pl.ds(pl.multiple_of(first + j * BY, BY), BY), :][0:1]
            to[6 * own + 3 + j : 6 * own + 4 + j, :] = row
    for n in range(3):
        for x in range(width):
            grad[n, x] = (keep[n, x] + received[n, x]) * scale
        swept[n, 0] = sweep(grad[n, 0], None, grad[n, 1], w)
        swept[n, 1] = sweep(grad[n, last], grad[n, last - 1], None, w)
        for to, x, side in ((up, last, 1), (down, 0, 0)):
            to[2 * n * own : (2 * n + 1) * own, :] = grad[n, x, mine, :]
            to[(2 * n + 1) * own : (2 * n + 2) * own, :] = swept[n, side, mine, :]
            to[6 * own + n : 6 * own + n + 1, :] = grad[n, x, edge, :]
    hand_out(by_pair, by_next, up, down)


def inner_kernel(grad, swept, weights, full, half):
    width = grad.shape[1]
    last = width - 1
    w = [weights[k] for k in range(3)]
    for n in range(3):
        full[n, 0] = swept[n, 0]
        full[n, last] = swept[n, 1]
        for x in range(1, last):
            full[n, x] = sweep(grad[n, x], grad[n, x - 1], grad[n, x + 1], w)
        for x in range(1, last):
            half[n, x - 1] = sweep(
                full[n, x],
                full[n, x - 1] if x > 1 else None,
                full[n, x + 1] if x < last - 1 else None,
                w,
            )


def side_kernel(near, *refs):
    got, *refs = refs
    if not near:
        _, *refs = refs
    grad, full, half, weights, out, beside, result, sems = refs
    width, count, size_z = grad.shape[1:]
    own = count - BY
    me = lax.axis_index("shot")
    first = pl.multiple_of(me * BY, BY)
    mine = pl.ds(first, own)
    edge = pl.ds(edge_row(me, own), 1)
    upper = is_even() if near else jnp.logical_not(is_even())
    end = jnp.where(upper, width - 1, 0)
    inner = jnp.where(upper, width - 2, 1)
    beside[...] = jnp.zeros(beside.shape, jnp.float32)
    for n in range(3):
        beside[n, mine, :] = got[2 * n * own : (2 * n + 1) * own, :]
        beside[n, edge, :] = got[6 * own + n : 6 * own + n + 1, :]
        beside[3 + n, mine, :] = got[(2 * n + 1) * own : (2 * n + 2) * own, :]
    for j in range(own // BY):
        row = got[6 * own + 3 + j : 6 * own + 4 + j, :]
        to = pl.ds(pl.multiple_of(first + j * BY, BY), BY)
        beside[6, to, :] = jnp.broadcast_to(row, (BY, size_z))
    w = [weights[k] for k in range(3)]
    for n in range(3):
        value = full[n, end] + w[0] * beside[n]
        outer = beside[3 + n] + beside[6] * grad[n, end]
        result[n, 0] = sweep(value, outer, full[n, inner], w)
        result[n, 1] = half[n, inner - 1] + w[0] * value
    copies = [
        pltpu.make_async_copy(result.at[:, k, mine, :], out.at[:, x], sems.at[k])
        for k, x in enumerate((end, inner))
    ]
    for copy in copies:
        copy.start()
    for copy in copies:
        copy.wait()


def extended(block, sides, width):
    for axis, dim in sides:
        count = lax.axis_size(axis)
        forward = [(i, i + 1) for i in range(count - 1)]
        backward = [(target, source) for source, target in forward]
        low = lax.ppermute(
            lax.slice_in_dim(block, block.shape[dim] - width, None, axis=dim), axis, forward
        )
        high = lax.ppermute(lax.slice_in_dim(block, 0, width, axis=dim), axis, backward)
        block = jnp.concatenate([low, block, high], axis=dim)
    return block


def smooth_anywhere(image, orientation):
    groups = lax.axis_size("shot")
    owned = image.shape[2] // groups
    total = lax.psum(image, "shot")
    grad = lax.dynamic_slice_in_dim(total, lax.axis_index("shot") * owned, owned, 2)
    grad = grad * (STEPS * groups) ** (-0.5)
    weights = []
    for column in range(3):
        table = jnp.zeros(orientation.shape, jnp.float32)
        for klass in range(4):
            table = table + (orientation == klass).astype(jnp.float32) * weight_table[klass][column]
        table = jnp.repeat(jnp.repeat(table, image.shape[1], 0), BY, 1)
        weights.append(jnp.repeat(table, BZ, 2))
    for _ in range(SWEEPS):
        padded = extended(grad, (("shot", 2), ("tile", 1)), 1)
        padded = jnp.pad(padded, ((0, 0), (0, 0), (0, 0), (1, 1)))
        center = padded[:, 1:-1, 1:-1, 1:-1]
        lap_x = padded[:, 2:, 1:-1, 1:-1] + padded[:, :-2, 1:-1, 1:-1] - 2.0 * center
        lap_y = padded[:, 1:-1, 2:, 1:-1] + padded[:, 1:-1, :-2, 1:-1] - 2.0 * center
        lap_z = padded[:, 1:-1, 1:-1, 2:] + padded[:, 1:-1, 1:-1, :-2] - 2.0 * center
        grad = grad + smooth_rate * (weights[0] * lap_x + weights[1] * lap_y + weights[2] * lap_z)
    return grad


def both_ways(by_pair, by_next):
    count = lax.axis_size("tile")
    out = []
    for array, start in ((by_pair, 0), (by_next, 1)):
        pairs = [(i, i + 1) for i in range(start, count - 1, 2)]
        out.append(lax.ppermute(array, "tile", pairs + [(b, a) for a, b in pairs]))
    return out


def f32(*shape):
    return jax.ShapeDtypeStruct(shape, jnp.float32)


def in_hbm(array):
    return pltpu.with_memory_space_constraint(array, pltpu.HBM)


def call(kernel, outs, args, scratch, scalars=(), space=VMEM, out_space=VMEM, held=None):
    specs = [SMEM if n in scalars else HBM if n == held else space for n in range(len(args))]
    return pl.pallas_call(
        kernel,
        out_shape=outs,
        in_specs=specs,
        out_specs=jax.tree.map(lambda _: out_space, outs),
        scratch_shapes=[
            pltpu.VMEM(shape, jnp.float32) if isinstance(shape, tuple) else shape
            for shape in scratch
        ],
        input_output_aliases={} if held is None else {held: 0},
        compiler_params=pltpu.CompilerParams(vmem_limit_bytes=24 * 1024 * 1024),
    )(*args)


def local(
    adjoint_state,
    adjoint_source,
    forward_field,
    lame_first,
    shear_modulus,
    buoyancy,
    active_blocks,
    orientation,
):
    width, size_y, size_z = lame_first.shape
    plane = (size_y, size_z)
    groups = lax.axis_size("shot")
    state, source, forward = adjoint_state[0], adjoint_source[0], forward_field[0]
    active = jnp.swapaxes(active_blocks, 1, 2)
    grid = f32(9, width, *plane)
    count = size_y // 2 if groups == 2 else size_y
    early = (3 * size_y + 4 * count, size_z)
    by_pair, by_next, cells, tile = call(
        functools.partial(early_kernel, groups),
        [f32(*early), f32(*early), f32(*plane), f32(BY, size_z)],
        [
            in_hbm(a)
            for a in (active, orientation, state, source, lame_first, shear_modulus, buoyancy)
        ],
        [
            early,
            early,
            (9, *plane),
            pltpu.VMEM(plane, source.dtype),
            (7, *plane),
            pltpu.SMEM(active.shape, jnp.int32),
            pltpu.SMEM(orientation.shape, jnp.int32),
            pltpu.SemaphoreType.DMA((14,)),
        ],
        space=HBM,
    )
    by_pair, by_next = both_ways(by_pair, by_next)
    late_pair, late_next, st, push, coef = call(
        late_kernel,
        [f32(6, *plane), f32(6, *plane), grid, f32(STEPS, width, *plane), f32(3, width, *plane)],
        [*(in_hbm(a) for a in (state, source, buoyancy, lame_first, shear_modulus)), cells],
        [(3, 3, *plane), (6, *plane), (6, *plane), (6, *plane)],
    )
    late_pair, late_next = both_ways(late_pair, late_next)
    args, outs, scalars = [by_pair, by_next], [], ()
    scratch = [early, early, (3, *plane), (3, 6, *plane), (3, 3, *plane)]
    owned = size_y // groups
    held = owned + BY
    if groups == 2:
        swapped = jnp.concatenate([by_pair[3 * size_y :], by_next[3 * size_y :], tile])
        swapped = lax.ppermute(swapped, "shot", [(0, 1), (1, 0)])
        args += [swapped, orientation]
        outs = [f32(3, held, size_z)]
        scratch += [(held, size_z)]
        scalars = (3,)
    three = f32(3, width, *plane)
    end, w, third, outer, parts, known, *weights = call(
        functools.partial(near_kernel, groups),
        [f32(2, 9, *plane), grid, three, f32(7, *plane), f32(4, 3, *plane), three, *outs],
        [*args, state, st, coef, cells, push, forward],
        scratch,
        scalars,
    )
    block = (3, width, held, size_z)
    images = [f32(*block), f32(*block)] if groups == 2 else [f32(3, width, *plane)]
    final, *images = call(
        functools.partial(far_kernel, groups),
        [pltpu.VMEM(grid.shape, grid.dtype), *images],
        [late_pair, late_next, st, end, w, third, outer, parts, known, coef, push, forward],
        [(6, *plane), (6, *plane), (2, 9, *plane), (3, *plane), (3, *plane), (3, width, *plane)],
    )
    if groups != 2:
        return final[None], smooth_anywhere(images[0], orientation)
    give, keep = images
    (weights,) = weights
    received = lax.ppermute(give, "shot", [(0, 1), (1, 0)])
    message = (6 * owned + BY, size_z)
    by_pair, by_next, grad, swept = call(
        functools.partial(sum_kernel, (STEPS * groups) ** (-0.5)),
        [f32(*message), f32(*message), f32(*block), f32(3, 2, held, size_z)],
        (keep, received, weights),
        [message, message],
    )
    by_pair, by_next = both_ways(by_pair, by_next)
    full, half = call(
        inner_kernel,
        [f32(*block), f32(3, width - 2, held, size_z)],
        (grad, swept, weights),
        [],
    )
    gradient = f32(3, width, owned, size_z)
    scratch = [(7, held, size_z), (3, 2, held, size_z), pltpu.SemaphoreType.DMA((2,))]
    rest = (grad, full, half, weights)
    gradient = call(
        functools.partial(side_kernel, True), gradient, (by_pair, *rest), scratch, out_space=HBM
    )
    gradient = call(
        functools.partial(side_kernel, False),
        f32(*gradient.shape),
        (by_next, gradient, *rest),
        scratch,
        out_space=HBM,
        held=1,
    )
    return final[None], gradient


def solution(mesh):
    return jax.shard_map(
        local,
        mesh=mesh,
        in_specs=(
            P("shot", None, "tile", None, None),
            P("shot", None, "tile", None, None),
            P("shot", None, "tile", None, None),
            P("tile", None, None),
            P("tile", None, None),
            P("tile", None, None),
            P("tile", None, None),
            P("tile", "shot", None),
        ),
        out_specs=(P("shot", None, "tile", None, None), P(None, "tile", "shot", None)),
        check_vma=False,
    )
```

```python
import functools

import jax
import jax.numpy as jnp
from jax import lax
from jax.experimental import pallas as pl
from jax.experimental.pallas import tpu as pltpu
from jax.sharding import PartitionSpec as P

BY = 8
BZ = 32
STEPS = 3
SWEEPS = 2

time_step = 0.25
smooth_rate = 0.1
weight_table = ((1.0, 1.0, 0.25), (0.25, 1.0, 1.0), (1.0, 0.25, 1.0), (0.6, 0.6, 0.6))

VX, VY, VZ, XX, YY, ZZ, XY, XZ, YZ = range(9)
VEL = (VX, VY, VZ)
SIDE = (XX, XY, XZ)
STRESS = (XX, YY, ZZ, XY, XZ, YZ)
ROWS = 32
VMEM = pl.BlockSpec(memory_space=pltpu.VMEM)
SMEM = pl.BlockSpec(memory_space=pltpu.SMEM)
HBM = pl.BlockSpec(memory_space=pltpu.HBM)


def lanes(shape):
    return lax.broadcasted_iota(jnp.int32, shape, len(shape) - 1)


def rows(shape):
    return lax.broadcasted_iota(jnp.int32, shape, len(shape) - 2)


def z_prev(f):
    return jnp.where(lanes(f.shape) == 0, 0.0, pltpu.roll(f, 1, f.ndim - 1))


def z_next(f):
    size = f.shape[-1]
    return jnp.where(lanes(f.shape) == size - 1, 0.0, pltpu.roll(f, size - 1, f.ndim - 1))


class Plane:
    def __init__(self, ref, *index):
        self.ref, self.index = ref, index
        self.size = ref.shape[len(index)]

    def at(self, row, count):
        return self.ref[self.index + (slice(row, row + count),)]

    def prev(self, row, count):
        if row:
            return self.at(row - 1, count)
        edge = pltpu.roll(self.at(0, 8), 1, 0)
        edge = jnp.where(rows(edge.shape) == 0, 0.0, edge)
        return jnp.concatenate([edge, self.at(7, count - 8)], 0)

    def next(self, row, count):
        if row + count < self.size:
            return self.at(row + 1, count)
        edge = pltpu.roll(self.at(self.size - 8, 8), 7, 0)
        edge = jnp.where(rows(edge.shape) == 7, 0.0, edge)
        return jnp.concatenate([self.at(row + 1, count - 8), edge], 0)

    def set(self, row, value):
        self.ref[self.index + (slice(row, row + value.shape[0]),)] = value


def planes(ref, comps, *index):
    return {c: Plane(ref, n, *index) for n, c in enumerate(comps)}


def divergence(s, before, row, count, have=(XX, YY, ZZ, XY, XZ, YZ)):
    def along_x(c):
        here = s[c].at(row, count)
        return here - before[c].at(row, count) if before is not None else here

    def along_y(c):
        return s[c].at(row, count) - s[c].prev(row, count)

    def along_z(c):
        here = s[c].at(row, count)
        return here - z_prev(here)

    out = []
    for c_x, c_y, c_z in ((XX, XY, XZ), (XY, YY, YZ), (XZ, YZ, ZZ)):
        terms = along_x(c_x)
        if c_y in have:
            terms = terms + along_y(c_y)
        if c_z in have:
            terms = terms + along_z(c_z)
        out.append(terms)
    return out


def strain(v, after, row, count, want=(XX, YY, ZZ, XY, XZ, YZ)):
    x, y, z = (v[c].at(row, count) for c in (VX, VY, VZ))
    if after is None:
        d_x = [-x, -y, -z]
    else:
        d_x = [after[c].at(row, count) - f for c, f in ((VX, x), (VY, y), (VZ, z))]
    out = {XX: d_x[0], YY: v[VY].next(row, count) - y, ZZ: z_next(z) - z}
    out["div"] = out[XX] + out[YY] + out[ZZ]
    if XY in want:
        out[XY] = v[VX].next(row, count) - x + d_x[1]
    if XZ in want:
        out[XZ] = z_next(x) - x + d_x[2]
    if YZ in want:
        out[YZ] = z_next(y) - y + (v[VZ].next(row, count) - z)
    return out


def stress_rate(e, lame, shear, want=(XX, YY, ZZ, XY, XZ, YZ)):
    spread = lame * e["div"]
    return {
        c: spread + 2.0 * shear * e[c] if c in (XX, YY, ZZ) else shear * e[c] for c in want
    }


def cell_plane(active, out):
    shape = (BY, out.shape[1])
    for j in range(out.shape[0] // BY):
        row = jnp.full(shape, active[0, 0, j].astype(jnp.float32))
        for k in range(1, out.shape[1] // BZ):
            row = jnp.where(lanes(shape) >= k * BZ, active[0, k, j].astype(jnp.float32), row)
        out[j * BY : (j + 1) * BY, :] = row


def chunks(size):
    return range(0, size, ROWS)


def is_even():
    return lax.rem(lax.axis_index("tile"), 2) == 0


def hand_out(by_pair, by_next, up, down):
    even = is_even()

    @pl.when(even)
    def _():
        by_pair[...] = up[...]
        by_next[...] = down[...]

    @pl.when(jnp.logical_not(even))
    def _():
        by_pair[...] = down[...]
        by_next[...] = up[...]


def take_in(by_pair, by_next, low, high):
    even = is_even()

    @pl.when(even)
    def _():
        low[...] = by_next[...]
        high[...] = by_pair[...]

    @pl.when(jnp.logical_not(even))
    def _():
        low[...] = by_pair[...]
        high[...] = by_next[...]

    clear_ends(low, high)


def no_neighbour(upper):
    return lax.axis_index("tile") == (lax.axis_size("tile") - 1 if upper else 0)


def clear_ends(low, high):
    for upper, ref in ((False, low), (True, high)):

        @pl.when(no_neighbour(upper))
        def _(ref=ref):
            ref[...] = jnp.zeros(ref.shape, jnp.float32)


def class_tile(orientation, j, size_z):
    shape = (BY, size_z)
    out = jnp.full(shape, orientation[0, j, 0].astype(jnp.float32))
    for k in range(1, size_z // BZ):
        out = jnp.where(lanes(shape) >= k * BZ, orientation[0, j, k].astype(jnp.float32), out)
    return out


def here(row):
    return slice(row, row + ROWS)


def early_kernel(
    groups,
    active_hbm,
    orientation_hbm,
    state_hbm,
    source_hbm,
    lame_hbm,
    shear_hbm,
    buoyancy_hbm,
    by_pair,
    by_next,
    cells,
    tile,
    up,
    down,
    first,
    push,
    params,
    active,
    orientation,
    sems,
):
    size_y, size_z = cells.shape
    last = state_hbm.shape[1] - 1
    planes_at = (0, 0, 0, 1, last, last, last)
    arrays = (buoyancy_hbm, lame_hbm, shear_hbm)
    ends = [(active_hbm, active), (orientation_hbm, orientation)]
    ends += [(arrays[n % 3].at[x], params.at[n]) for n, x in enumerate(planes_at)]
    ends += [(state_hbm.at[:, 0], first), (source_hbm.at[0, 0], push)]
    ends += [
        (state_hbm.at[c, last], up.at[n * size_y : (n + 1) * size_y]) for n, c in enumerate(SIDE)
    ]
    copies = [pltpu.make_async_copy(*pair, sems.at[n]) for n, pair in enumerate(ends)]
    for copy in copies:
        copy.start()
    for copy in copies[:2]:
        copy.wait()
    cell_plane(active, cells)
    me = lax.axis_index("shot") if groups == 2 else 0
    last_block = orientation.shape[1] - 1
    tile[...] = class_tile(orientation, jnp.where(me == 0, last_block, 0), size_z)
    for copy in copies[2:9]:
        copy.wait()
    for row in chunks(size_y):
        c = time_step * cells[here(row), :]
        for n in range(7):
            params[n, here(row)] = c * params[n, here(row)]
    count = (up.shape[0] - 3 * size_y) // 4
    mine = pl.ds(pl.multiple_of(me * count, 8), count) if groups == 2 else slice(0, count)
    for n in range(4):
        to = slice(3 * size_y + n * count, 3 * size_y + (n + 1) * count)
        down[to] = params[n, mine]
        up[to] = params[(6, 4, 5, 6)[n], mine]
    for copy in copies[9:]:
        copy.wait()
    raw = {c: Plane(first, c) for c in range(9)}
    for row in chunks(size_y):
        c, cb = cells[here(row), :], params[0, here(row)]
        for n, term in enumerate(divergence(raw, None, row, ROWS)):
            value = c * raw[n].at(row, ROWS) + cb * term
            if n == VZ:
                value = value + time_step * c * push[here(row)].astype(jnp.float32)
            down[n * size_y + row : n * size_y + row + ROWS] = value
    hand_out(by_pair, by_next, up, down)


def late_kernel(
    state, source, buoyancy, lame, shear, cells, by_pair, by_next, st, push, coef, v2, s2, up, down
):
    width, size_y = state.shape[1], state.shape[2]
    last = width - 1
    for row in chunks(size_y):
        c = time_step * cells[here(row), :]
        for step in range(STEPS):
            for x in range(width):
                push[step, x, here(row)] = c * source[step, x, here(row)].astype(jnp.float32)
        for n, param in enumerate((buoyancy, lame, shear)):
            for x in range(width):
                coef[n, x, here(row)] = c * param[x, here(row)]

    def coefs(x, row):
        return [coef[n, x, here(row)] for n in range(3)]

    raw = [{c: Plane(state, c, x) for c in range(9)} for x in range(width)]
    one = [{c: Plane(st, c, x) for c in range(9)} for x in range(width)]
    two = {x: {c: Plane(v2, n, c) for c in VEL} for n, x in enumerate((0, 1, last))}
    for x in range(width):
        for row in chunks(size_y):
            c = cells[here(row), :]
            cb = coefs(x, row)[0]
            terms = divergence(raw[x], raw[x - 1] if x else None, row, ROWS)
            for comp, term in zip(VEL, terms):
                value = c * raw[x][comp].at(row, ROWS) + cb * term
                if comp == VZ:
                    value = value + push[0, x, here(row)]
                one[x][comp].set(row, value)
    for x in range(width):
        for row in chunks(size_y):
            c = cells[here(row), :]
            _, cl, cm = coefs(x, row)
            rate = stress_rate(strain(one[x], one[x + 1] if x < last else None, row, ROWS), cl, cm)
            for comp, term in rate.items():
                one[x][comp].set(row, c * raw[x][comp].at(row, ROWS) + term)
    for x in two:
        for row in chunks(size_y):
            cb = coefs(x, row)[0]
            terms = divergence(one[x], one[x - 1] if x else None, row, ROWS)
            for comp, term in zip(VEL, terms):
                value = one[x][comp].at(row, ROWS) + cb * term
                if comp == VZ:
                    value = value + push[1, x, here(row)]
                two[x][comp].set(row, value)
    stress = {c: Plane(s2, c - XX) for c in STRESS}
    for row in chunks(size_y):
        _, cl, cm = coefs(0, row)
        rate = stress_rate(strain(two[0], two[1], row, ROWS), cl, cm)
        for comp, term in rate.items():
            stress[comp].set(row, one[0][comp].at(row, ROWS) + term)
        _, cl, cm = coefs(last, row)
        rate = stress_rate(strain(two[last], None, row, ROWS, SIDE), cl, cm, SIDE)
        for n, comp in enumerate(SIDE):
            value = one[last][comp].at(row, ROWS)
            up[n, here(row)] = value
            up[3 + n, here(row)] = value + rate[comp]
    for row in chunks(size_y):
        cb = coefs(0, row)[0]
        terms = divergence(stress, None, row, ROWS)
        for comp, term in zip(VEL, terms):
            before = two[0][comp].at(row, ROWS)
            value = before + cb * term
            if comp == VZ:
                value = value + push[2, 0, here(row)]
            down[comp, here(row)] = before
            down[3 + comp, here(row)] = value
    hand_out(by_pair, by_next, up, down)


def beyond(v, cl, cm):
    spread = cl * v[0]
    return {XX: spread + 2.0 * cm * v[0], YY: spread, ZZ: spread, XY: cm * v[1], XZ: cm * v[2]}


def add(terms):
    return functools.reduce(jnp.add, terms)


def imaged(moved, forward, x, row):
    f = [forward[n, x, here(row)].astype(jnp.float32) for n in range(9)]
    trace = (moved[XX] + moved[YY] + moved[ZZ]) * (f[0] + f[1] + f[2])
    shear = add([moved[comp] * f[n] for n, comp in enumerate(STRESS)])
    density = add([moved[c] * f[6 + c] for c in VEL]) if VX in moved else None
    return trace, shear, density


def own_planes(st, end):
    width = st.shape[1]
    one = [{c: Plane(st, c, x) for c in range(9)} for x in range(width)]
    one[0] = {c: Plane(end, 0, c) for c in range(9)}
    one[-1] = {c: Plane(st, c, width - 1) if c in VEL else Plane(end, 1, c) for c in range(9)}
    return one


def near_kernel(groups, *refs):
    by_pair, by_next, *refs = refs
    if groups == 2:
        swapped, orientation, *refs = refs
    state, st, coef, cells, push, forward, end, w, third, outer, parts, known, *refs = refs
    if groups == 2:
        weights, *refs = refs
    low, high, high_v, d_s, d_v, *classes = refs
    width, size_y = st.shape[1], st.shape[2]
    last = width - 1
    take_in(by_pair, by_next, low, high)
    count = (low.shape[0] - 3 * size_y) // 4
    base = 3 * size_y
    if groups == 2:
        me = lax.axis_index("shot")
        mine = pl.ds(pl.multiple_of(me * count, 8), count)
        theirs = pl.ds(pl.multiple_of((1 - me) * count, 8), count)
        low_at = pl.multiple_of(jnp.where(is_even(), 4 * count, 0), 8)
        high_at = pl.multiple_of(jnp.where(is_even(), 0, 4 * count), 8)
        for n in range(4):
            if n < 3:
                outer[n, mine] = low[base + n * count : base + (n + 1) * count]
                outer[n, theirs] = swapped[pl.ds(low_at + n * count, count)]
            outer[3 + n, mine] = high[base + n * count : base + (n + 1) * count]
            outer[3 + n, theirs] = swapped[pl.ds(high_at + n * count, count)]
    else:
        for n in range(4):
            if n < 3:
                outer[n] = low[base + n * count : base + (n + 1) * count]
            outer[3 + n] = high[base + n * count : base + (n + 1) * count]
    clear_ends(outer.at[0:3], outer.at[3:7])

    def coefs(x, row):
        if x < 0:
            return [outer[n, here(row)] for n in range(3)]
        if x > last:
            return [outer[3 + n, here(row)] for n in range(3)]
        return [coef[n, x, here(row)] for n in range(3)]

    raw = [{c: Plane(state, c, x) for c in range(9)} for x in range(width)]
    old = [{c: Plane(st, c, x) for c in range(9)} for x in range(width)]
    one = own_planes(st, end)
    two = [{c: Plane(w, c, x) for c in range(9)} for x in range(width)]
    high_one = {c: Plane(high_v, c) for c in VEL}
    d_low_s, d_high_s, d_high_s_two = ({c: Plane(d_s, k, c - XX) for c in STRESS} for k in range(3))
    d_high_v, d_far_v, d_low_v = ({c: Plane(d_v, k, c) for c in VEL} for k in range(3))
    part_v, part_low, d_high_v_two, part_high = (
        {c: Plane(parts, k, n) for n, c in enumerate(names)}
        for k, names in enumerate((VEL, SIDE, VEL, VEL))
    )

    for row in chunks(size_y):
        cb, cb_high = coefs(0, row)[0], coefs(last + 1, row)[0]
        for n, (comp, c) in enumerate(zip(VEL, SIDE)):
            at = slice(n * size_y + row, n * size_y + row + ROWS)
            one[0][comp].set(row, old[0][comp].at(row, ROWS) - cb * low[at])
            delta = -cb_high * raw[last][c].at(row, ROWS)
            d_high_v[comp].set(row, delta)
            high_one[comp].set(row, high[at] + delta)
    for row in chunks(size_y):
        c = cells[here(row), :]
        _, cl, cm = coefs(0, row)
        for comp, term in stress_rate(strain(one[0], one[1], row, ROWS), cl, cm).items():
            one[0][comp].set(row, c * raw[0][comp].at(row, ROWS) + term)
        _, cl, cm = coefs(last, row)
        terms = beyond([high_one[comp].at(row, ROWS) for comp in VEL], cl, cm)
        for comp in STRESS:
            value = old[last][comp].at(row, ROWS)
            one[last][comp].set(row, value + terms[comp] if comp in terms else value)
        _, cl, cm = coefs(-1, row)
        for comp, term in beyond([one[0][comp].at(row, ROWS) for comp in VEL], cl, cm).items():
            d_low_s[comp].set(row, term)
        _, cl, cm = coefs(last + 1, row)
        for comp, term in stress_rate(strain(d_high_v, None, row, ROWS), cl, cm).items():
            d_high_s[comp].set(row, term)

    for row in chunks(size_y):
        for x in range(width):
            cb = coefs(x, row)[0]
            terms = divergence(one[x], one[x - 1] if x else d_low_s, row, ROWS)
            for comp, term in zip(VEL, terms):
                value = one[x][comp].at(row, ROWS) + cb * term
                if comp == VZ:
                    value = value + push[1, x, here(row)]
                (two[x] if x else part_v)[comp].set(row, value)
        cb = coefs(last + 1, row)[0]
        for comp, term in zip(VEL, divergence(d_high_s, one[last], row, ROWS)):
            d_high_v_two[comp].set(row, d_high_v[comp].at(row, ROWS) + cb * term)
        cb = outer[6, here(row)]
        for comp, c in zip(VEL, SIDE):
            d_far_v[comp].set(row, -cb * d_high_s[c].at(row, ROWS))
        cb = coefs(-1, row)[0]
        terms = divergence(d_low_s, None, row, ROWS, (XX, YY, ZZ, XY, XZ))
        for comp, term in zip(VEL, terms):
            d_low_v[comp].set(row, cb * term)
    for row in chunks(size_y):
        for x in range(1, width):
            _, cl, cm = coefs(x, row)
            after = two[x + 1] if x < last else None
            for comp, term in stress_rate(strain(two[x], after, row, ROWS), cl, cm).items():
                two[x][comp].set(row, one[x][comp].at(row, ROWS) + term)
        _, cl, cm = coefs(-1, row)
        rate = stress_rate(strain(d_low_v, None, row, ROWS, SIDE), cl, cm, SIDE)
        for comp, term in rate.items():
            part_low[comp].set(row, d_low_s[comp].at(row, ROWS) + term)
        _, cl, cm = coefs(last + 1, row)
        for comp, term in stress_rate(strain(d_high_v_two, d_far_v, row, ROWS), cl, cm).items():
            d_high_s_two[comp].set(row, d_high_s[comp].at(row, ROWS) + term)
    for row in chunks(size_y):
        cb = coefs(last + 1, row)[0]
        for comp, term in zip(VEL, divergence(d_high_s_two, None, row, ROWS)):
            part_high[comp].set(row, d_high_v_two[comp].at(row, ROWS) + cb * term)
        for x in range(2, last):
            cb = coefs(x, row)[0]
            for comp, term in zip(VEL, divergence(two[x], two[x - 1], row, ROWS)):
                value = two[x][comp].at(row, ROWS) + cb * term
                if comp == VZ:
                    value = value + push[2, x, here(row)]
                third[comp, x, here(row)] = value
    for row in chunks(size_y):
        for x in range(width):
            inner = 1 <= x < last
            v, t = [one[x]], [one[x]] + [two[x]] * inner
            if x:
                v.append(two[x])
            if 2 <= x < last:
                v.append({c: Plane(third, c, x) for c in VEL})
            moved = {c: add([k[c].at(row, ROWS) for k in v]) for c in VEL}
            moved |= {c: add([k[c].at(row, ROWS) for k in t]) for c in STRESS}
            for n, value in enumerate(imaged(moved, forward, x, row)):
                known[n, x, here(row)] = value
    if groups != 2:
        return

    (classes,) = classes
    rows_held = weights.shape[1]
    own = rows_held - BY
    first = pl.multiple_of(me * BY, BY)
    for j in range(own // BY):
        classes[pl.ds(first + j * BY, BY), :] = class_tile(orientation, j, weights.shape[2])
    classes[pl.ds(pl.multiple_of((1 - me) * own, BY), BY), :] = swapped[8 * count :, :]
    klass = classes[...]
    for column in range(3):
        table = jnp.full(klass.shape, weight_table[3][column], jnp.float32)
        for k in range(3):
            table = jnp.where(klass == k, weight_table[k][column], table)
        weights[column] = smooth_rate * table


def far_kernel(groups, *refs):
    by_pair, by_next, st, end, w, third, outer, parts, known, coef, push, forward, final, *refs = refs
    *images, low, high, edge, low_s, high_v, image = refs
    width, size_y = st.shape[1], st.shape[2]
    last = width - 1
    take_in(by_pair, by_next, low, high)

    def coefs(x, row):
        if x < 0:
            return [outer[n, here(row)] for n in range(3)]
        if x > last:
            return [outer[3 + n, here(row)] for n in range(3)]
        return [coef[n, x, here(row)] for n in range(3)]

    one = own_planes(st, end)
    part = [{c: Plane(w, c, x) for c in range(9)} for x in range(width)]
    two = [dict(p) for p in part]
    for c in range(9):
        two[0][c] = Plane(edge, 0, c)
        if c >= XX:
            two[last][c] = Plane(edge, 1, c)
    three = [{c: Plane(final, c, x) for c in range(9)} for x in range(width)]
    part_v, part_low, d_high_v_two, part_high = (
        {c: Plane(parts, k, n) for n, c in enumerate(names)}
        for k, names in enumerate((VEL, SIDE, VEL, VEL))
    )
    low_two = {c: Plane(low_s, n) for n, c in enumerate(SIDE)}
    high_three = {c: Plane(high_v, c) for c in VEL}

    for row in chunks(size_y):
        cb = coefs(0, row)[0]
        moved = []
        for n, comp in enumerate(VEL):
            moved.append(part_v[comp].at(row, ROWS) - cb * low[n, here(row)])
            two[0][comp].set(row, moved[n])
        _, cl, cm = coefs(-1, row)
        terms = beyond(moved, cl, cm)
        for n, comp in enumerate(SIDE):
            value = low[3 + n, here(row)] + part_low[comp].at(row, ROWS)
            low_two[comp].set(row, value + terms[comp])
        _, cl, cm = coefs(last, row)
        cb = coefs(last + 1, row)[0]
        moved = [high[n, here(row)] + d_high_v_two[n].at(row, ROWS) for n in VEL]
        terms = beyond(moved, cl, cm)
        values = {}
        for comp in STRESS:
            value = part[last][comp].at(row, ROWS)
            values[comp] = value + terms[comp] if comp in terms else value
            two[last][comp].set(row, values[comp])
        for n, comp in enumerate(SIDE):
            value = high[3 + n, here(row)] + part_high[n].at(row, ROWS)
            high_three[n].set(row, value - cb * values[comp])
    for row in chunks(size_y):
        _, cl, cm = coefs(0, row)
        for comp, term in stress_rate(strain(two[0], two[1], row, ROWS), cl, cm).items():
            two[0][comp].set(row, one[0][comp].at(row, ROWS) + term)

    for row in chunks(size_y):
        for x in range(width):
            if 2 <= x < last:
                for comp in VEL:
                    three[x][comp].set(row, third[comp, x, here(row)])
                continue
            cb = coefs(x, row)[0]
            terms = divergence(two[x], two[x - 1] if x else low_two, row, ROWS)
            for comp, term in zip(VEL, terms):
                value = two[x][comp].at(row, ROWS) + cb * term
                if comp == VZ:
                    value = value + push[2, x, here(row)]
                three[x][comp].set(row, value)
    for row in chunks(size_y):
        for x in range(width):
            _, cl, cm = coefs(x, row)
            after = three[x + 1] if x < last else high_three
            rate = stress_rate(strain(three[x], after, row, ROWS), cl, cm)
            moved = {}
            for comp in STRESS:
                before = two[x][comp].at(row, ROWS)
                value = before + rate[comp]
                three[x][comp].set(row, value)
                moved[comp] = value if 1 <= x < last else before + value
            if not 2 <= x < last:
                for comp in VEL:
                    moved[comp] = three[x][comp].at(row, ROWS)
                    if not x:
                        moved[comp] = two[x][comp].at(row, ROWS) + moved[comp]
            for n, value in enumerate(imaged(moved, forward, x, row)):
                before = known[n, x, here(row)]
                image[n, x, here(row)] = before if value is None else before + value

    if groups != 2:
        images[0][...] = image[...]
        return
    give, keep = images
    me = lax.axis_index("shot")
    count = keep.shape[2]
    mine = pl.ds(pl.multiple_of(me * (size_y - count), 8), count)
    theirs = pl.ds(pl.multiple_of((1 - me) * (size_y - count), 8), count)
    for n in range(3):
        for x in range(width):
            give[n, x] = image[n, x, theirs, :]
            keep[n, x] = image[n, x, mine, :]


def y_prev(f):
    return jnp.where(rows(f.shape) == 0, 0.0, pltpu.roll(f, 1, f.ndim - 2))


def y_next(f):
    size = f.shape[-2]
    return jnp.where(rows(f.shape) == size - 1, 0.0, pltpu.roll(f, size - 1, f.ndim - 2))


def sweep(g, before, after, weights):
    w_x, w_y, w_z = weights
    twice = 2.0 * g
    along_x = -twice
    for plane in (before, after):
        if plane is not None:
            along_x = along_x + plane
    along_y = y_next(g) + y_prev(g) - twice
    along_z = z_next(g) + z_prev(g) - twice
    return g + (w_x * along_x + w_y * along_y + w_z * along_z)


def edge_row(me, own):
    return jnp.where(me == 0, own, BY - 1)


def sum_kernel(scale, keep, received, weights, by_pair, by_next, grad, swept, up, down):
    width, count, size_z = grad.shape[1:]
    own = count - BY
    me = lax.axis_index("shot")
    first = pl.multiple_of(me * BY, BY)
    mine = pl.ds(first, own)
    edge = pl.ds(edge_row(me, own), 1)
    last = width - 1
    w = [weights[k] for k in range(3)]
    for to in (up, down):
        to[6 * own :, :] = jnp.zeros((BY, size_z), jnp.float32)
        for j in range(own // BY):
            row = weights[0, pl.ds(pl.multiple_of(first + j * BY, BY), BY), :][0:1]
            to[6 * own + 3 + j : 6 * own + 4 + j, :] = row
    for n in range(3):
        for x in range(width):
            grad[n, x] = (keep[n, x] + received[n, x]) * scale
        swept[n, 0] = sweep(grad[n, 0], None, grad[n, 1], w)
        swept[n, 1] = sweep(grad[n, last], grad[n, last - 1], None, w)
        for to, x, side in ((up, last, 1), (down, 0, 0)):
            to[2 * n * own : (2 * n + 1) * own, :] = grad[n, x, mine, :]
            to[(2 * n + 1) * own : (2 * n + 2) * own, :] = swept[n, side, mine, :]
            to[6 * own + n : 6 * own + n + 1, :] = grad[n, x, edge, :]
    hand_out(by_pair, by_next, up, down)


def inner_kernel(grad, swept, weights, full, half):
    width = grad.shape[1]
    last = width - 1
    w = [weights[k] for k in range(3)]
    for n in range(3):
        full[n, 0] = swept[n, 0]
        full[n, last] = swept[n, 1]
        for x in range(1, last):
            full[n, x] = sweep(grad[n, x], grad[n, x - 1], grad[n, x + 1], w)
        for x in range(1, last):
            half[n, x - 1] = sweep(
                full[n, x],
                full[n, x - 1] if x > 1 else None,
                full[n, x + 1] if x < last - 1 else None,
                w,
            )


def side_kernel(near, *refs):
    got, *refs = refs
    if not near:
        _, *refs = refs
    grad, full, half, weights, out, beside, result, sems = refs
    width, count, size_z = grad.shape[1:]
    own = count - BY
    me = lax.axis_index("shot")
    first = pl.multiple_of(me * BY, BY)
    mine = pl.ds(first, own)
    edge = pl.ds(edge_row(me, own), 1)
    upper = is_even() if near else jnp.logical_not(is_even())
    end = jnp.where(upper, width - 1, 0)
    inner = jnp.where(upper, width - 2, 1)
    beside[...] = jnp.zeros(beside.shape, jnp.float32)
    for n in range(3):
        beside[n, mine, :] = got[2 * n * own : (2 * n + 1) * own, :]
        beside[n, edge, :] = got[6 * own + n : 6 * own + n + 1, :]
        beside[3 + n, mine, :] = got[(2 * n + 1) * own : (2 * n + 2) * own, :]
    for j in range(own // BY):
        row = got[6 * own + 3 + j : 6 * own + 4 + j, :]
        to = pl.ds(pl.multiple_of(first + j * BY, BY), BY)
        beside[6, to, :] = jnp.broadcast_to(row, (BY, size_z))
    @pl.when(jnp.where(upper, no_neighbour(True), no_neighbour(False)))
    def _():
        beside[...] = jnp.zeros(beside.shape, jnp.float32)

    w = [weights[k] for k in range(3)]
    for n in range(3):
        value = full[n, end] + w[0] * beside[n]
        outer = beside[3 + n] + beside[6] * grad[n, end]
        result[n, 0] = sweep(value, outer, full[n, inner], w)
        result[n, 1] = half[n, inner - 1] + w[0] * value
    copies = [
        pltpu.make_async_copy(result.at[:, k, mine, :], out.at[:, x], sems.at[k])
        for k, x in enumerate((end, inner))
    ]
    for copy in copies:
        copy.start()
    for copy in copies:
        copy.wait()


def extended(block, sides, width):
    for axis, dim in sides:
        count = lax.axis_size(axis)
        forward = [(i, i + 1) for i in range(count - 1)]
        backward = [(target, source) for source, target in forward]
        low = lax.ppermute(
            lax.slice_in_dim(block, block.shape[dim] - width, None, axis=dim), axis, forward
        )
        high = lax.ppermute(lax.slice_in_dim(block, 0, width, axis=dim), axis, backward)
        block = jnp.concatenate([low, block, high], axis=dim)
    return block


def smooth_anywhere(image, orientation):
    groups = lax.axis_size("shot")
    owned = image.shape[2] // groups
    total = lax.psum(image, "shot")
    grad = lax.dynamic_slice_in_dim(total, lax.axis_index("shot") * owned, owned, 2)
    grad = grad * (STEPS * groups) ** (-0.5)
    weights = []
    for column in range(3):
        table = jnp.zeros(orientation.shape, jnp.float32)
        for klass in range(4):
            table = table + (orientation == klass).astype(jnp.float32) * weight_table[klass][column]
        table = jnp.repeat(jnp.repeat(table, image.shape[1], 0), BY, 1)
        weights.append(jnp.repeat(table, BZ, 2))
    for _ in range(SWEEPS):
        padded = extended(grad, (("shot", 2), ("tile", 1)), 1)
        padded = jnp.pad(padded, ((0, 0), (0, 0), (0, 0), (1, 1)))
        center = padded[:, 1:-1, 1:-1, 1:-1]
        lap_x = padded[:, 2:, 1:-1, 1:-1] + padded[:, :-2, 1:-1, 1:-1] - 2.0 * center
        lap_y = padded[:, 1:-1, 2:, 1:-1] + padded[:, 1:-1, :-2, 1:-1] - 2.0 * center
        lap_z = padded[:, 1:-1, 1:-1, 2:] + padded[:, 1:-1, 1:-1, :-2] - 2.0 * center
        grad = grad + smooth_rate * (weights[0] * lap_x + weights[1] * lap_y + weights[2] * lap_z)
    return grad


def both_ways(by_pair, by_next):
    count, groups = lax.axis_size("tile"), lax.axis_size("shot")
    out = []
    for array, start in ((by_pair, 0), (by_next, 1)):
        to = {}
        for i in range(start, count - 1, 2):
            to[i], to[i + 1] = i + 1, i
        pairs = [
            (shot * count + i, shot * count + to[i] if i in to else (shot + 1) % groups * count + i)
            for shot in range(groups)
            for i in range(count)
        ]
        out.append(lax.ppermute(array, ("shot", "tile"), pairs))
    return out


def f32(*shape):
    return jax.ShapeDtypeStruct(shape, jnp.float32)


def in_hbm(array):
    return pltpu.with_memory_space_constraint(array, pltpu.HBM)


def call(kernel, outs, args, scratch, scalars=(), space=VMEM, out_space=VMEM, held=None):
    specs = [SMEM if n in scalars else HBM if n == held else space for n in range(len(args))]
    return pl.pallas_call(
        kernel,
        out_shape=outs,
        in_specs=specs,
        out_specs=jax.tree.map(lambda _: out_space, outs),
        scratch_shapes=[
            pltpu.VMEM(shape, jnp.float32) if isinstance(shape, tuple) else shape
            for shape in scratch
        ],
        input_output_aliases={} if held is None else {held: 0},
        compiler_params=pltpu.CompilerParams(vmem_limit_bytes=24 * 1024 * 1024),
    )(*args)


def local(
    adjoint_state,
    adjoint_source,
    forward_field,
    lame_first,
    shear_modulus,
    buoyancy,
    active_blocks,
    orientation,
):
    width, size_y, size_z = lame_first.shape
    plane = (size_y, size_z)
    groups = lax.axis_size("shot")
    state, source, forward = adjoint_state[0], adjoint_source[0], forward_field[0]
    active = jnp.swapaxes(active_blocks, 1, 2)
    grid = f32(9, width, *plane)
    count = size_y // 2 if groups == 2 else size_y
    early = (3 * size_y + 4 * count, size_z)
    by_pair, by_next, cells, tile = call(
        functools.partial(early_kernel, groups),
        [f32(*early), f32(*early), f32(*plane), f32(BY, size_z)],
        [
            in_hbm(a)
            for a in (active, orientation, state, source, lame_first, shear_modulus, buoyancy)
        ],
        [
            early,
            early,
            (9, *plane),
            pltpu.VMEM(plane, source.dtype),
            (7, *plane),
            pltpu.SMEM(active.shape, jnp.int32),
            pltpu.SMEM(orientation.shape, jnp.int32),
            pltpu.SemaphoreType.DMA((14,)),
        ],
        space=HBM,
    )
    by_pair, by_next = both_ways(by_pair, by_next)
    late_pair, late_next, st, push, coef = call(
        late_kernel,
        [f32(6, *plane), f32(6, *plane), grid, f32(STEPS, width, *plane), f32(3, width, *plane)],
        [*(in_hbm(a) for a in (state, source, buoyancy, lame_first, shear_modulus)), cells],
        [(3, 3, *plane), (6, *plane), (6, *plane), (6, *plane)],
    )
    late_pair, late_next = both_ways(late_pair, late_next)
    args, outs, scalars = [by_pair, by_next], [], ()
    scratch = [early, early, (3, *plane), (3, 6, *plane), (3, 3, *plane)]
    owned = size_y // groups
    held = owned + BY
    if groups == 2:
        swapped = jnp.concatenate([by_pair[3 * size_y :], by_next[3 * size_y :], tile])
        swapped = lax.ppermute(swapped, "shot", [(0, 1), (1, 0)])
        args += [swapped, orientation]
        outs = [f32(3, held, size_z)]
        scratch += [(held, size_z)]
        scalars = (3,)
    three = f32(3, width, *plane)
    end, w, third, outer, parts, known, *weights = call(
        functools.partial(near_kernel, groups),
        [f32(2, 9, *plane), grid, three, f32(7, *plane), f32(4, 3, *plane), three, *outs],
        [*args, state, st, coef, cells, push, forward],
        scratch,
        scalars,
    )
    block = (3, width, held, size_z)
    images = [f32(*block), f32(*block)] if groups == 2 else [f32(3, width, *plane)]
    final, *images = call(
        functools.partial(far_kernel, groups),
        [pltpu.VMEM(grid.shape, grid.dtype), *images],
        [late_pair, late_next, st, end, w, third, outer, parts, known, coef, push, forward],
        [(6, *plane), (6, *plane), (2, 9, *plane), (3, *plane), (3, *plane), (3, width, *plane)],
    )
    if groups != 2:
        return final[None], smooth_anywhere(images[0], orientation)
    give, keep = images
    (weights,) = weights
    received = lax.ppermute(give, "shot", [(0, 1), (1, 0)])
    message = (6 * owned + BY, size_z)
    by_pair, by_next, grad, swept = call(
        functools.partial(sum_kernel, (STEPS * groups) ** (-0.5)),
        [f32(*message), f32(*message), f32(*block), f32(3, 2, held, size_z)],
        (keep, received, weights),
        [message, message],
    )
    by_pair, by_next = both_ways(by_pair, by_next)
    full, half = call(
        inner_kernel,
        [f32(*block), f32(3, width - 2, held, size_z)],
        (grad, swept, weights),
        [],
    )
    gradient = f32(3, width, owned, size_z)
    scratch = [(7, held, size_z), (3, 2, held, size_z), pltpu.SemaphoreType.DMA((2,))]
    rest = (grad, full, half, weights)
    gradient = call(
        functools.partial(side_kernel, True), gradient, (by_pair, *rest), scratch, out_space=HBM
    )
    gradient = call(
        functools.partial(side_kernel, False),
        f32(*gradient.shape),
        (by_next, gradient, *rest),
        scratch,
        out_space=HBM,
        held=1,
    )
    return final[None], gradient


def solution(mesh):
    return jax.shard_map(
        local,
        mesh=mesh,
        in_specs=(
            P("shot", None, "tile", None, None),
            P("shot", None, "tile", None, None),
            P("shot", None, "tile", None, None),
            P("tile", None, None),
            P("tile", None, None),
            P("tile", None, None),
            P("tile", None, None),
            P("tile", "shot", None),
        ),
        out_specs=(P("shot", None, "tile", None, None), P(None, "tile", "shot", None)),
        check_vma=False,
    )
```

```python
import functools

import jax
import jax.numpy as jnp
from jax import lax
from jax.experimental import pallas as pl
from jax.experimental.pallas import tpu as pltpu
from jax.sharding import PartitionSpec as P

BY = 8
BZ = 32
STEPS = 3
SWEEPS = 2

time_step = 0.25
smooth_rate = 0.1
weight_table = ((1.0, 1.0, 0.25), (0.25, 1.0, 1.0), (1.0, 0.25, 1.0), (0.6, 0.6, 0.6))

VX, VY, VZ, XX, YY, ZZ, XY, XZ, YZ = range(9)
VEL = (VX, VY, VZ)
SIDE = (XX, XY, XZ)
STRESS = (XX, YY, ZZ, XY, XZ, YZ)
ROWS = 32
VMEM = pl.BlockSpec(memory_space=pltpu.VMEM)
SMEM = pl.BlockSpec(memory_space=pltpu.SMEM)
HBM = pl.BlockSpec(memory_space=pltpu.HBM)


def lanes(shape):
    return lax.broadcasted_iota(jnp.int32, shape, len(shape) - 1)


def rows(shape):
    return lax.broadcasted_iota(jnp.int32, shape, len(shape) - 2)


def z_prev(f):
    return jnp.where(lanes(f.shape) == 0, 0.0, pltpu.roll(f, 1, f.ndim - 1))


def z_next(f):
    size = f.shape[-1]
    return jnp.where(lanes(f.shape) == size - 1, 0.0, pltpu.roll(f, size - 1, f.ndim - 1))


class Plane:
    def __init__(self, ref, *index):
        self.ref, self.index = ref, index
        self.size = ref.shape[len(index)]

    def at(self, row, count):
        return self.ref[self.index + (slice(row, row + count),)]

    def prev(self, row, count):
        if row:
            return self.at(row - 1, count)
        edge = pltpu.roll(self.at(0, 8), 1, 0)
        edge = jnp.where(rows(edge.shape) == 0, 0.0, edge)
        return jnp.concatenate([edge, self.at(7, count - 8)], 0)

    def next(self, row, count):
        if row + count < self.size:
            return self.at(row + 1, count)
        edge = pltpu.roll(self.at(self.size - 8, 8), 7, 0)
        edge = jnp.where(rows(edge.shape) == 7, 0.0, edge)
        return jnp.concatenate([self.at(row + 1, count - 8), edge], 0)

    def set(self, row, value):
        self.ref[self.index + (slice(row, row + value.shape[0]),)] = value


def planes(ref, comps, *index):
    return {c: Plane(ref, n, *index) for n, c in enumerate(comps)}


def divergence(s, before, row, count, have=(XX, YY, ZZ, XY, XZ, YZ)):
    def along_x(c):
        here = s[c].at(row, count)
        return here - before[c].at(row, count) if before is not None else here

    def along_y(c):
        return s[c].at(row, count) - s[c].prev(row, count)

    def along_z(c):
        here = s[c].at(row, count)
        return here - z_prev(here)

    out = []
    for c_x, c_y, c_z in ((XX, XY, XZ), (XY, YY, YZ), (XZ, YZ, ZZ)):
        terms = along_x(c_x)
        if c_y in have:
            terms = terms + along_y(c_y)
        if c_z in have:
            terms = terms + along_z(c_z)
        out.append(terms)
    return out


def strain(v, after, row, count, want=(XX, YY, ZZ, XY, XZ, YZ)):
    x, y, z = (v[c].at(row, count) for c in (VX, VY, VZ))
    if after is None:
        d_x = [-x, -y, -z]
    else:
        d_x = [after[c].at(row, count) - f for c, f in ((VX, x), (VY, y), (VZ, z))]
    out = {XX: d_x[0], YY: v[VY].next(row, count) - y, ZZ: z_next(z) - z}
    out["div"] = out[XX] + out[YY] + out[ZZ]
    if XY in want:
        out[XY] = v[VX].next(row, count) - x + d_x[1]
    if XZ in want:
        out[XZ] = z_next(x) - x + d_x[2]
    if YZ in want:
        out[YZ] = z_next(y) - y + (v[VZ].next(row, count) - z)
    return out


def stress_rate(e, lame, shear, want=(XX, YY, ZZ, XY, XZ, YZ)):
    spread = lame * e["div"]
    return {
        c: spread + 2.0 * shear * e[c] if c in (XX, YY, ZZ) else shear * e[c] for c in want
    }


def cell_plane(active, out):
    shape = (BY, out.shape[1])
    for j in range(out.shape[0] // BY):
        row = jnp.full(shape, active[0, 0, j].astype(jnp.float32))
        for k in range(1, out.shape[1] // BZ):
            row = jnp.where(lanes(shape) >= k * BZ, active[0, k, j].astype(jnp.float32), row)
        out[j * BY : (j + 1) * BY, :] = row


def chunks(size):
    return range(0, size, ROWS)


def is_even():
    return lax.rem(lax.axis_index("tile"), 2) == 0


def hand_out(by_pair, by_next, up, down):
    even = is_even()

    @pl.when(even)
    def _():
        by_pair[...] = up[...]
        by_next[...] = down[...]

    @pl.when(jnp.logical_not(even))
    def _():
        by_pair[...] = down[...]
        by_next[...] = up[...]


def take_in(by_pair, by_next, low, high):
    even = is_even()

    @pl.when(even)
    def _():
        low[...] = by_next[...]
        high[...] = by_pair[...]

    @pl.when(jnp.logical_not(even))
    def _():
        low[...] = by_pair[...]
        high[...] = by_next[...]

    clear_ends(low, high)


def no_neighbour(upper):
    return lax.axis_index("tile") == (lax.axis_size("tile") - 1 if upper else 0)


def clear_ends(low, high):
    for upper, ref in ((False, low), (True, high)):

        @pl.when(no_neighbour(upper))
        def _(ref=ref):
            ref[...] = jnp.zeros(ref.shape, jnp.float32)


def class_tile(orientation, j, size_z):
    shape = (BY, size_z)
    out = jnp.full(shape, orientation[0, j, 0].astype(jnp.float32))
    for k in range(1, size_z // BZ):
        out = jnp.where(lanes(shape) >= k * BZ, orientation[0, j, k].astype(jnp.float32), out)
    return out


def here(row):
    return slice(row, row + ROWS)


def early_kernel(
    groups,
    active_hbm,
    orientation_hbm,
    state_hbm,
    source_hbm,
    lame_hbm,
    shear_hbm,
    buoyancy_hbm,
    by_pair,
    by_next,
    cells,
    tile,
    up,
    down,
    first,
    push,
    params,
    active,
    orientation,
    sems,
):
    size_y, size_z = cells.shape
    last = state_hbm.shape[1] - 1
    planes_at = (0, 0, 0, 1, last, last, last)
    arrays = (buoyancy_hbm, lame_hbm, shear_hbm)
    ends = [(active_hbm, active), (orientation_hbm, orientation)]
    ends += [(arrays[n % 3].at[x], params.at[n]) for n, x in enumerate(planes_at)]
    ends += [(state_hbm.at[:, 0], first), (source_hbm.at[0, 0], push)]
    ends += [
        (state_hbm.at[c, last], up.at[n * size_y : (n + 1) * size_y]) for n, c in enumerate(SIDE)
    ]
    copies = [pltpu.make_async_copy(*pair, sems.at[n]) for n, pair in enumerate(ends)]
    for copy in copies:
        copy.start()
    for copy in copies[:2]:
        copy.wait()
    cell_plane(active, cells)
    me = lax.axis_index("shot") if groups == 2 else 0
    last_block = orientation.shape[1] - 1
    tile[...] = class_tile(orientation, jnp.where(me == 0, last_block, 0), size_z)
    for copy in copies[2:9]:
        copy.wait()
    for row in chunks(size_y):
        c = time_step * cells[here(row), :]
        for n in range(7):
            params[n, here(row)] = c * params[n, here(row)]
    count = (up.shape[0] - 3 * size_y) // 4
    mine = pl.ds(pl.multiple_of(me * count, 8), count) if groups == 2 else slice(0, count)
    for n in range(4):
        to = slice(3 * size_y + n * count, 3 * size_y + (n + 1) * count)
        down[to] = params[n, mine]
        up[to] = params[(6, 4, 5, 6)[n], mine]
    for copy in copies[9:]:
        copy.wait()
    raw = {c: Plane(first, c) for c in range(9)}
    for row in chunks(size_y):
        c, cb = cells[here(row), :], params[0, here(row)]
        for n, term in enumerate(divergence(raw, None, row, ROWS)):
            value = c * raw[n].at(row, ROWS) + cb * term
            if n == VZ:
                value = value + time_step * c * push[here(row)].astype(jnp.float32)
            down[n * size_y + row : n * size_y + row + ROWS] = value
    hand_out(by_pair, by_next, up, down)


def late_kernel(
    state, source, buoyancy, lame, shear, cells, by_pair, by_next, st, push, coef, v2, s2, up, down
):
    width, size_y = state.shape[1], state.shape[2]
    last = width - 1
    for row in chunks(size_y):
        c = time_step * cells[here(row), :]
        for step in range(STEPS):
            for x in range(width):
                push[step, x, here(row)] = c * source[step, x, here(row)].astype(jnp.float32)
        for n, param in enumerate((buoyancy, lame, shear)):
            for x in range(width):
                coef[n, x, here(row)] = c * param[x, here(row)]

    def coefs(x, row):
        return [coef[n, x, here(row)] for n in range(3)]

    raw = [{c: Plane(state, c, x) for c in range(9)} for x in range(width)]
    one = [{c: Plane(st, c, x) for c in range(9)} for x in range(width)]
    two = {x: {c: Plane(v2, n, c) for c in VEL} for n, x in enumerate((0, 1, last))}
    for x in range(width):
        for row in chunks(size_y):
            c = cells[here(row), :]
            cb = coefs(x, row)[0]
            terms = divergence(raw[x], raw[x - 1] if x else None, row, ROWS)
            for comp, term in zip(VEL, terms):
                value = c * raw[x][comp].at(row, ROWS) + cb * term
                if comp == VZ:
                    value = value + push[0, x, here(row)]
                one[x][comp].set(row, value)
    for x in range(width):
        for row in chunks(size_y):
            c = cells[here(row), :]
            _, cl, cm = coefs(x, row)
            rate = stress_rate(strain(one[x], one[x + 1] if x < last else None, row, ROWS), cl, cm)
            for comp, term in rate.items():
                one[x][comp].set(row, c * raw[x][comp].at(row, ROWS) + term)
    for x in two:
        for row in chunks(size_y):
            cb = coefs(x, row)[0]
            terms = divergence(one[x], one[x - 1] if x else None, row, ROWS)
            for comp, term in zip(VEL, terms):
                value = one[x][comp].at(row, ROWS) + cb * term
                if comp == VZ:
                    value = value + push[1, x, here(row)]
                two[x][comp].set(row, value)
    stress = {c: Plane(s2, c - XX) for c in STRESS}
    for row in chunks(size_y):
        _, cl, cm = coefs(0, row)
        rate = stress_rate(strain(two[0], two[1], row, ROWS), cl, cm)
        for comp, term in rate.items():
            stress[comp].set(row, one[0][comp].at(row, ROWS) + term)
        _, cl, cm = coefs(last, row)
        rate = stress_rate(strain(two[last], None, row, ROWS, SIDE), cl, cm, SIDE)
        for n, comp in enumerate(SIDE):
            value = one[last][comp].at(row, ROWS)
            up[n, here(row)] = value
            up[3 + n, here(row)] = value + rate[comp]
    for row in chunks(size_y):
        cb = coefs(0, row)[0]
        terms = divergence(stress, None, row, ROWS)
        for comp, term in zip(VEL, terms):
            before = two[0][comp].at(row, ROWS)
            value = before + cb * term
            if comp == VZ:
                value = value + push[2, 0, here(row)]
            down[comp, here(row)] = before
            down[3 + comp, here(row)] = value
    hand_out(by_pair, by_next, up, down)


def beyond(v, cl, cm):
    spread = cl * v[0]
    return {XX: spread + 2.0 * cm * v[0], YY: spread, ZZ: spread, XY: cm * v[1], XZ: cm * v[2]}


def add(terms):
    return functools.reduce(jnp.add, terms)


def imaged(moved, forward, x, row):
    f = [forward[n, x, here(row)].astype(jnp.float32) for n in range(9)]
    trace = (moved[XX] + moved[YY] + moved[ZZ]) * (f[0] + f[1] + f[2])
    shear = add([moved[comp] * f[n] for n, comp in enumerate(STRESS)])
    density = add([moved[c] * f[6 + c] for c in VEL]) if VX in moved else None
    return trace, shear, density


def own_planes(st, end):
    width = st.shape[1]
    one = [{c: Plane(st, c, x) for c in range(9)} for x in range(width)]
    one[0] = {c: Plane(end, 0, c) for c in range(9)}
    one[-1] = {c: Plane(st, c, width - 1) if c in VEL else Plane(end, 1, c) for c in range(9)}
    return one


def near_kernel(groups, *refs):
    by_pair, by_next, *refs = refs
    if groups == 2:
        swapped, orientation, *refs = refs
    state, st, coef, cells, push, forward, end, w, third, outer, parts, known, *refs = refs
    if groups == 2:
        weights, *refs = refs
    low, high, high_v, d_s, d_v, *classes = refs
    width, size_y = st.shape[1], st.shape[2]
    last = width - 1
    take_in(by_pair, by_next, low, high)
    count = (low.shape[0] - 3 * size_y) // 4
    base = 3 * size_y
    if groups == 2:
        me = lax.axis_index("shot")
        mine = pl.ds(pl.multiple_of(me * count, 8), count)
        theirs = pl.ds(pl.multiple_of((1 - me) * count, 8), count)
        low_at = pl.multiple_of(jnp.where(is_even(), 4 * count, 0), 8)
        high_at = pl.multiple_of(jnp.where(is_even(), 0, 4 * count), 8)
        for n in range(4):
            if n < 3:
                outer[n, mine] = low[base + n * count : base + (n + 1) * count]
                outer[n, theirs] = swapped[pl.ds(low_at + n * count, count)]
            outer[3 + n, mine] = high[base + n * count : base + (n + 1) * count]
            outer[3 + n, theirs] = swapped[pl.ds(high_at + n * count, count)]
    else:
        for n in range(4):
            if n < 3:
                outer[n] = low[base + n * count : base + (n + 1) * count]
            outer[3 + n] = high[base + n * count : base + (n + 1) * count]
    clear_ends(outer.at[0:3], outer.at[3:7])

    def coefs(x, row):
        if x < 0:
            return [outer[n, here(row)] for n in range(3)]
        if x > last:
            return [outer[3 + n, here(row)] for n in range(3)]
        return [coef[n, x, here(row)] for n in range(3)]

    raw = [{c: Plane(state, c, x) for c in range(9)} for x in range(width)]
    old = [{c: Plane(st, c, x) for c in range(9)} for x in range(width)]
    one = own_planes(st, end)
    two = [{c: Plane(w, c, x) for c in range(9)} for x in range(width)]
    high_one = {c: Plane(high_v, c) for c in VEL}
    d_low_s, d_high_s, d_high_s_two = ({c: Plane(d_s, k, c - XX) for c in STRESS} for k in range(3))
    d_high_v, d_far_v, d_low_v = ({c: Plane(d_v, k, c) for c in VEL} for k in range(3))
    part_v, part_low, d_high_v_two, part_high = (
        {c: Plane(parts, k, n) for n, c in enumerate(names)}
        for k, names in enumerate((VEL, SIDE, VEL, VEL))
    )

    for row in chunks(size_y):
        cb, cb_high = coefs(0, row)[0], coefs(last + 1, row)[0]
        for n, (comp, c) in enumerate(zip(VEL, SIDE)):
            at = slice(n * size_y + row, n * size_y + row + ROWS)
            one[0][comp].set(row, old[0][comp].at(row, ROWS) - cb * low[at])
            delta = -cb_high * raw[last][c].at(row, ROWS)
            d_high_v[comp].set(row, delta)
            high_one[comp].set(row, high[at] + delta)
    for row in chunks(size_y):
        c = cells[here(row), :]
        _, cl, cm = coefs(0, row)
        for comp, term in stress_rate(strain(one[0], one[1], row, ROWS), cl, cm).items():
            one[0][comp].set(row, c * raw[0][comp].at(row, ROWS) + term)
        _, cl, cm = coefs(last, row)
        terms = beyond([high_one[comp].at(row, ROWS) for comp in VEL], cl, cm)
        for comp in STRESS:
            value = old[last][comp].at(row, ROWS)
            one[last][comp].set(row, value + terms[comp] if comp in terms else value)
        _, cl, cm = coefs(-1, row)
        for comp, term in beyond([one[0][comp].at(row, ROWS) for comp in VEL], cl, cm).items():
            d_low_s[comp].set(row, term)
        _, cl, cm = coefs(last + 1, row)
        for comp, term in stress_rate(strain(d_high_v, None, row, ROWS), cl, cm).items():
            d_high_s[comp].set(row, term)

    for row in chunks(size_y):
        for x in range(width):
            cb = coefs(x, row)[0]
            terms = divergence(one[x], one[x - 1] if x else d_low_s, row, ROWS)
            for comp, term in zip(VEL, terms):
                value = one[x][comp].at(row, ROWS) + cb * term
                if comp == VZ:
                    value = value + push[1, x, here(row)]
                (two[x] if x else part_v)[comp].set(row, value)
        cb = coefs(last + 1, row)[0]
        for comp, term in zip(VEL, divergence(d_high_s, one[last], row, ROWS)):
            d_high_v_two[comp].set(row, d_high_v[comp].at(row, ROWS) + cb * term)
        cb = outer[6, here(row)]
        for comp, c in zip(VEL, SIDE):
            d_far_v[comp].set(row, -cb * d_high_s[c].at(row, ROWS))
        cb = coefs(-1, row)[0]
        terms = divergence(d_low_s, None, row, ROWS, (XX, YY, ZZ, XY, XZ))
        for comp, term in zip(VEL, terms):
            d_low_v[comp].set(row, cb * term)
    for row in chunks(size_y):
        for x in range(1, width):
            _, cl, cm = coefs(x, row)
            after = two[x + 1] if x < last else None
            for comp, term in stress_rate(strain(two[x], after, row, ROWS), cl, cm).items():
                two[x][comp].set(row, one[x][comp].at(row, ROWS) + term)
        _, cl, cm = coefs(-1, row)
        rate = stress_rate(strain(d_low_v, None, row, ROWS, SIDE), cl, cm, SIDE)
        for comp, term in rate.items():
            part_low[comp].set(row, d_low_s[comp].at(row, ROWS) + term)
        _, cl, cm = coefs(last + 1, row)
        for comp, term in stress_rate(strain(d_high_v_two, d_far_v, row, ROWS), cl, cm).items():
            d_high_s_two[comp].set(row, d_high_s[comp].at(row, ROWS) + term)
    for row in chunks(size_y):
        cb = coefs(last + 1, row)[0]
        for comp, term in zip(VEL, divergence(d_high_s_two, None, row, ROWS)):
            part_high[comp].set(row, d_high_v_two[comp].at(row, ROWS) + cb * term)
        for x in range(2, last):
            cb = coefs(x, row)[0]
            for comp, term in zip(VEL, divergence(two[x], two[x - 1], row, ROWS)):
                value = two[x][comp].at(row, ROWS) + cb * term
                if comp == VZ:
                    value = value + push[2, x, here(row)]
                third[comp, x, here(row)] = value
    for row in chunks(size_y):
        for x in range(width):
            inner = 1 <= x < last
            v, t = [one[x]], [one[x]] + [two[x]] * inner
            if x:
                v.append(two[x])
            if 2 <= x < last:
                v.append({c: Plane(third, c, x) for c in VEL})
            moved = {c: add([k[c].at(row, ROWS) for k in v]) for c in VEL}
            moved |= {c: add([k[c].at(row, ROWS) for k in t]) for c in STRESS}
            for n, value in enumerate(imaged(moved, forward, x, row)):
                known[n, x, here(row)] = value
    if groups != 2:
        return

    (classes,) = classes
    rows_held = weights.shape[1]
    own = rows_held - BY
    first = pl.multiple_of(me * BY, BY)
    for j in range(own // BY):
        classes[pl.ds(first + j * BY, BY), :] = class_tile(orientation, j, weights.shape[2])
    classes[pl.ds(pl.multiple_of((1 - me) * own, BY), BY), :] = swapped[8 * count :, :]
    klass = classes[...]
    for column in range(3):
        table = jnp.full(klass.shape, weight_table[3][column], jnp.float32)
        for k in range(3):
            table = jnp.where(klass == k, weight_table[k][column], table)
        weights[column] = smooth_rate * table


def far_kernel(groups, *refs):
    by_next, by_pair, st, end, w, third, outer, parts, known, coef, push, forward, final, *refs = refs
    *images, low, high, edge, low_s, high_v, image = refs
    width, size_y = st.shape[1], st.shape[2]
    last = width - 1
    take_in(by_pair, by_next, low, high)

    def coefs(x, row):
        if x < 0:
            return [outer[n, here(row)] for n in range(3)]
        if x > last:
            return [outer[3 + n, here(row)] for n in range(3)]
        return [coef[n, x, here(row)] for n in range(3)]

    one = own_planes(st, end)
    part = [{c: Plane(w, c, x) for c in range(9)} for x in range(width)]
    two = [dict(p) for p in part]
    for c in range(9):
        two[0][c] = Plane(edge, 0, c)
        if c >= XX:
            two[last][c] = Plane(edge, 1, c)
    three = [{c: Plane(final, c, x) for c in range(9)} for x in range(width)]
    part_v, part_low, d_high_v_two, part_high = (
        {c: Plane(parts, k, n) for n, c in enumerate(names)}
        for k, names in enumerate((VEL, SIDE, VEL, VEL))
    )
    low_two = {c: Plane(low_s, n) for n, c in enumerate(SIDE)}
    high_three = {c: Plane(high_v, c) for c in VEL}

    for row in chunks(size_y):
        cb = coefs(0, row)[0]
        moved = []
        for n, comp in enumerate(VEL):
            moved.append(part_v[comp].at(row, ROWS) - cb * low[n, here(row)])
            two[0][comp].set(row, moved[n])
        _, cl, cm = coefs(-1, row)
        terms = beyond(moved, cl, cm)
        for n, comp in enumerate(SIDE):
            value = low[3 + n, here(row)] + part_low[comp].at(row, ROWS)
            low_two[comp].set(row, value + terms[comp])
        _, cl, cm = coefs(last, row)
        cb = coefs(last + 1, row)[0]
        moved = [high[n, here(row)] + d_high_v_two[n].at(row, ROWS) for n in VEL]
        terms = beyond(moved, cl, cm)
        values = {}
        for comp in STRESS:
            value = part[last][comp].at(row, ROWS)
            values[comp] = value + terms[comp] if comp in terms else value
            two[last][comp].set(row, values[comp])
        for n, comp in enumerate(SIDE):
            value = high[3 + n, here(row)] + part_high[n].at(row, ROWS)
            high_three[n].set(row, value - cb * values[comp])
    for row in chunks(size_y):
        _, cl, cm = coefs(0, row)
        for comp, term in stress_rate(strain(two[0], two[1], row, ROWS), cl, cm).items():
            two[0][comp].set(row, one[0][comp].at(row, ROWS) + term)

    for row in chunks(size_y):
        for x in range(width):
            if 2 <= x < last:
                for comp in VEL:
                    three[x][comp].set(row, third[comp, x, here(row)])
                continue
            cb = coefs(x, row)[0]
            terms = divergence(two[x], two[x - 1] if x else low_two, row, ROWS)
            for comp, term in zip(VEL, terms):
                value = two[x][comp].at(row, ROWS) + cb * term
                if comp == VZ:
                    value = value + push[2, x, here(row)]
                three[x][comp].set(row, value)
    for row in chunks(size_y):
        for x in range(width):
            _, cl, cm = coefs(x, row)
            after = three[x + 1] if x < last else high_three
            rate = stress_rate(strain(three[x], after, row, ROWS), cl, cm)
            moved = {}
            for comp in STRESS:
                before = two[x][comp].at(row, ROWS)
                value = before + rate[comp]
                three[x][comp].set(row, value)
                moved[comp] = value if 1 <= x < last else before + value
            if not 2 <= x < last:
                for comp in VEL:
                    moved[comp] = three[x][comp].at(row, ROWS)
                    if not x:
                        moved[comp] = two[x][comp].at(row, ROWS) + moved[comp]
            for n, value in enumerate(imaged(moved, forward, x, row)):
                before = known[n, x, here(row)]
                image[n, x, here(row)] = before if value is None else before + value

    if groups != 2:
        images[0][...] = image[...]
        return
    give, keep = images
    me = lax.axis_index("shot")
    count = keep.shape[2]
    mine = pl.ds(pl.multiple_of(me * (size_y - count), 8), count)
    theirs = pl.ds(pl.multiple_of((1 - me) * (size_y - count), 8), count)
    for n in range(3):
        for x in range(width):
            give[n, x] = image[n, x, theirs, :]
            keep[n, x] = image[n, x, mine, :]


def y_prev(f):
    return jnp.where(rows(f.shape) == 0, 0.0, pltpu.roll(f, 1, f.ndim - 2))


def y_next(f):
    size = f.shape[-2]
    return jnp.where(rows(f.shape) == size - 1, 0.0, pltpu.roll(f, size - 1, f.ndim - 2))


def sweep(g, before, after, weights):
    w_x, w_y, w_z = weights
    twice = 2.0 * g
    along_x = -twice
    for plane in (before, after):
        if plane is not None:
            along_x = along_x + plane
    along_y = y_next(g) + y_prev(g) - twice
    along_z = z_next(g) + z_prev(g) - twice
    return g + (w_x * along_x + w_y * along_y + w_z * along_z)


def edge_row(me, own):
    return jnp.where(me == 0, own, BY - 1)


def sum_kernel(scale, keep, received, weights, by_pair, by_next, grad, swept, up, down):
    width, count, size_z = grad.shape[1:]
    own = count - BY
    me = lax.axis_index("shot")
    first = pl.multiple_of(me * BY, BY)
    mine = pl.ds(first, own)
    edge = pl.ds(edge_row(me, own), 1)
    last = width - 1
    w = [weights[k] for k in range(3)]
    for to in (up, down):
        to[6 * own :, :] = jnp.zeros((BY, size_z), jnp.float32)
        for j in range(own // BY):
            row = weights[0, pl.ds(pl.multiple_of(first + j * BY, BY), BY), :][0:1]
            to[6 * own + 3 + j : 6 * own + 4 + j, :] = row
    for n in range(3):
        for x in range(width):
            grad[n, x] = (keep[n, x] + received[n, x]) * scale
        swept[n, 0] = sweep(grad[n, 0], None, grad[n, 1], w)
        swept[n, 1] = sweep(grad[n, last], grad[n, last - 1], None, w)
        for to, x, side in ((up, last, 1), (down, 0, 0)):
            to[2 * n * own : (2 * n + 1) * own, :] = grad[n, x, mine, :]
            to[(2 * n + 1) * own : (2 * n + 2) * own, :] = swept[n, side, mine, :]
            to[6 * own + n : 6 * own + n + 1, :] = grad[n, x, edge, :]
    hand_out(by_pair, by_next, up, down)


def inner_kernel(grad, swept, weights, full, half):
    width = grad.shape[1]
    last = width - 1
    w = [weights[k] for k in range(3)]
    for n in range(3):
        full[n, 0] = swept[n, 0]
        full[n, last] = swept[n, 1]
        for x in range(1, last):
            full[n, x] = sweep(grad[n, x], grad[n, x - 1], grad[n, x + 1], w)
        for x in range(1, last):
            half[n, x - 1] = sweep(
                full[n, x],
                full[n, x - 1] if x > 1 else None,
                full[n, x + 1] if x < last - 1 else None,
                w,
            )


def side_kernel(near, *refs):
    got, *refs = refs
    if not near:
        _, *refs = refs
    grad, full, half, weights, out, beside, result, sems = refs
    width, count, size_z = grad.shape[1:]
    own = count - BY
    me = lax.axis_index("shot")
    first = pl.multiple_of(me * BY, BY)
    mine = pl.ds(first, own)
    edge = pl.ds(edge_row(me, own), 1)
    upper = is_even() if near else jnp.logical_not(is_even())
    end = jnp.where(upper, width - 1, 0)
    inner = jnp.where(upper, width - 2, 1)
    beside[...] = jnp.zeros(beside.shape, jnp.float32)
    for n in range(3):
        beside[n, mine, :] = got[2 * n * own : (2 * n + 1) * own, :]
        beside[n, edge, :] = got[6 * own + n : 6 * own + n + 1, :]
        beside[3 + n, mine, :] = got[(2 * n + 1) * own : (2 * n + 2) * own, :]
    for j in range(own // BY):
        row = got[6 * own + 3 + j : 6 * own + 4 + j, :]
        to = pl.ds(pl.multiple_of(first + j * BY, BY), BY)
        beside[6, to, :] = jnp.broadcast_to(row, (BY, size_z))
    @pl.when(jnp.where(upper, no_neighbour(True), no_neighbour(False)))
    def _():
        beside[...] = jnp.zeros(beside.shape, jnp.float32)

    w = [weights[k] for k in range(3)]
    for n in range(3):
        value = full[n, end] + w[0] * beside[n]
        outer = beside[3 + n] + beside[6] * grad[n, end]
        result[n, 0] = sweep(value, outer, full[n, inner], w)
        result[n, 1] = half[n, inner - 1] + w[0] * value
    copies = [
        pltpu.make_async_copy(result.at[:, k, mine, :], out.at[:, x], sems.at[k])
        for k, x in enumerate((end, inner))
    ]
    for copy in copies:
        copy.start()
    for copy in copies:
        copy.wait()


def extended(block, sides, width):
    for axis, dim in sides:
        count = lax.axis_size(axis)
        forward = [(i, i + 1) for i in range(count - 1)]
        backward = [(target, source) for source, target in forward]
        low = lax.ppermute(
            lax.slice_in_dim(block, block.shape[dim] - width, None, axis=dim), axis, forward
        )
        high = lax.ppermute(lax.slice_in_dim(block, 0, width, axis=dim), axis, backward)
        block = jnp.concatenate([low, block, high], axis=dim)
    return block


def smooth_anywhere(image, orientation):
    groups = lax.axis_size("shot")
    owned = image.shape[2] // groups
    total = lax.psum(image, "shot")
    grad = lax.dynamic_slice_in_dim(total, lax.axis_index("shot") * owned, owned, 2)
    grad = grad * (STEPS * groups) ** (-0.5)
    weights = []
    for column in range(3):
        table = jnp.zeros(orientation.shape, jnp.float32)
        for klass in range(4):
            table = table + (orientation == klass).astype(jnp.float32) * weight_table[klass][column]
        table = jnp.repeat(jnp.repeat(table, image.shape[1], 0), BY, 1)
        weights.append(jnp.repeat(table, BZ, 2))
    for _ in range(SWEEPS):
        padded = extended(grad, (("shot", 2), ("tile", 1)), 1)
        padded = jnp.pad(padded, ((0, 0), (0, 0), (0, 0), (1, 1)))
        center = padded[:, 1:-1, 1:-1, 1:-1]
        lap_x = padded[:, 2:, 1:-1, 1:-1] + padded[:, :-2, 1:-1, 1:-1] - 2.0 * center
        lap_y = padded[:, 1:-1, 2:, 1:-1] + padded[:, 1:-1, :-2, 1:-1] - 2.0 * center
        lap_z = padded[:, 1:-1, 1:-1, 2:] + padded[:, 1:-1, 1:-1, :-2] - 2.0 * center
        grad = grad + smooth_rate * (weights[0] * lap_x + weights[1] * lap_y + weights[2] * lap_z)
    return grad


def both_ways(by_pair, by_next):
    count, groups = lax.axis_size("tile"), lax.axis_size("shot")
    out = []
    for array, start in ((by_pair, 0), (by_next, 1)):
        to = {}
        for i in range(start, count - 1, 2):
            to[i], to[i + 1] = i + 1, i
        pairs = [
            (shot * count + i, shot * count + to[i] if i in to else (shot + 1) % groups * count + i)
            for shot in range(groups)
            for i in range(count)
        ]
        out.append(lax.ppermute(array, ("shot", "tile"), pairs))
    return out


def f32(*shape):
    return jax.ShapeDtypeStruct(shape, jnp.float32)


def in_hbm(array):
    return pltpu.with_memory_space_constraint(array, pltpu.HBM)


def call(kernel, outs, args, scratch, scalars=(), space=VMEM, out_space=VMEM, held=None):
    specs = [SMEM if n in scalars else HBM if n == held else space for n in range(len(args))]
    return pl.pallas_call(
        kernel,
        out_shape=outs,
        in_specs=specs,
        out_specs=jax.tree.map(lambda _: out_space, outs),
        scratch_shapes=[
            pltpu.VMEM(shape, jnp.float32) if isinstance(shape, tuple) else shape
            for shape in scratch
        ],
        input_output_aliases={} if held is None else {held: 0},
        compiler_params=pltpu.CompilerParams(vmem_limit_bytes=24 * 1024 * 1024),
    )(*args)


def local(
    adjoint_state,
    adjoint_source,
    forward_field,
    lame_first,
    shear_modulus,
    buoyancy,
    active_blocks,
    orientation,
):
    width, size_y, size_z = lame_first.shape
    plane = (size_y, size_z)
    groups = lax.axis_size("shot")
    state, source, forward = adjoint_state[0], adjoint_source[0], forward_field[0]
    active = jnp.swapaxes(active_blocks, 1, 2)
    grid = f32(9, width, *plane)
    count = size_y // 2 if groups == 2 else size_y
    early = (3 * size_y + 4 * count, size_z)
    by_pair, by_next, cells, tile = call(
        functools.partial(early_kernel, groups),
        [f32(*early), f32(*early), f32(*plane), f32(BY, size_z)],
        [
            in_hbm(a)
            for a in (active, orientation, state, source, lame_first, shear_modulus, buoyancy)
        ],
        [
            early,
            early,
            (9, *plane),
            pltpu.VMEM(plane, source.dtype),
            (7, *plane),
            pltpu.SMEM(active.shape, jnp.int32),
            pltpu.SMEM(orientation.shape, jnp.int32),
            pltpu.SemaphoreType.DMA((14,)),
        ],
        space=HBM,
    )
    by_pair, by_next = both_ways(by_pair, by_next)
    late_pair, late_next, st, push, coef = call(
        late_kernel,
        [f32(6, *plane), f32(6, *plane), grid, f32(STEPS, width, *plane), f32(3, width, *plane)],
        [*(in_hbm(a) for a in (state, source, buoyancy, lame_first, shear_modulus)), cells],
        [(3, 3, *plane), (6, *plane), (6, *plane), (6, *plane)],
    )
    late_pair, late_next = both_ways(late_pair, late_next)
    args, outs, scalars = [by_pair, by_next], [], ()
    scratch = [early, early, (3, *plane), (3, 6, *plane), (3, 3, *plane)]
    owned = size_y // groups
    held = owned + BY
    if groups == 2:
        swapped = jnp.concatenate([by_pair[3 * size_y :], by_next[3 * size_y :], tile])
        swapped = lax.ppermute(swapped, "shot", [(0, 1), (1, 0)])
        args += [swapped, orientation]
        outs = [f32(3, held, size_z)]
        scratch += [(held, size_z)]
        scalars = (3,)
    three = f32(3, width, *plane)
    end, w, third, outer, parts, known, *weights = call(
        functools.partial(near_kernel, groups),
        [f32(2, 9, *plane), grid, three, f32(7, *plane), f32(4, 3, *plane), three, *outs],
        [*args, state, st, coef, cells, push, forward],
        scratch,
        scalars,
    )
    block = (3, width, held, size_z)
    images = [f32(*block), f32(*block)] if groups == 2 else [f32(3, width, *plane)]
    final, *images = call(
        functools.partial(far_kernel, groups),
        [pltpu.VMEM(grid.shape, grid.dtype), *images],
        [late_next, late_pair, st, end, w, third, outer, parts, known, coef, push, forward],
        [(6, *plane), (6, *plane), (2, 9, *plane), (3, *plane), (3, *plane), (3, width, *plane)],
    )
    if groups != 2:
        return final[None], smooth_anywhere(images[0], orientation)
    give, keep = images
    (weights,) = weights
    received = lax.ppermute(give, "shot", [(0, 1), (1, 0)])
    message = (6 * owned + BY, size_z)
    by_pair, by_next, grad, swept = call(
        functools.partial(sum_kernel, (STEPS * groups) ** (-0.5)),
        [f32(*message), f32(*message), f32(*block), f32(3, 2, held, size_z)],
        (keep, received, weights),
        [message, message],
    )
    by_pair, by_next = both_ways(by_pair, by_next)
    full, half = call(
        inner_kernel,
        [f32(*block), f32(3, width - 2, held, size_z)],
        (grad, swept, weights),
        [],
    )
    gradient = f32(3, width, owned, size_z)
    scratch = [(7, held, size_z), (3, 2, held, size_z), pltpu.SemaphoreType.DMA((2,))]
    rest = (grad, full, half, weights)
    gradient = call(
        functools.partial(side_kernel, True), gradient, (by_pair, *rest), scratch, out_space=HBM
    )
    gradient = call(
        functools.partial(side_kernel, False),
        f32(*gradient.shape),
        (by_next, gradient, *rest),
        scratch,
        out_space=HBM,
        held=1,
    )
    return final[None], gradient


def solution(mesh):
    return jax.shard_map(
        local,
        mesh=mesh,
        in_specs=(
            P("shot", None, "tile", None, None),
            P("shot", None, "tile", None, None),
            P("shot", None, "tile", None, None),
            P("tile", None, None),
            P("tile", None, None),
            P("tile", None, None),
            P("tile", None, None),
            P("tile", "shot", None),
        ),
        out_specs=(P("shot", None, "tile", None, None), P(None, "tile", "shot", None)),
        check_vma=False,
    )
```

```python
import functools

import jax
import jax.numpy as jnp
from jax import lax
from jax.experimental import pallas as pl
from jax.experimental.pallas import tpu as pltpu
from jax.sharding import PartitionSpec as P

BY = 8
BZ = 32
STEPS = 3
SWEEPS = 2

time_step = 0.25
smooth_rate = 0.1
weight_table = ((1.0, 1.0, 0.25), (0.25, 1.0, 1.0), (1.0, 0.25, 1.0), (0.6, 0.6, 0.6))

VX, VY, VZ, XX, YY, ZZ, XY, XZ, YZ = range(9)
VEL = (VX, VY, VZ)
SIDE = (XX, XY, XZ)
STRESS = (XX, YY, ZZ, XY, XZ, YZ)
ROWS = 32
VMEM = pl.BlockSpec(memory_space=pltpu.VMEM)
SMEM = pl.BlockSpec(memory_space=pltpu.SMEM)
HBM = pl.BlockSpec(memory_space=pltpu.HBM)


def lanes(shape):
    return lax.broadcasted_iota(jnp.int32, shape, len(shape) - 1)


def rows(shape):
    return lax.broadcasted_iota(jnp.int32, shape, len(shape) - 2)


def z_prev(f):
    return jnp.where(lanes(f.shape) == 0, 0.0, pltpu.roll(f, 1, f.ndim - 1))


def z_next(f):
    size = f.shape[-1]
    return jnp.where(lanes(f.shape) == size - 1, 0.0, pltpu.roll(f, size - 1, f.ndim - 1))


class Plane:
    def __init__(self, ref, *index):
        self.ref, self.index = ref, index
        self.size = ref.shape[len(index)]

    def at(self, row, count):
        return self.ref[self.index + (slice(row, row + count),)]

    def prev(self, row, count):
        if row:
            return self.at(row - 1, count)
        edge = pltpu.roll(self.at(0, 8), 1, 0)
        edge = jnp.where(rows(edge.shape) == 0, 0.0, edge)
        return jnp.concatenate([edge, self.at(7, count - 8)], 0)

    def next(self, row, count):
        if row + count < self.size:
            return self.at(row + 1, count)
        edge = pltpu.roll(self.at(self.size - 8, 8), 7, 0)
        edge = jnp.where(rows(edge.shape) == 7, 0.0, edge)
        return jnp.concatenate([self.at(row + 1, count - 8), edge], 0)

    def set(self, row, value):
        self.ref[self.index + (slice(row, row + value.shape[0]),)] = value


def planes(ref, comps, *index):
    return {c: Plane(ref, n, *index) for n, c in enumerate(comps)}


def divergence(s, before, row, count, have=(XX, YY, ZZ, XY, XZ, YZ)):
    def along_x(c):
        here = s[c].at(row, count)
        return here - before[c].at(row, count) if before is not None else here

    def along_y(c):
        return s[c].at(row, count) - s[c].prev(row, count)

    def along_z(c):
        here = s[c].at(row, count)
        return here - z_prev(here)

    out = []
    for c_x, c_y, c_z in ((XX, XY, XZ), (XY, YY, YZ), (XZ, YZ, ZZ)):
        terms = along_x(c_x)
        if c_y in have:
            terms = terms + along_y(c_y)
        if c_z in have:
            terms = terms + along_z(c_z)
        out.append(terms)
    return out


def strain(v, after, row, count, want=(XX, YY, ZZ, XY, XZ, YZ)):
    x, y, z = (v[c].at(row, count) for c in (VX, VY, VZ))
    if after is None:
        d_x = [-x, -y, -z]
    else:
        d_x = [after[c].at(row, count) - f for c, f in ((VX, x), (VY, y), (VZ, z))]
    out = {XX: d_x[0], YY: v[VY].next(row, count) - y, ZZ: z_next(z) - z}
    out["div"] = out[XX] + out[YY] + out[ZZ]
    if XY in want:
        out[XY] = v[VX].next(row, count) - x + d_x[1]
    if XZ in want:
        out[XZ] = z_next(x) - x + d_x[2]
    if YZ in want:
        out[YZ] = z_next(y) - y + (v[VZ].next(row, count) - z)
    return out


def stress_rate(e, lame, shear, want=(XX, YY, ZZ, XY, XZ, YZ)):
    spread = lame * e["div"]
    return {
        c: spread + 2.0 * shear * e[c] if c in (XX, YY, ZZ) else shear * e[c] for c in want
    }


def cell_plane(active, out):
    shape = (BY, out.shape[1])
    for j in range(out.shape[0] // BY):
        row = jnp.full(shape, active[0, 0, j].astype(jnp.float32))
        for k in range(1, out.shape[1] // BZ):
            row = jnp.where(lanes(shape) >= k * BZ, active[0, k, j].astype(jnp.float32), row)
        out[j * BY : (j + 1) * BY, :] = row


def chunks(size):
    return range(0, size, ROWS)


def is_even():
    return lax.rem(lax.axis_index("tile"), 2) == 0


def hand_out(by_pair, by_next, up, down):
    even = is_even()

    @pl.when(even)
    def _():
        by_pair[...] = up[...]
        by_next[...] = down[...]

    @pl.when(jnp.logical_not(even))
    def _():
        by_pair[...] = down[...]
        by_next[...] = up[...]


def take_in(by_pair, by_next, low, high):
    even = is_even()

    @pl.when(even)
    def _():
        low[...] = by_next[...]
        high[...] = by_pair[...]

    @pl.when(jnp.logical_not(even))
    def _():
        low[...] = by_pair[...]
        high[...] = by_next[...]

    clear_ends(low, high)


def no_neighbour(upper):
    return lax.axis_index("tile") == (lax.axis_size("tile") - 1 if upper else 0)


def clear_ends(low, high):
    for upper, ref in ((False, low), (True, high)):

        @pl.when(no_neighbour(upper))
        def _(ref=ref):
            ref[...] = jnp.zeros(ref.shape, jnp.float32)


def class_tile(orientation, j, size_z):
    shape = (BY, size_z)
    out = jnp.full(shape, orientation[0, j, 0].astype(jnp.float32))
    for k in range(1, size_z // BZ):
        out = jnp.where(lanes(shape) >= k * BZ, orientation[0, j, k].astype(jnp.float32), out)
    return out


def here(row):
    return slice(row, row + ROWS)


def early_kernel(
    groups,
    active_hbm,
    orientation_hbm,
    state_hbm,
    source_hbm,
    lame_hbm,
    shear_hbm,
    buoyancy_hbm,
    by_pair,
    by_next,
    cells,
    tile,
    up,
    down,
    first,
    push,
    params,
    active,
    orientation,
    sems,
):
    size_y, size_z = cells.shape
    last = state_hbm.shape[1] - 1
    planes_at = (0, 0, 0, 1, last, last, last)
    arrays = (buoyancy_hbm, lame_hbm, shear_hbm)
    ends = [(active_hbm, active), (orientation_hbm, orientation)]
    ends += [(arrays[n % 3].at[x], params.at[n]) for n, x in enumerate(planes_at)]
    ends += [(state_hbm.at[:, 0], first), (source_hbm.at[0, 0], push)]
    ends += [
        (state_hbm.at[c, last], up.at[n * size_y : (n + 1) * size_y]) for n, c in enumerate(SIDE)
    ]
    copies = [pltpu.make_async_copy(*pair, sems.at[n]) for n, pair in enumerate(ends)]
    for copy in (copies[9], *copies[2:9], *copies[:2], *copies[10:]):
        copy.start()
    for copy in copies[:2]:
        copy.wait()
    cell_plane(active, cells)
    me = lax.axis_index("shot") if groups == 2 else 0
    last_block = orientation.shape[1] - 1
    tile[...] = class_tile(orientation, jnp.where(me == 0, last_block, 0), size_z)
    for copy in copies[2:9]:
        copy.wait()
    for row in chunks(size_y):
        c = time_step * cells[here(row), :]
        for n in range(7):
            params[n, here(row)] = c * params[n, here(row)]
    count = (up.shape[0] - 3 * size_y) // 4
    mine = pl.ds(pl.multiple_of(me * count, 8), count) if groups == 2 else slice(0, count)
    for n in range(4):
        to = slice(3 * size_y + n * count, 3 * size_y + (n + 1) * count)
        down[to] = params[n, mine]
        up[to] = params[(6, 4, 5, 6)[n], mine]
    for copy in copies[9:]:
        copy.wait()
    raw = {c: Plane(first, c) for c in range(9)}
    for row in chunks(size_y):
        c, cb = cells[here(row), :], params[0, here(row)]
        for n, term in enumerate(divergence(raw, None, row, ROWS)):
            value = c * raw[n].at(row, ROWS) + cb * term
            if n == VZ:
                value = value + time_step * c * push[here(row)].astype(jnp.float32)
            down[n * size_y + row : n * size_y + row + ROWS] = value
    hand_out(by_pair, by_next, up, down)


def late_kernel(
    state, source, buoyancy, lame, shear, cells, by_pair, by_next, st, push, coef, v2, s2, up, down
):
    width, size_y = state.shape[1], state.shape[2]
    last = width - 1
    for row in chunks(size_y):
        c = time_step * cells[here(row), :]
        for step in range(STEPS):
            for x in range(width):
                push[step, x, here(row)] = c * source[step, x, here(row)].astype(jnp.float32)
        for n, param in enumerate((buoyancy, lame, shear)):
            for x in range(width):
                coef[n, x, here(row)] = c * param[x, here(row)]

    def coefs(x, row):
        return [coef[n, x, here(row)] for n in range(3)]

    raw = [{c: Plane(state, c, x) for c in range(9)} for x in range(width)]
    one = [{c: Plane(st, c, x) for c in range(9)} for x in range(width)]
    two = {x: {c: Plane(v2, n, c) for c in VEL} for n, x in enumerate((0, 1, last))}
    for x in range(width):
        for row in chunks(size_y):
            c = cells[here(row), :]
            cb = coefs(x, row)[0]
            terms = divergence(raw[x], raw[x - 1] if x else None, row, ROWS)
            for comp, term in zip(VEL, terms):
                value = c * raw[x][comp].at(row, ROWS) + cb * term
                if comp == VZ:
                    value = value + push[0, x, here(row)]
                one[x][comp].set(row, value)
    for x in range(width):
        for row in chunks(size_y):
            c = cells[here(row), :]
            _, cl, cm = coefs(x, row)
            rate = stress_rate(strain(one[x], one[x + 1] if x < last else None, row, ROWS), cl, cm)
            for comp, term in rate.items():
                one[x][comp].set(row, c * raw[x][comp].at(row, ROWS) + term)
    for x in two:
        for row in chunks(size_y):
            cb = coefs(x, row)[0]
            terms = divergence(one[x], one[x - 1] if x else None, row, ROWS)
            for comp, term in zip(VEL, terms):
                value = one[x][comp].at(row, ROWS) + cb * term
                if comp == VZ:
                    value = value + push[1, x, here(row)]
                two[x][comp].set(row, value)
    stress = {c: Plane(s2, c - XX) for c in STRESS}
    for row in chunks(size_y):
        _, cl, cm = coefs(0, row)
        rate = stress_rate(strain(two[0], two[1], row, ROWS), cl, cm)
        for comp, term in rate.items():
            stress[comp].set(row, one[0][comp].at(row, ROWS) + term)
        _, cl, cm = coefs(last, row)
        rate = stress_rate(strain(two[last], None, row, ROWS, SIDE), cl, cm, SIDE)
        for n, comp in enumerate(SIDE):
            value = one[last][comp].at(row, ROWS)
            up[n, here(row)] = value
            up[3 + n, here(row)] = value + rate[comp]
    for row in chunks(size_y):
        cb = coefs(0, row)[0]
        terms = divergence(stress, None, row, ROWS)
        for comp, term in zip(VEL, terms):
            before = two[0][comp].at(row, ROWS)
            value = before + cb * term
            if comp == VZ:
                value = value + push[2, 0, here(row)]
            down[comp, here(row)] = before
            down[3 + comp, here(row)] = value
    hand_out(by_pair, by_next, up, down)


def beyond(v, cl, cm):
    spread = cl * v[0]
    return {XX: spread + 2.0 * cm * v[0], YY: spread, ZZ: spread, XY: cm * v[1], XZ: cm * v[2]}


def add(terms):
    return functools.reduce(jnp.add, terms)


def imaged(moved, forward, x, row):
    f = [forward[n, x, here(row)].astype(jnp.float32) for n in range(9)]
    trace = (moved[XX] + moved[YY] + moved[ZZ]) * (f[0] + f[1] + f[2])
    shear = add([moved[comp] * f[n] for n, comp in enumerate(STRESS)])
    density = add([moved[c] * f[6 + c] for c in VEL]) if VX in moved else None
    return trace, shear, density


def own_planes(st, end):
    width = st.shape[1]
    one = [{c: Plane(st, c, x) for c in range(9)} for x in range(width)]
    one[0] = {c: Plane(end, 0, c) for c in range(9)}
    one[-1] = {c: Plane(st, c, width - 1) if c in VEL else Plane(end, 1, c) for c in range(9)}
    return one


def near_kernel(groups, *refs):
    by_pair, by_next, *refs = refs
    if groups == 2:
        swapped, orientation, *refs = refs
    state, st, coef, cells, push, forward, end, w, third, outer, parts, known, *refs = refs
    if groups == 2:
        weights, *refs = refs
    low, high, high_v, d_s, d_v, *classes = refs
    width, size_y = st.shape[1], st.shape[2]
    last = width - 1
    take_in(by_pair, by_next, low, high)
    count = (low.shape[0] - 3 * size_y) // 4
    base = 3 * size_y
    if groups == 2:
        me = lax.axis_index("shot")
        mine = pl.ds(pl.multiple_of(me * count, 8), count)
        theirs = pl.ds(pl.multiple_of((1 - me) * count, 8), count)
        low_at = pl.multiple_of(jnp.where(is_even(), 4 * count, 0), 8)
        high_at = pl.multiple_of(jnp.where(is_even(), 0, 4 * count), 8)
        for n in range(4):
            if n < 3:
                outer[n, mine] = low[base + n * count : base + (n + 1) * count]
                outer[n, theirs] = swapped[pl.ds(low_at + n * count, count)]
            outer[3 + n, mine] = high[base + n * count : base + (n + 1) * count]
            outer[3 + n, theirs] = swapped[pl.ds(high_at + n * count, count)]
    else:
        for n in range(4):
            if n < 3:
                outer[n] = low[base + n * count : base + (n + 1) * count]
            outer[3 + n] = high[base + n * count : base + (n + 1) * count]
    clear_ends(outer.at[0:3], outer.at[3:7])

    def coefs(x, row):
        if x < 0:
            return [outer[n, here(row)] for n in range(3)]
        if x > last:
            return [outer[3 + n, here(row)] for n in range(3)]
        return [coef[n, x, here(row)] for n in range(3)]

    raw = [{c: Plane(state, c, x) for c in range(9)} for x in range(width)]
    old = [{c: Plane(st, c, x) for c in range(9)} for x in range(width)]
    one = own_planes(st, end)
    two = [{c: Plane(w, c, x) for c in range(9)} for x in range(width)]
    high_one = {c: Plane(high_v, c) for c in VEL}
    d_low_s, d_high_s, d_high_s_two = ({c: Plane(d_s, k, c - XX) for c in STRESS} for k in range(3))
    d_high_v, d_far_v, d_low_v = ({c: Plane(d_v, k, c) for c in VEL} for k in range(3))
    part_v, part_low, d_high_v_two, part_high = (
        {c: Plane(parts, k, n) for n, c in enumerate(names)}
        for k, names in enumerate((VEL, SIDE, VEL, VEL))
    )

    for row in chunks(size_y):
        cb, cb_high = coefs(0, row)[0], coefs(last + 1, row)[0]
        for n, (comp, c) in enumerate(zip(VEL, SIDE)):
            at = slice(n * size_y + row, n * size_y + row + ROWS)
            one[0][comp].set(row, old[0][comp].at(row, ROWS) - cb * low[at])
            delta = -cb_high * raw[last][c].at(row, ROWS)
            d_high_v[comp].set(row, delta)
            high_one[comp].set(row, high[at] + delta)
    for row in chunks(size_y):
        c = cells[here(row), :]
        _, cl, cm = coefs(0, row)
        for comp, term in stress_rate(strain(one[0], one[1], row, ROWS), cl, cm).items():
            one[0][comp].set(row, c * raw[0][comp].at(row, ROWS) + term)
        _, cl, cm = coefs(last, row)
        terms = beyond([high_one[comp].at(row, ROWS) for comp in VEL], cl, cm)
        for comp in STRESS:
            value = old[last][comp].at(row, ROWS)
            one[last][comp].set(row, value + terms[comp] if comp in terms else value)
        _, cl, cm = coefs(-1, row)
        for comp, term in beyond([one[0][comp].at(row, ROWS) for comp in VEL], cl, cm).items():
            d_low_s[comp].set(row, term)
        _, cl, cm = coefs(last + 1, row)
        for comp, term in stress_rate(strain(d_high_v, None, row, ROWS), cl, cm).items():
            d_high_s[comp].set(row, term)

    for row in chunks(size_y):
        for x in range(width):
            cb = coefs(x, row)[0]
            terms = divergence(one[x], one[x - 1] if x else d_low_s, row, ROWS)
            for comp, term in zip(VEL, terms):
                value = one[x][comp].at(row, ROWS) + cb * term
                if comp == VZ:
                    value = value + push[1, x, here(row)]
                (two[x] if x else part_v)[comp].set(row, value)
        cb = coefs(last + 1, row)[0]
        for comp, term in zip(VEL, divergence(d_high_s, one[last], row, ROWS)):
            d_high_v_two[comp].set(row, d_high_v[comp].at(row, ROWS) + cb * term)
        cb = outer[6, here(row)]
        for comp, c in zip(VEL, SIDE):
            d_far_v[comp].set(row, -cb * d_high_s[c].at(row, ROWS))
        cb = coefs(-1, row)[0]
        terms = divergence(d_low_s, None, row, ROWS, (XX, YY, ZZ, XY, XZ))
        for comp, term in zip(VEL, terms):
            d_low_v[comp].set(row, cb * term)
    for row in chunks(size_y):
        for x in range(1, width):
            _, cl, cm = coefs(x, row)
            after = two[x + 1] if x < last else None
            for comp, term in stress_rate(strain(two[x], after, row, ROWS), cl, cm).items():
                two[x][comp].set(row, one[x][comp].at(row, ROWS) + term)
        _, cl, cm = coefs(-1, row)
        rate = stress_rate(strain(d_low_v, None, row, ROWS, SIDE), cl, cm, SIDE)
        for comp, term in rate.items():
            part_low[comp].set(row, d_low_s[comp].at(row, ROWS) + term)
        _, cl, cm = coefs(last + 1, row)
        for comp, term in stress_rate(strain(d_high_v_two, d_far_v, row, ROWS), cl, cm).items():
            d_high_s_two[comp].set(row, d_high_s[comp].at(row, ROWS) + term)
    for row in chunks(size_y):
        cb = coefs(last + 1, row)[0]
        for comp, term in zip(VEL, divergence(d_high_s_two, None, row, ROWS)):
            part_high[comp].set(row, d_high_v_two[comp].at(row, ROWS) + cb * term)
        for x in range(2, last):
            cb = coefs(x, row)[0]
            for comp, term in zip(VEL, divergence(two[x], two[x - 1], row, ROWS)):
                value = two[x][comp].at(row, ROWS) + cb * term
                if comp == VZ:
                    value = value + push[2, x, here(row)]
                third[comp, x, here(row)] = value
    for row in chunks(size_y):
        for x in range(width):
            inner = 1 <= x < last
            v, t = [one[x]], [one[x]] + [two[x]] * inner
            if x:
                v.append(two[x])
            if 2 <= x < last:
                v.append({c: Plane(third, c, x) for c in VEL})
            moved = {c: add([k[c].at(row, ROWS) for k in v]) for c in VEL}
            moved |= {c: add([k[c].at(row, ROWS) for k in t]) for c in STRESS}
            for n, value in enumerate(imaged(moved, forward, x, row)):
                known[n, x, here(row)] = value
    if groups != 2:
        return

    (classes,) = classes
    rows_held = weights.shape[1]
    own = rows_held - BY
    first = pl.multiple_of(me * BY, BY)
    for j in range(own // BY):
        classes[pl.ds(first + j * BY, BY), :] = class_tile(orientation, j, weights.shape[2])
    classes[pl.ds(pl.multiple_of((1 - me) * own, BY), BY), :] = swapped[8 * count :, :]
    klass = classes[...]
    for column in range(3):
        table = jnp.full(klass.shape, weight_table[3][column], jnp.float32)
        for k in range(3):
            table = jnp.where(klass == k, weight_table[k][column], table)
        weights[column] = smooth_rate * table


def far_kernel(groups, *refs):
    by_next, by_pair, st, end, w, third, outer, parts, known, coef, push, forward, final, *refs = refs
    *images, low, high, edge, low_s, high_v, image = refs
    width, size_y = st.shape[1], st.shape[2]
    last = width - 1
    take_in(by_pair, by_next, low, high)

    def coefs(x, row):
        if x < 0:
            return [outer[n, here(row)] for n in range(3)]
        if x > last:
            return [outer[3 + n, here(row)] for n in range(3)]
        return [coef[n, x, here(row)] for n in range(3)]

    one = own_planes(st, end)
    part = [{c: Plane(w, c, x) for c in range(9)} for x in range(width)]
    two = [dict(p) for p in part]
    for c in range(9):
        two[0][c] = Plane(edge, 0, c)
        if c >= XX:
            two[last][c] = Plane(edge, 1, c)
    three = [{c: Plane(final, c, x) for c in range(9)} for x in range(width)]
    part_v, part_low, d_high_v_two, part_high = (
        {c: Plane(parts, k, n) for n, c in enumerate(names)}
        for k, names in enumerate((VEL, SIDE, VEL, VEL))
    )
    low_two = {c: Plane(low_s, n) for n, c in enumerate(SIDE)}
    high_three = {c: Plane(high_v, c) for c in VEL}

    for row in chunks(size_y):
        cb = coefs(0, row)[0]
        moved = []
        for n, comp in enumerate(VEL):
            moved.append(part_v[comp].at(row, ROWS) - cb * low[n, here(row)])
            two[0][comp].set(row, moved[n])
        _, cl, cm = coefs(-1, row)
        terms = beyond(moved, cl, cm)
        for n, comp in enumerate(SIDE):
            value = low[3 + n, here(row)] + part_low[comp].at(row, ROWS)
            low_two[comp].set(row, value + terms[comp])
        _, cl, cm = coefs(last, row)
        cb = coefs(last + 1, row)[0]
        moved = [high[n, here(row)] + d_high_v_two[n].at(row, ROWS) for n in VEL]
        terms = beyond(moved, cl, cm)
        values = {}
        for comp in STRESS:
            value = part[last][comp].at(row, ROWS)
            values[comp] = value + terms[comp] if comp in terms else value
            two[last][comp].set(row, values[comp])
        for n, comp in enumerate(SIDE):
            value = high[3 + n, here(row)] + part_high[n].at(row, ROWS)
            high_three[n].set(row, value - cb * values[comp])
    for row in chunks(size_y):
        _, cl, cm = coefs(0, row)
        for comp, term in stress_rate(strain(two[0], two[1], row, ROWS), cl, cm).items():
            two[0][comp].set(row, one[0][comp].at(row, ROWS) + term)

    for row in chunks(size_y):
        for x in range(width):
            if 2 <= x < last:
                for comp in VEL:
                    three[x][comp].set(row, third[comp, x, here(row)])
                continue
            cb = coefs(x, row)[0]
            terms = divergence(two[x], two[x - 1] if x else low_two, row, ROWS)
            for comp, term in zip(VEL, terms):
                value = two[x][comp].at(row, ROWS) + cb * term
                if comp == VZ:
                    value = value + push[2, x, here(row)]
                three[x][comp].set(row, value)
    for row in chunks(size_y):
        for x in range(width):
            _, cl, cm = coefs(x, row)
            after = three[x + 1] if x < last else high_three
            rate = stress_rate(strain(three[x], after, row, ROWS), cl, cm)
            moved = {}
            for comp in STRESS:
                before = two[x][comp].at(row, ROWS)
                value = before + rate[comp]
                three[x][comp].set(row, value)
                moved[comp] = value if 1 <= x < last else before + value
            if not 2 <= x < last:
                for comp in VEL:
                    moved[comp] = three[x][comp].at(row, ROWS)
                    if not x:
                        moved[comp] = two[x][comp].at(row, ROWS) + moved[comp]
            for n, value in enumerate(imaged(moved, forward, x, row)):
                before = known[n, x, here(row)]
                image[n, x, here(row)] = before if value is None else before + value

    if groups != 2:
        images[0][...] = image[...]
        return
    give, keep = images
    me = lax.axis_index("shot")
    count = keep.shape[2]
    mine = pl.ds(pl.multiple_of(me * (size_y - count), 8), count)
    theirs = pl.ds(pl.multiple_of((1 - me) * (size_y - count), 8), count)
    for n in range(3):
        for x in range(width):
            give[n, x] = image[n, x, theirs, :]
            keep[n, x] = image[n, x, mine, :]


def y_prev(f):
    return jnp.where(rows(f.shape) == 0, 0.0, pltpu.roll(f, 1, f.ndim - 2))


def y_next(f):
    size = f.shape[-2]
    return jnp.where(rows(f.shape) == size - 1, 0.0, pltpu.roll(f, size - 1, f.ndim - 2))


def sweep(g, before, after, weights):
    w_x, w_y, w_z = weights
    twice = 2.0 * g
    along_x = -twice
    for plane in (before, after):
        if plane is not None:
            along_x = along_x + plane
    along_y = y_next(g) + y_prev(g) - twice
    along_z = z_next(g) + z_prev(g) - twice
    return g + (w_x * along_x + w_y * along_y + w_z * along_z)


def edge_row(me, own):
    return jnp.where(me == 0, own, BY - 1)


def sum_kernel(scale, keep, received, weights, by_pair, by_next, grad, swept, up, down):
    width, count, size_z = grad.shape[1:]
    own = count - BY
    me = lax.axis_index("shot")
    first = pl.multiple_of(me * BY, BY)
    mine = pl.ds(first, own)
    edge = pl.ds(edge_row(me, own), 1)
    last = width - 1
    w = [weights[k] for k in range(3)]
    for to in (up, down):
        to[6 * own :, :] = jnp.zeros((BY, size_z), jnp.float32)
        for j in range(own // BY):
            row = weights[0, pl.ds(pl.multiple_of(first + j * BY, BY), BY), :][0:1]
            to[6 * own + 3 + j : 6 * own + 4 + j, :] = row
    for n in range(3):
        for x in range(width):
            grad[n, x] = (keep[n, x] + received[n, x]) * scale
        swept[n, 0] = sweep(grad[n, 0], None, grad[n, 1], w)
        swept[n, 1] = sweep(grad[n, last], grad[n, last - 1], None, w)
        for to, x, side in ((up, last, 1), (down, 0, 0)):
            to[2 * n * own : (2 * n + 1) * own, :] = grad[n, x, mine, :]
            to[(2 * n + 1) * own : (2 * n + 2) * own, :] = swept[n, side, mine, :]
            to[6 * own + n : 6 * own + n + 1, :] = grad[n, x, edge, :]
    hand_out(by_pair, by_next, up, down)


def inner_kernel(grad, swept, weights, full, half):
    width = grad.shape[1]
    last = width - 1
    w = [weights[k] for k in range(3)]
    for n in range(3):
        full[n, 0] = swept[n, 0]
        full[n, last] = swept[n, 1]
        for x in range(1, last):
            full[n, x] = sweep(grad[n, x], grad[n, x - 1], grad[n, x + 1], w)
        for x in range(1, last):
            half[n, x - 1] = sweep(
                full[n, x],
                full[n, x - 1] if x > 1 else None,
                full[n, x + 1] if x < last - 1 else None,
                w,
            )


def side_kernel(near, *refs):
    got, *refs = refs
    if not near:
        _, *refs = refs
    grad, full, half, weights, out, beside, result, sems = refs
    width, count, size_z = grad.shape[1:]
    own = count - BY
    me = lax.axis_index("shot")
    first = pl.multiple_of(me * BY, BY)
    mine = pl.ds(first, own)
    edge = pl.ds(edge_row(me, own), 1)
    upper = is_even() if near else jnp.logical_not(is_even())
    end = jnp.where(upper, width - 1, 0)
    inner = jnp.where(upper, width - 2, 1)
    beside[...] = jnp.zeros(beside.shape, jnp.float32)
    for n in range(3):
        beside[n, mine, :] = got[2 * n * own : (2 * n + 1) * own, :]
        beside[n, edge, :] = got[6 * own + n : 6 * own + n + 1, :]
        beside[3 + n, mine, :] = got[(2 * n + 1) * own : (2 * n + 2) * own, :]
    for j in range(own // BY):
        row = got[6 * own + 3 + j : 6 * own + 4 + j, :]
        to = pl.ds(pl.multiple_of(first + j * BY, BY), BY)
        beside[6, to, :] = jnp.broadcast_to(row, (BY, size_z))
    @pl.when(jnp.where(upper, no_neighbour(True), no_neighbour(False)))
    def _():
        beside[...] = jnp.zeros(beside.shape, jnp.float32)

    w = [weights[k] for k in range(3)]
    for n in range(3):
        value = full[n, end] + w[0] * beside[n]
        outer = beside[3 + n] + beside[6] * grad[n, end]
        result[n, 0] = sweep(value, outer, full[n, inner], w)
        result[n, 1] = half[n, inner - 1] + w[0] * value
    copies = [
        pltpu.make_async_copy(result.at[:, k, mine, :], out.at[:, x], sems.at[k])
        for k, x in enumerate((end, inner))
    ]
    for copy in copies:
        copy.start()
    for copy in copies:
        copy.wait()


def extended(block, sides, width):
    for axis, dim in sides:
        count = lax.axis_size(axis)
        forward = [(i, i + 1) for i in range(count - 1)]
        backward = [(target, source) for source, target in forward]
        low = lax.ppermute(
            lax.slice_in_dim(block, block.shape[dim] - width, None, axis=dim), axis, forward
        )
        high = lax.ppermute(lax.slice_in_dim(block, 0, width, axis=dim), axis, backward)
        block = jnp.concatenate([low, block, high], axis=dim)
    return block


def smooth_anywhere(image, orientation):
    groups = lax.axis_size("shot")
    owned = image.shape[2] // groups
    total = lax.psum(image, "shot")
    grad = lax.dynamic_slice_in_dim(total, lax.axis_index("shot") * owned, owned, 2)
    grad = grad * (STEPS * groups) ** (-0.5)
    weights = []
    for column in range(3):
        table = jnp.zeros(orientation.shape, jnp.float32)
        for klass in range(4):
            table = table + (orientation == klass).astype(jnp.float32) * weight_table[klass][column]
        table = jnp.repeat(jnp.repeat(table, image.shape[1], 0), BY, 1)
        weights.append(jnp.repeat(table, BZ, 2))
    for _ in range(SWEEPS):
        padded = extended(grad, (("shot", 2), ("tile", 1)), 1)
        padded = jnp.pad(padded, ((0, 0), (0, 0), (0, 0), (1, 1)))
        center = padded[:, 1:-1, 1:-1, 1:-1]
        lap_x = padded[:, 2:, 1:-1, 1:-1] + padded[:, :-2, 1:-1, 1:-1] - 2.0 * center
        lap_y = padded[:, 1:-1, 2:, 1:-1] + padded[:, 1:-1, :-2, 1:-1] - 2.0 * center
        lap_z = padded[:, 1:-1, 1:-1, 2:] + padded[:, 1:-1, 1:-1, :-2] - 2.0 * center
        grad = grad + smooth_rate * (weights[0] * lap_x + weights[1] * lap_y + weights[2] * lap_z)
    return grad


def both_ways(by_pair, by_next):
    count, groups = lax.axis_size("tile"), lax.axis_size("shot")
    out = []
    for array, start in ((by_pair, 0), (by_next, 1)):
        to = {}
        for i in range(start, count - 1, 2):
            to[i], to[i + 1] = i + 1, i
        pairs = [
            (shot * count + i, shot * count + to[i] if i in to else (shot + 1) % groups * count + i)
            for shot in range(groups)
            for i in range(count)
        ]
        out.append(lax.ppermute(array, ("shot", "tile"), pairs))
    return out


def f32(*shape):
    return jax.ShapeDtypeStruct(shape, jnp.float32)


def in_hbm(array):
    return pltpu.with_memory_space_constraint(array, pltpu.HBM)


def call(kernel, outs, args, scratch, scalars=(), space=VMEM, out_space=VMEM, held=None):
    specs = [SMEM if n in scalars else HBM if n == held else space for n in range(len(args))]
    return pl.pallas_call(
        kernel,
        out_shape=outs,
        in_specs=specs,
        out_specs=jax.tree.map(lambda _: out_space, outs),
        scratch_shapes=[
            pltpu.VMEM(shape, jnp.float32) if isinstance(shape, tuple) else shape
            for shape in scratch
        ],
        input_output_aliases={} if held is None else {held: 0},
        compiler_params=pltpu.CompilerParams(vmem_limit_bytes=24 * 1024 * 1024),
    )(*args)


def local(
    adjoint_state,
    adjoint_source,
    forward_field,
    lame_first,
    shear_modulus,
    buoyancy,
    active_blocks,
    orientation,
):
    width, size_y, size_z = lame_first.shape
    plane = (size_y, size_z)
    groups = lax.axis_size("shot")
    state, source, forward = adjoint_state[0], adjoint_source[0], forward_field[0]
    active = jnp.swapaxes(active_blocks, 1, 2)
    grid = f32(9, width, *plane)
    count = size_y // 2 if groups == 2 else size_y
    early = (3 * size_y + 4 * count, size_z)
    by_pair, by_next, cells, tile = call(
        functools.partial(early_kernel, groups),
        [f32(*early), f32(*early), f32(*plane), f32(BY, size_z)],
        [
            in_hbm(a)
            for a in (active, orientation, state, source, lame_first, shear_modulus, buoyancy)
        ],
        [
            early,
            early,
            (9, *plane),
            pltpu.VMEM(plane, source.dtype),
            (7, *plane),
            pltpu.SMEM(active.shape, jnp.int32),
            pltpu.SMEM(orientation.shape, jnp.int32),
            pltpu.SemaphoreType.DMA((14,)),
        ],
        space=HBM,
    )
    by_pair, by_next = both_ways(by_pair, by_next)
    late_pair, late_next, st, push, coef = call(
        late_kernel,
        [f32(6, *plane), f32(6, *plane), grid, f32(STEPS, width, *plane), f32(3, width, *plane)],
        [*(in_hbm(a) for a in (state, source, buoyancy, lame_first, shear_modulus)), cells],
        [(3, 3, *plane), (6, *plane), (6, *plane), (6, *plane)],
    )
    late_pair, late_next = both_ways(late_pair, late_next)
    args, outs, scalars = [by_pair, by_next], [], ()
    scratch = [early, early, (3, *plane), (3, 6, *plane), (3, 3, *plane)]
    owned = size_y // groups
    held = owned + BY
    if groups == 2:
        swapped = jnp.concatenate([by_pair[3 * size_y :], by_next[3 * size_y :], tile])
        swapped = lax.ppermute(swapped, "shot", [(0, 1), (1, 0)])
        args += [swapped, orientation]
        outs = [f32(3, held, size_z)]
        scratch += [(held, size_z)]
        scalars = (3,)
    three = f32(3, width, *plane)
    end, w, third, outer, parts, known, *weights = call(
        functools.partial(near_kernel, groups),
        [f32(2, 9, *plane), grid, three, f32(7, *plane), f32(4, 3, *plane), three, *outs],
        [*args, state, st, coef, cells, push, forward],
        scratch,
        scalars,
    )
    block = (3, width, held, size_z)
    images = [f32(*block), f32(*block)] if groups == 2 else [f32(3, width, *plane)]
    final, *images = call(
        functools.partial(far_kernel, groups),
        [pltpu.VMEM(grid.shape, grid.dtype), *images],
        [late_next, late_pair, st, end, w, third, outer, parts, known, coef, push, forward],
        [(6, *plane), (6, *plane), (2, 9, *plane), (3, *plane), (3, *plane), (3, width, *plane)],
    )
    if groups != 2:
        return final[None], smooth_anywhere(images[0], orientation)
    give, keep = images
    (weights,) = weights
    received = lax.ppermute(give, "shot", [(0, 1), (1, 0)])
    message = (6 * owned + BY, size_z)
    by_pair, by_next, grad, swept = call(
        functools.partial(sum_kernel, (STEPS * groups) ** (-0.5)),
        [f32(*message), f32(*message), f32(*block), f32(3, 2, held, size_z)],
        (keep, received, weights),
        [message, message],
    )
    by_pair, by_next = both_ways(by_pair, by_next)
    full, half = call(
        inner_kernel,
        [f32(*block), f32(3, width - 2, held, size_z)],
        (grad, swept, weights),
        [],
    )
    gradient = f32(3, width, owned, size_z)
    scratch = [(7, held, size_z), (3, 2, held, size_z), pltpu.SemaphoreType.DMA((2,))]
    rest = (grad, full, half, weights)
    gradient = call(
        functools.partial(side_kernel, True), gradient, (by_pair, *rest), scratch, out_space=HBM
    )
    gradient = call(
        functools.partial(side_kernel, False),
        f32(*gradient.shape),
        (by_next, gradient, *rest),
        scratch,
        out_space=HBM,
        held=1,
    )
    return final[None], gradient


def solution(mesh):
    return jax.shard_map(
        local,
        mesh=mesh,
        in_specs=(
            P("shot", None, "tile", None, None),
            P("shot", None, "tile", None, None),
            P("shot", None, "tile", None, None),
            P("tile", None, None),
            P("tile", None, None),
            P("tile", None, None),
            P("tile", None, None),
            P("tile", "shot", None),
        ),
        out_specs=(P("shot", None, "tile", None, None), P(None, "tile", "shot", None)),
        check_vma=False,
    )
```

```python
import functools

import jax
import jax.numpy as jnp
from jax import lax
from jax.experimental import pallas as pl
from jax.experimental.pallas import tpu as pltpu
from jax.sharding import PartitionSpec as P

BY = 8
BZ = 32
STEPS = 3
SWEEPS = 2

time_step = 0.25
smooth_rate = 0.1
weight_table = ((1.0, 1.0, 0.25), (0.25, 1.0, 1.0), (1.0, 0.25, 1.0), (0.6, 0.6, 0.6))

VX, VY, VZ, XX, YY, ZZ, XY, XZ, YZ = range(9)
VEL = (VX, VY, VZ)
SIDE = (XX, XY, XZ)
STRESS = (XX, YY, ZZ, XY, XZ, YZ)
ROWS = 32
VMEM = pl.BlockSpec(memory_space=pltpu.VMEM)
SMEM = pl.BlockSpec(memory_space=pltpu.SMEM)
HBM = pl.BlockSpec(memory_space=pltpu.HBM)


def lanes(shape):
    return lax.broadcasted_iota(jnp.int32, shape, len(shape) - 1)


def rows(shape):
    return lax.broadcasted_iota(jnp.int32, shape, len(shape) - 2)


def z_prev(f):
    return jnp.where(lanes(f.shape) == 0, 0.0, pltpu.roll(f, 1, f.ndim - 1))


def z_next(f):
    size = f.shape[-1]
    return jnp.where(lanes(f.shape) == size - 1, 0.0, pltpu.roll(f, size - 1, f.ndim - 1))


class Plane:
    def __init__(self, ref, *index):
        self.ref, self.index = ref, index
        self.size = ref.shape[len(index)]

    def at(self, row, count):
        return self.ref[self.index + (slice(row, row + count),)]

    def prev(self, row, count):
        if row:
            return self.at(row - 1, count)
        edge = pltpu.roll(self.at(0, 8), 1, 0)
        edge = jnp.where(rows(edge.shape) == 0, 0.0, edge)
        return jnp.concatenate([edge, self.at(7, count - 8)], 0)

    def next(self, row, count):
        if row + count < self.size:
            return self.at(row + 1, count)
        edge = pltpu.roll(self.at(self.size - 8, 8), 7, 0)
        edge = jnp.where(rows(edge.shape) == 7, 0.0, edge)
        return jnp.concatenate([self.at(row + 1, count - 8), edge], 0)

    def set(self, row, value):
        self.ref[self.index + (slice(row, row + value.shape[0]),)] = value


def planes(ref, comps, *index):
    return {c: Plane(ref, n, *index) for n, c in enumerate(comps)}


def divergence(s, before, row, count, have=(XX, YY, ZZ, XY, XZ, YZ)):
    def along_x(c):
        here = s[c].at(row, count)
        return here - before[c].at(row, count) if before is not None else here

    def along_y(c):
        return s[c].at(row, count) - s[c].prev(row, count)

    def along_z(c):
        here = s[c].at(row, count)
        return here - z_prev(here)

    out = []
    for c_x, c_y, c_z in ((XX, XY, XZ), (XY, YY, YZ), (XZ, YZ, ZZ)):
        terms = along_x(c_x)
        if c_y in have:
            terms = terms + along_y(c_y)
        if c_z in have:
            terms = terms + along_z(c_z)
        out.append(terms)
    return out


def strain(v, after, row, count, want=(XX, YY, ZZ, XY, XZ, YZ)):
    x, y, z = (v[c].at(row, count) for c in (VX, VY, VZ))
    if after is None:
        d_x = [-x, -y, -z]
    else:
        d_x = [after[c].at(row, count) - f for c, f in ((VX, x), (VY, y), (VZ, z))]
    out = {XX: d_x[0], YY: v[VY].next(row, count) - y, ZZ: z_next(z) - z}
    out["div"] = out[XX] + out[YY] + out[ZZ]
    if XY in want:
        out[XY] = v[VX].next(row, count) - x + d_x[1]
    if XZ in want:
        out[XZ] = z_next(x) - x + d_x[2]
    if YZ in want:
        out[YZ] = z_next(y) - y + (v[VZ].next(row, count) - z)
    return out


def stress_rate(e, lame, shear, want=(XX, YY, ZZ, XY, XZ, YZ)):
    spread = lame * e["div"]
    return {
        c: spread + 2.0 * shear * e[c] if c in (XX, YY, ZZ) else shear * e[c] for c in want
    }


def cell_plane(active, out):
    shape = (BY, out.shape[1])
    for j in range(out.shape[0] // BY):
        row = jnp.full(shape, active[0, 0, j].astype(jnp.float32))
        for k in range(1, out.shape[1] // BZ):
            row = jnp.where(lanes(shape) >= k * BZ, active[0, k, j].astype(jnp.float32), row)
        out[j * BY : (j + 1) * BY, :] = row


def chunks(size):
    return range(0, size, ROWS)


def is_even():
    return lax.rem(lax.axis_index("tile"), 2) == 0


def hand_out(by_pair, by_next, up, down):
    even = is_even()

    @pl.when(even)
    def _():
        by_pair[...] = up[...]
        by_next[...] = down[...]

    @pl.when(jnp.logical_not(even))
    def _():
        by_pair[...] = down[...]
        by_next[...] = up[...]


def take_in(by_pair, by_next, low, high):
    even = is_even()

    @pl.when(even)
    def _():
        low[...] = by_next[...]
        high[...] = by_pair[...]

    @pl.when(jnp.logical_not(even))
    def _():
        low[...] = by_pair[...]
        high[...] = by_next[...]

    clear_ends(low, high)


def no_neighbour(upper):
    return lax.axis_index("tile") == (lax.axis_size("tile") - 1 if upper else 0)


def clear_ends(low, high):
    for upper, ref in ((False, low), (True, high)):

        @pl.when(no_neighbour(upper))
        def _(ref=ref):
            ref[...] = jnp.zeros(ref.shape, jnp.float32)


def class_tile(orientation, j, size_z):
    shape = (BY, size_z)
    out = jnp.full(shape, orientation[0, j, 0].astype(jnp.float32))
    for k in range(1, size_z // BZ):
        out = jnp.where(lanes(shape) >= k * BZ, orientation[0, j, k].astype(jnp.float32), out)
    return out


def here(row):
    return slice(row, row + ROWS)


def early_kernel(
    groups,
    active_hbm,
    orientation_hbm,
    state_hbm,
    source_hbm,
    lame_hbm,
    shear_hbm,
    buoyancy_hbm,
    by_pair,
    by_next,
    cells,
    tile,
    up,
    down,
    first,
    push,
    params,
    active,
    orientation,
    sems,
):
    size_y, size_z = cells.shape
    last = state_hbm.shape[1] - 1
    planes_at = (0, 0, 0, 1, last, last, last)
    arrays = (buoyancy_hbm, lame_hbm, shear_hbm)
    ends = [(active_hbm, active), (orientation_hbm, orientation)]
    ends += [(arrays[n % 3].at[x], params.at[n]) for n, x in enumerate(planes_at)]
    ends += [(state_hbm.at[:, 0], first), (source_hbm.at[0, 0], push)]
    ends += [
        (state_hbm.at[c, last], up.at[n * size_y : (n + 1) * size_y]) for n, c in enumerate(SIDE)
    ]
    copies = [pltpu.make_async_copy(*pair, sems.at[n]) for n, pair in enumerate(ends)]
    for copy in (copies[9], *copies[2:9], *copies[:2], *copies[10:]):
        copy.start()
    for copy in copies[:2]:
        copy.wait()
    cell_plane(active, cells)
    me = lax.axis_index("shot") if groups == 2 else 0
    last_block = orientation.shape[1] - 1
    tile[...] = class_tile(orientation, jnp.where(me == 0, last_block, 0), size_z)
    for copy in copies[2:9]:
        copy.wait()
    for row in chunks(size_y):
        c = time_step * cells[here(row), :]
        for n in range(7):
            params[n, here(row)] = c * params[n, here(row)]
    count = (up.shape[0] - 3 * size_y) // 4
    mine = pl.ds(pl.multiple_of(me * count, 8), count) if groups == 2 else slice(0, count)
    for n in range(4):
        to = slice(3 * size_y + n * count, 3 * size_y + (n + 1) * count)
        down[to] = params[n, mine]
        up[to] = params[(6, 4, 5, 6)[n], mine]
    for copy in copies[9:]:
        copy.wait()
    raw = {c: Plane(first, c) for c in range(9)}
    for row in chunks(size_y):
        c, cb = cells[here(row), :], params[0, here(row)]
        for n, term in enumerate(divergence(raw, None, row, ROWS)):
            value = c * raw[n].at(row, ROWS) + cb * term
            if n == VZ:
                value = value + time_step * c * push[here(row)].astype(jnp.float32)
            down[n * size_y + row : n * size_y + row + ROWS] = value
    hand_out(by_pair, by_next, up, down)


def late_kernel(
    state, source, buoyancy, lame, shear, forward, cells, by_pair, by_next, st, push, coef, field, early, v2, s2, up, down
):
    width, size_y = state.shape[1], state.shape[2]
    last = width - 1
    for row in chunks(size_y):
        c = time_step * cells[here(row), :]
        for step in range(STEPS):
            for x in range(width):
                push[step, x, here(row)] = c * source[step, x, here(row)].astype(jnp.float32)
        for n, param in enumerate((buoyancy, lame, shear)):
            for x in range(width):
                coef[n, x, here(row)] = c * param[x, here(row)]

    for row in chunks(size_y):
        for x in range(width):
            for n in range(9):
                field[n, x, here(row)] = forward[n, x, here(row)].astype(jnp.float32)

    def coefs(x, row):
        return [coef[n, x, here(row)] for n in range(3)]

    raw = [{c: Plane(state, c, x) for c in range(9)} for x in range(width)]
    one = [{c: Plane(st, c, x) for c in range(9)} for x in range(width)]
    two = {x: {c: Plane(v2, n, c) for c in VEL} for n, x in enumerate((0, 1, last))}
    for x in range(width):
        for row in chunks(size_y):
            c = cells[here(row), :]
            cb = coefs(x, row)[0]
            terms = divergence(raw[x], raw[x - 1] if x else None, row, ROWS)
            for comp, term in zip(VEL, terms):
                value = c * raw[x][comp].at(row, ROWS) + cb * term
                if comp == VZ:
                    value = value + push[0, x, here(row)]
                one[x][comp].set(row, value)
    for x in range(width):
        for row in chunks(size_y):
            c = cells[here(row), :]
            _, cl, cm = coefs(x, row)
            rate = stress_rate(strain(one[x], one[x + 1] if x < last else None, row, ROWS), cl, cm)
            for comp, term in rate.items():
                one[x][comp].set(row, c * raw[x][comp].at(row, ROWS) + term)
    for x in two:
        for row in chunks(size_y):
            cb = coefs(x, row)[0]
            terms = divergence(one[x], one[x - 1] if x else None, row, ROWS)
            for comp, term in zip(VEL, terms):
                value = one[x][comp].at(row, ROWS) + cb * term
                if comp == VZ:
                    value = value + push[1, x, here(row)]
                two[x][comp].set(row, value)
    stress = {c: Plane(s2, c - XX) for c in STRESS}
    for row in chunks(size_y):
        _, cl, cm = coefs(0, row)
        rate = stress_rate(strain(two[0], two[1], row, ROWS), cl, cm)
        for comp, term in rate.items():
            stress[comp].set(row, one[0][comp].at(row, ROWS) + term)
        _, cl, cm = coefs(last, row)
        rate = stress_rate(strain(two[last], None, row, ROWS, SIDE), cl, cm, SIDE)
        for n, comp in enumerate(SIDE):
            value = one[last][comp].at(row, ROWS)
            up[n, here(row)] = value
            up[3 + n, here(row)] = value + rate[comp]
    for row in chunks(size_y):
        cb = coefs(0, row)[0]
        terms = divergence(stress, None, row, ROWS)
        for comp, term in zip(VEL, terms):
            before = two[0][comp].at(row, ROWS)
            value = before + cb * term
            if comp == VZ:
                value = value + push[2, 0, here(row)]
            down[comp, here(row)] = before
            down[3 + comp, here(row)] = value
    for row in chunks(size_y):
        for x in range(1, width):
            if x < last:
                moved = {c: one[x][c].at(row, ROWS) for c in range(9)}
                values = imaged(moved, field, x, row)
            else:
                moved = [one[x][c].at(row, ROWS) * field[6 + c, x, here(row)] for c in VEL]
                values = [None, None, add(moved)]
            for n, value in enumerate(values):
                if value is not None:
                    early[n, x, here(row)] = value
    hand_out(by_pair, by_next, up, down)


def beyond(v, cl, cm):
    spread = cl * v[0]
    return {XX: spread + 2.0 * cm * v[0], YY: spread, ZZ: spread, XY: cm * v[1], XZ: cm * v[2]}


def add(terms):
    return functools.reduce(jnp.add, terms)


def imaged(moved, forward, x, row):
    f = [forward[n, x, here(row)] for n in range(9)]
    trace = (moved[XX] + moved[YY] + moved[ZZ]) * (f[0] + f[1] + f[2])
    shear = add([moved[comp] * f[n] for n, comp in enumerate(STRESS)])
    density = add([moved[c] * f[6 + c] for c in VEL]) if VX in moved else None
    return trace, shear, density


def own_planes(st, end):
    width = st.shape[1]
    one = [{c: Plane(st, c, x) for c in range(9)} for x in range(width)]
    one[0] = {c: Plane(end, 0, c) for c in range(9)}
    one[-1] = {c: Plane(st, c, width - 1) if c in VEL else Plane(end, 1, c) for c in range(9)}
    return one


def near_kernel(groups, *refs):
    by_pair, by_next, *refs = refs
    if groups == 2:
        swapped, orientation, *refs = refs
    state, st, coef, cells, push, forward, early, end, w, third, outer, parts, known, *refs = refs
    if groups == 2:
        weights, *refs = refs
    low, high, high_v, d_s, d_v, *classes = refs
    width, size_y = st.shape[1], st.shape[2]
    last = width - 1
    take_in(by_pair, by_next, low, high)
    count = (low.shape[0] - 3 * size_y) // 4
    base = 3 * size_y
    if groups == 2:
        me = lax.axis_index("shot")
        mine = pl.ds(pl.multiple_of(me * count, 8), count)
        theirs = pl.ds(pl.multiple_of((1 - me) * count, 8), count)
        low_at = pl.multiple_of(jnp.where(is_even(), 4 * count, 0), 8)
        high_at = pl.multiple_of(jnp.where(is_even(), 0, 4 * count), 8)
        for n in range(4):
            if n < 3:
                outer[n, mine] = low[base + n * count : base + (n + 1) * count]
                outer[n, theirs] = swapped[pl.ds(low_at + n * count, count)]
            outer[3 + n, mine] = high[base + n * count : base + (n + 1) * count]
            outer[3 + n, theirs] = swapped[pl.ds(high_at + n * count, count)]
    else:
        for n in range(4):
            if n < 3:
                outer[n] = low[base + n * count : base + (n + 1) * count]
            outer[3 + n] = high[base + n * count : base + (n + 1) * count]
    clear_ends(outer.at[0:3], outer.at[3:7])

    def coefs(x, row):
        if x < 0:
            return [outer[n, here(row)] for n in range(3)]
        if x > last:
            return [outer[3 + n, here(row)] for n in range(3)]
        return [coef[n, x, here(row)] for n in range(3)]

    raw = [{c: Plane(state, c, x) for c in range(9)} for x in range(width)]
    old = [{c: Plane(st, c, x) for c in range(9)} for x in range(width)]
    one = own_planes(st, end)
    two = [{c: Plane(w, c, x) for c in range(9)} for x in range(width)]
    high_one = {c: Plane(high_v, c) for c in VEL}
    d_low_s, d_high_s, d_high_s_two = ({c: Plane(d_s, k, c - XX) for c in STRESS} for k in range(3))
    d_high_v, d_far_v, d_low_v = ({c: Plane(d_v, k, c) for c in VEL} for k in range(3))
    part_v, part_low, d_high_v_two, part_high = (
        {c: Plane(parts, k, n) for n, c in enumerate(names)}
        for k, names in enumerate((VEL, SIDE, VEL, VEL))
    )

    for row in chunks(size_y):
        cb, cb_high = coefs(0, row)[0], coefs(last + 1, row)[0]
        for n, (comp, c) in enumerate(zip(VEL, SIDE)):
            at = slice(n * size_y + row, n * size_y + row + ROWS)
            one[0][comp].set(row, old[0][comp].at(row, ROWS) - cb * low[at])
            delta = -cb_high * raw[last][c].at(row, ROWS)
            d_high_v[comp].set(row, delta)
            high_one[comp].set(row, high[at] + delta)
    for row in chunks(size_y):
        c = cells[here(row), :]
        _, cl, cm = coefs(0, row)
        for comp, term in stress_rate(strain(one[0], one[1], row, ROWS), cl, cm).items():
            one[0][comp].set(row, c * raw[0][comp].at(row, ROWS) + term)
        _, cl, cm = coefs(last, row)
        terms = beyond([high_one[comp].at(row, ROWS) for comp in VEL], cl, cm)
        for comp in STRESS:
            value = old[last][comp].at(row, ROWS)
            one[last][comp].set(row, value + terms[comp] if comp in terms else value)
        _, cl, cm = coefs(-1, row)
        for comp, term in beyond([one[0][comp].at(row, ROWS) for comp in VEL], cl, cm).items():
            d_low_s[comp].set(row, term)
        _, cl, cm = coefs(last + 1, row)
        for comp, term in stress_rate(strain(d_high_v, None, row, ROWS), cl, cm).items():
            d_high_s[comp].set(row, term)

    for row in chunks(size_y):
        for x in range(width):
            cb = coefs(x, row)[0]
            terms = divergence(one[x], one[x - 1] if x else d_low_s, row, ROWS)
            for comp, term in zip(VEL, terms):
                value = one[x][comp].at(row, ROWS) + cb * term
                if comp == VZ:
                    value = value + push[1, x, here(row)]
                (two[x] if x else part_v)[comp].set(row, value)
        cb = coefs(last + 1, row)[0]
        for comp, term in zip(VEL, divergence(d_high_s, one[last], row, ROWS)):
            d_high_v_two[comp].set(row, d_high_v[comp].at(row, ROWS) + cb * term)
        cb = outer[6, here(row)]
        for comp, c in zip(VEL, SIDE):
            d_far_v[comp].set(row, -cb * d_high_s[c].at(row, ROWS))
        cb = coefs(-1, row)[0]
        terms = divergence(d_low_s, None, row, ROWS, (XX, YY, ZZ, XY, XZ))
        for comp, term in zip(VEL, terms):
            d_low_v[comp].set(row, cb * term)
    for row in chunks(size_y):
        for x in range(1, width):
            _, cl, cm = coefs(x, row)
            after = two[x + 1] if x < last else None
            for comp, term in stress_rate(strain(two[x], after, row, ROWS), cl, cm).items():
                two[x][comp].set(row, one[x][comp].at(row, ROWS) + term)
        _, cl, cm = coefs(-1, row)
        rate = stress_rate(strain(d_low_v, None, row, ROWS, SIDE), cl, cm, SIDE)
        for comp, term in rate.items():
            part_low[comp].set(row, d_low_s[comp].at(row, ROWS) + term)
        _, cl, cm = coefs(last + 1, row)
        for comp, term in stress_rate(strain(d_high_v_two, d_far_v, row, ROWS), cl, cm).items():
            d_high_s_two[comp].set(row, d_high_s[comp].at(row, ROWS) + term)
    for row in chunks(size_y):
        cb = coefs(last + 1, row)[0]
        for comp, term in zip(VEL, divergence(d_high_s_two, None, row, ROWS)):
            part_high[comp].set(row, d_high_v_two[comp].at(row, ROWS) + cb * term)
        for x in range(2, last):
            cb = coefs(x, row)[0]
            for comp, term in zip(VEL, divergence(two[x], two[x - 1], row, ROWS)):
                value = two[x][comp].at(row, ROWS) + cb * term
                if comp == VZ:
                    value = value + push[2, x, here(row)]
                third[comp, x, here(row)] = value
    for row in chunks(size_y):
        for x in range(width):
            inner = 1 <= x < last
            v = [two[x]] if x else [one[x]]
            if 2 <= x < last:
                v.append({c: Plane(third, c, x) for c in VEL})
            t = two[x] if inner else one[x]
            moved = {c: add([k[c].at(row, ROWS) for k in v]) for c in VEL}
            moved |= {c: t[c].at(row, ROWS) for c in STRESS}
            for n, value in enumerate(imaged(moved, forward, x, row)):
                if inner or (x and n == 2):
                    value = value + early[n, x, here(row)]
                known[n, x, here(row)] = value
    if groups != 2:
        return

    (classes,) = classes
    rows_held = weights.shape[1]
    own = rows_held - BY
    first = pl.multiple_of(me * BY, BY)
    for j in range(own // BY):
        classes[pl.ds(first + j * BY, BY), :] = class_tile(orientation, j, weights.shape[2])
    classes[pl.ds(pl.multiple_of((1 - me) * own, BY), BY), :] = swapped[8 * count :, :]
    klass = classes[...]
    for column in range(3):
        table = jnp.full(klass.shape, weight_table[3][column], jnp.float32)
        for k in range(3):
            table = jnp.where(klass == k, weight_table[k][column], table)
        weights[column] = smooth_rate * table


def far_kernel(groups, *refs):
    by_next, by_pair, st, end, w, third, outer, parts, known, coef, push, forward, final, *refs = refs
    *images, low, high, edge, low_s, high_v, image = refs
    width, size_y = st.shape[1], st.shape[2]
    last = width - 1
    take_in(by_pair, by_next, low, high)

    def coefs(x, row):
        if x < 0:
            return [outer[n, here(row)] for n in range(3)]
        if x > last:
            return [outer[3 + n, here(row)] for n in range(3)]
        return [coef[n, x, here(row)] for n in range(3)]

    one = own_planes(st, end)
    part = [{c: Plane(w, c, x) for c in range(9)} for x in range(width)]
    two = [dict(p) for p in part]
    for c in range(9):
        two[0][c] = Plane(edge, 0, c)
        if c >= XX:
            two[last][c] = Plane(edge, 1, c)
    three = [{c: Plane(final, c, x) for c in range(9)} for x in range(width)]
    part_v, part_low, d_high_v_two, part_high = (
        {c: Plane(parts, k, n) for n, c in enumerate(names)}
        for k, names in enumerate((VEL, SIDE, VEL, VEL))
    )
    low_two = {c: Plane(low_s, n) for n, c in enumerate(SIDE)}
    high_three = {c: Plane(high_v, c) for c in VEL}

    for row in chunks(size_y):
        cb = coefs(0, row)[0]
        moved = []
        for n, comp in enumerate(VEL):
            moved.append(part_v[comp].at(row, ROWS) - cb * low[n, here(row)])
            two[0][comp].set(row, moved[n])
        _, cl, cm = coefs(-1, row)
        terms = beyond(moved, cl, cm)
        for n, comp in enumerate(SIDE):
            value = low[3 + n, here(row)] + part_low[comp].at(row, ROWS)
            low_two[comp].set(row, value + terms[comp])
        _, cl, cm = coefs(last, row)
        cb = coefs(last + 1, row)[0]
        moved = [high[n, here(row)] + d_high_v_two[n].at(row, ROWS) for n in VEL]
        terms = beyond(moved, cl, cm)
        values = {}
        for comp in STRESS:
            value = part[last][comp].at(row, ROWS)
            values[comp] = value + terms[comp] if comp in terms else value
            two[last][comp].set(row, values[comp])
        for n, comp in enumerate(SIDE):
            value = high[3 + n, here(row)] + part_high[n].at(row, ROWS)
            high_three[n].set(row, value - cb * values[comp])
    for row in chunks(size_y):
        _, cl, cm = coefs(0, row)
        for comp, term in stress_rate(strain(two[0], two[1], row, ROWS), cl, cm).items():
            two[0][comp].set(row, one[0][comp].at(row, ROWS) + term)

    for row in chunks(size_y):
        for x in range(width):
            if 2 <= x < last:
                for comp in VEL:
                    three[x][comp].set(row, third[comp, x, here(row)])
                continue
            cb = coefs(x, row)[0]
            terms = divergence(two[x], two[x - 1] if x else low_two, row, ROWS)
            for comp, term in zip(VEL, terms):
                value = two[x][comp].at(row, ROWS) + cb * term
                if comp == VZ:
                    value = value + push[2, x, here(row)]
                three[x][comp].set(row, value)
    for row in chunks(size_y):
        for x in range(width):
            _, cl, cm = coefs(x, row)
            after = three[x + 1] if x < last else high_three
            rate = stress_rate(strain(three[x], after, row, ROWS), cl, cm)
            moved = {}
            for comp in STRESS:
                before = two[x][comp].at(row, ROWS)
                value = before + rate[comp]
                three[x][comp].set(row, value)
                moved[comp] = value if 1 <= x < last else before + value
            if not 2 <= x < last:
                for comp in VEL:
                    moved[comp] = three[x][comp].at(row, ROWS)
                    if not x:
                        moved[comp] = two[x][comp].at(row, ROWS) + moved[comp]
            for n, value in enumerate(imaged(moved, forward, x, row)):
                before = known[n, x, here(row)]
                image[n, x, here(row)] = before if value is None else before + value

    if groups != 2:
        images[0][...] = image[...]
        return
    give, keep = images
    me = lax.axis_index("shot")
    count = keep.shape[2]
    mine = pl.ds(pl.multiple_of(me * (size_y - count), 8), count)
    theirs = pl.ds(pl.multiple_of((1 - me) * (size_y - count), 8), count)
    for n in range(3):
        for x in range(width):
            give[n, x] = image[n, x, theirs, :]
            keep[n, x] = image[n, x, mine, :]


def y_prev(f):
    return jnp.where(rows(f.shape) == 0, 0.0, pltpu.roll(f, 1, f.ndim - 2))


def y_next(f):
    size = f.shape[-2]
    return jnp.where(rows(f.shape) == size - 1, 0.0, pltpu.roll(f, size - 1, f.ndim - 2))


def sweep(g, before, after, weights):
    w_x, w_y, w_z = weights
    twice = 2.0 * g
    along_x = -twice
    for plane in (before, after):
        if plane is not None:
            along_x = along_x + plane
    along_y = y_next(g) + y_prev(g) - twice
    along_z = z_next(g) + z_prev(g) - twice
    return g + (w_x * along_x + w_y * along_y + w_z * along_z)


def edge_row(me, own):
    return jnp.where(me == 0, own, BY - 1)


def sum_kernel(scale, keep, received, weights, by_pair, by_next, grad, swept, up, down):
    width, count, size_z = grad.shape[1:]
    own = count - BY
    me = lax.axis_index("shot")
    first = pl.multiple_of(me * BY, BY)
    mine = pl.ds(first, own)
    edge = pl.ds(edge_row(me, own), 1)
    last = width - 1
    w = [weights[k] for k in range(3)]
    for to in (up, down):
        to[6 * own :, :] = jnp.zeros((BY, size_z), jnp.float32)
        for j in range(own // BY):
            row = weights[0, pl.ds(pl.multiple_of(first + j * BY, BY), BY), :][0:1]
            to[6 * own + 3 + j : 6 * own + 4 + j, :] = row
    for n in range(3):
        for x in range(width):
            grad[n, x] = (keep[n, x] + received[n, x]) * scale
        swept[n, 0] = sweep(grad[n, 0], None, grad[n, 1], w)
        swept[n, 1] = sweep(grad[n, last], grad[n, last - 1], None, w)
        for to, x, side in ((up, last, 1), (down, 0, 0)):
            to[2 * n * own : (2 * n + 1) * own, :] = grad[n, x, mine, :]
            to[(2 * n + 1) * own : (2 * n + 2) * own, :] = swept[n, side, mine, :]
            to[6 * own + n : 6 * own + n + 1, :] = grad[n, x, edge, :]
    hand_out(by_pair, by_next, up, down)


def inner_kernel(grad, swept, weights, full, half):
    width = grad.shape[1]
    last = width - 1
    w = [weights[k] for k in range(3)]
    for n in range(3):
        full[n, 0] = swept[n, 0]
        full[n, last] = swept[n, 1]
        for x in range(1, last):
            full[n, x] = sweep(grad[n, x], grad[n, x - 1], grad[n, x + 1], w)
        for x in range(1, last):
            half[n, x - 1] = sweep(
                full[n, x],
                full[n, x - 1] if x > 1 else None,
                full[n, x + 1] if x < last - 1 else None,
                w,
            )


def side_kernel(near, *refs):
    got, *refs = refs
    if not near:
        _, *refs = refs
    grad, full, half, weights, out, beside, result, sems = refs
    width, count, size_z = grad.shape[1:]
    own = count - BY
    me = lax.axis_index("shot")
    first = pl.multiple_of(me * BY, BY)
    mine = pl.ds(first, own)
    edge = pl.ds(edge_row(me, own), 1)
    upper = is_even() if near else jnp.logical_not(is_even())
    end = jnp.where(upper, width - 1, 0)
    inner = jnp.where(upper, width - 2, 1)
    beside[...] = jnp.zeros(beside.shape, jnp.float32)
    for n in range(3):
        beside[n, mine, :] = got[2 * n * own : (2 * n + 1) * own, :]
        beside[n, edge, :] = got[6 * own + n : 6 * own + n + 1, :]
        beside[3 + n, mine, :] = got[(2 * n + 1) * own : (2 * n + 2) * own, :]
    for j in range(own // BY):
        row = got[6 * own + 3 + j : 6 * own + 4 + j, :]
        to = pl.ds(pl.multiple_of(first + j * BY, BY), BY)
        beside[6, to, :] = jnp.broadcast_to(row, (BY, size_z))
    @pl.when(jnp.where(upper, no_neighbour(True), no_neighbour(False)))
    def _():
        beside[...] = jnp.zeros(beside.shape, jnp.float32)

    w = [weights[k] for k in range(3)]
    for n in range(3):
        value = full[n, end] + w[0] * beside[n]
        outer = beside[3 + n] + beside[6] * grad[n, end]
        result[n, 0] = sweep(value, outer, full[n, inner], w)
        result[n, 1] = half[n, inner - 1] + w[0] * value
    copies = [
        pltpu.make_async_copy(result.at[:, k, mine, :], out.at[:, x], sems.at[k])
        for k, x in enumerate((end, inner))
    ]
    for copy in copies:
        copy.start()
    for copy in copies:
        copy.wait()


def extended(block, sides, width):
    for axis, dim in sides:
        count = lax.axis_size(axis)
        forward = [(i, i + 1) for i in range(count - 1)]
        backward = [(target, source) for source, target in forward]
        low = lax.ppermute(
            lax.slice_in_dim(block, block.shape[dim] - width, None, axis=dim), axis, forward
        )
        high = lax.ppermute(lax.slice_in_dim(block, 0, width, axis=dim), axis, backward)
        block = jnp.concatenate([low, block, high], axis=dim)
    return block


def smooth_anywhere(image, orientation):
    groups = lax.axis_size("shot")
    owned = image.shape[2] // groups
    total = lax.psum(image, "shot")
    grad = lax.dynamic_slice_in_dim(total, lax.axis_index("shot") * owned, owned, 2)
    grad = grad * (STEPS * groups) ** (-0.5)
    weights = []
    for column in range(3):
        table = jnp.zeros(orientation.shape, jnp.float32)
        for klass in range(4):
            table = table + (orientation == klass).astype(jnp.float32) * weight_table[klass][column]
        table = jnp.repeat(jnp.repeat(table, image.shape[1], 0), BY, 1)
        weights.append(jnp.repeat(table, BZ, 2))
    for _ in range(SWEEPS):
        padded = extended(grad, (("shot", 2), ("tile", 1)), 1)
        padded = jnp.pad(padded, ((0, 0), (0, 0), (0, 0), (1, 1)))
        center = padded[:, 1:-1, 1:-1, 1:-1]
        lap_x = padded[:, 2:, 1:-1, 1:-1] + padded[:, :-2, 1:-1, 1:-1] - 2.0 * center
        lap_y = padded[:, 1:-1, 2:, 1:-1] + padded[:, 1:-1, :-2, 1:-1] - 2.0 * center
        lap_z = padded[:, 1:-1, 1:-1, 2:] + padded[:, 1:-1, 1:-1, :-2] - 2.0 * center
        grad = grad + smooth_rate * (weights[0] * lap_x + weights[1] * lap_y + weights[2] * lap_z)
    return grad


def both_ways(by_pair, by_next):
    count, groups = lax.axis_size("tile"), lax.axis_size("shot")
    out = []
    for array, start in ((by_pair, 0), (by_next, 1)):
        to = {}
        for i in range(start, count - 1, 2):
            to[i], to[i + 1] = i + 1, i
        pairs = [
            (shot * count + i, shot * count + to[i] if i in to else (shot + 1) % groups * count + i)
            for shot in range(groups)
            for i in range(count)
        ]
        out.append(lax.ppermute(array, ("shot", "tile"), pairs))
    return out


def f32(*shape):
    return jax.ShapeDtypeStruct(shape, jnp.float32)


def in_hbm(array):
    return pltpu.with_memory_space_constraint(array, pltpu.HBM)


def call(kernel, outs, args, scratch, scalars=(), space=VMEM, out_space=VMEM, held=None):
    specs = [SMEM if n in scalars else HBM if n == held else space for n in range(len(args))]
    return pl.pallas_call(
        kernel,
        out_shape=outs,
        in_specs=specs,
        out_specs=jax.tree.map(lambda _: out_space, outs),
        scratch_shapes=[
            pltpu.VMEM(shape, jnp.float32) if isinstance(shape, tuple) else shape
            for shape in scratch
        ],
        input_output_aliases={} if held is None else {held: 0},
        compiler_params=pltpu.CompilerParams(vmem_limit_bytes=24 * 1024 * 1024),
    )(*args)


def local(
    adjoint_state,
    adjoint_source,
    forward_field,
    lame_first,
    shear_modulus,
    buoyancy,
    active_blocks,
    orientation,
):
    width, size_y, size_z = lame_first.shape
    plane = (size_y, size_z)
    groups = lax.axis_size("shot")
    state, source, forward = adjoint_state[0], adjoint_source[0], forward_field[0]
    active = jnp.swapaxes(active_blocks, 1, 2)
    grid = f32(9, width, *plane)
    count = size_y // 2 if groups == 2 else size_y
    early = (3 * size_y + 4 * count, size_z)
    by_pair, by_next, cells, tile = call(
        functools.partial(early_kernel, groups),
        [f32(*early), f32(*early), f32(*plane), f32(BY, size_z)],
        [
            in_hbm(a)
            for a in (active, orientation, state, source, lame_first, shear_modulus, buoyancy)
        ],
        [
            early,
            early,
            (9, *plane),
            pltpu.VMEM(plane, source.dtype),
            (7, *plane),
            pltpu.SMEM(active.shape, jnp.int32),
            pltpu.SMEM(orientation.shape, jnp.int32),
            pltpu.SemaphoreType.DMA((14,)),
        ],
        space=HBM,
    )
    by_pair, by_next = both_ways(by_pair, by_next)
    late_pair, late_next, st, push, coef, forward, first_images = call(
        late_kernel,
        [
            f32(6, *plane),
            f32(6, *plane),
            grid,
            f32(STEPS, width, *plane),
            f32(3, width, *plane),
            grid,
            f32(3, width, *plane),
        ],
        [
            *(
                in_hbm(a)
                for a in (state, source, buoyancy, lame_first, shear_modulus, forward)
            ),
            cells,
        ],
        [(3, 3, *plane), (6, *plane), (6, *plane), (6, *plane)],
    )
    late_pair, late_next = both_ways(late_pair, late_next)
    args, outs, scalars = [by_pair, by_next], [], ()
    scratch = [early, early, (3, *plane), (3, 6, *plane), (3, 3, *plane)]
    owned = size_y // groups
    held = owned + BY
    if groups == 2:
        swapped = jnp.concatenate([by_pair[3 * size_y :], by_next[3 * size_y :], tile])
        swapped = lax.ppermute(swapped, "shot", [(0, 1), (1, 0)])
        args += [swapped, orientation]
        outs = [f32(3, held, size_z)]
        scratch += [(held, size_z)]
        scalars = (3,)
    three = f32(3, width, *plane)
    end, w, third, outer, parts, known, *weights = call(
        functools.partial(near_kernel, groups),
        [f32(2, 9, *plane), grid, three, f32(7, *plane), f32(4, 3, *plane), three, *outs],
        [*args, state, st, coef, cells, push, forward, first_images],
        scratch,
        scalars,
    )
    block = (3, width, held, size_z)
    images = [f32(*block), f32(*block)] if groups == 2 else [f32(3, width, *plane)]
    final, *images = call(
        functools.partial(far_kernel, groups),
        [pltpu.VMEM(grid.shape, grid.dtype), *images],
        [late_next, late_pair, st, end, w, third, outer, parts, known, coef, push, forward],
        [(6, *plane), (6, *plane), (2, 9, *plane), (3, *plane), (3, *plane), (3, width, *plane)],
    )
    if groups != 2:
        return final[None], smooth_anywhere(images[0], orientation)
    give, keep = images
    (weights,) = weights
    received = lax.ppermute(give, "shot", [(0, 1), (1, 0)])
    message = (6 * owned + BY, size_z)
    by_pair, by_next, grad, swept = call(
        functools.partial(sum_kernel, (STEPS * groups) ** (-0.5)),
        [f32(*message), f32(*message), f32(*block), f32(3, 2, held, size_z)],
        (keep, received, weights),
        [message, message],
    )
    by_pair, by_next = both_ways(by_pair, by_next)
    full, half = call(
        inner_kernel,
        [f32(*block), f32(3, width - 2, held, size_z)],
        (grad, swept, weights),
        [],
    )
    gradient = f32(3, width, owned, size_z)
    scratch = [(7, held, size_z), (3, 2, held, size_z), pltpu.SemaphoreType.DMA((2,))]
    rest = (grad, full, half, weights)
    gradient = call(
        functools.partial(side_kernel, True), gradient, (by_pair, *rest), scratch, out_space=HBM
    )
    gradient = call(
        functools.partial(side_kernel, False),
        f32(*gradient.shape),
        (by_next, gradient, *rest),
        scratch,
        out_space=HBM,
        held=1,
    )
    return final[None], gradient


def solution(mesh):
    return jax.shard_map(
        local,
        mesh=mesh,
        in_specs=(
            P("shot", None, "tile", None, None),
            P("shot", None, "tile", None, None),
            P("shot", None, "tile", None, None),
            P("tile", None, None),
            P("tile", None, None),
            P("tile", None, None),
            P("tile", None, None),
            P("tile", "shot", None),
        ),
        out_specs=(P("shot", None, "tile", None, None), P(None, "tile", "shot", None)),
        check_vma=False,
    )
```
